32 devices in a mesh: dp: 4 (over y, x), fsdp: 8 (over z, core).
Axes of the slice: x: 2, y: 2, z: 4, core: 2. Of those that a mesh axis runs over, the one named last changes fastest.
Arguments:
- tok_ids: int32 [64, 512], P(('dp', 'fsdp')), may hold values from 0 to 30591
- segments: int32 [64, 512], P(('dp', 'fsdp')), may hold values from 0 to 1, as said below
- seq_len: int32 [64], P(('dp', 'fsdp')), may hold values from 0 to 512, as said below
- label_pos: int32 [64, 64], P(('dp', 'fsdp')), may hold values from 1 to 511, as said below
- label_ids: int32 [64, 64], P(('dp', 'fsdp')), may hold values from 0 to 30591
- table: float32 [30592, 768], P(('dp', 'fsdp')), may hold values from -0.4375 to 0.4375
- w_qkv: float32 [768, 2304], P(('dp', 'fsdp')), may hold values from -0.21875 to 0.21875
- w_out: float32 [768, 768], P(('dp', 'fsdp')), may hold values from -0.875 to 0.875
- w_up: float32 [768, 3072], P(('dp', 'fsdp')), may hold values from -0.21875 to 0.21875
- w_down: float32 [3072, 768], P(('dp', 'fsdp')), may hold values from -0.109375 to 0.109375
- small: float32 [16, 768], P(None, ('dp', 'fsdp'))
- position: float32 [512, 768], P(None, ('dp', 'fsdp')), may hold values from -0.4375 to 0.4375
- t_table: bfloat16 [30592, 768], P(('dp', 'fsdp')), may hold values from -0.4375 to 0.4375
- t_qkv: bfloat16 [768, 2304], P(('dp', 'fsdp')), may hold values from -0.21875 to 0.21875
- t_out: bfloat16 [768, 768], P(('dp', 'fsdp')), may hold values from -0.875 to 0.875
- t_up: bfloat16 [768, 3072], P(('dp', 'fsdp')), may hold values from -0.21875 to 0.21875
- t_down: bfloat16 [3072, 768], P(('dp', 'fsdp')), may hold values from -0.109375 to 0.109375
- t_small: bfloat16 [16, 768], P(None, ('dp', 'fsdp'))
- t_position: bfloat16 [512, 768], P(None, ('dp', 'fsdp')), may hold values from -0.4375 to 0.4375
- mom_table: float32 [30592, 768], P(('dp', 'fsdp')), may hold values from -2.0861626e-07 to 2.0861626e-07
- mom_qkv: float32 [768, 2304], P(('dp', 'fsdp')), may hold values from -2.0861626e-07 to 2.0861626e-07
- mom_out: float32 [768, 768], P(('dp', 'fsdp')), may hold values from -2.0861626e-07 to 2.0861626e-07
- mom_up: float32 [768, 3072], P(('dp', 'fsdp')), may hold values from -2.0861626e-07 to 2.0861626e-07
- mom_down: float32 [3072, 768], P(('dp', 'fsdp')), may hold values from -2.0861626e-07 to 2.0861626e-07
- mom_small: float32 [16, 768], P(None, ('dp', 'fsdp')), may hold values from -2.0861626e-07 to 2.0861626e-07
- mom_position: float32 [512, 768], P(None, ('dp', 'fsdp')), may hold values from -2.0861626e-07 to 2.0861626e-07
- avg_table: float32 [30592, 768], P(('dp', 'fsdp')), may hold values from -0.4375 to 0.4375
- avg_qkv: float32 [768, 2304], P(('dp', 'fsdp')), may hold values from -0.21875 to 0.21875
- avg_out: float32 [768, 768], P(('dp', 'fsdp')), may hold values from -0.875 to 0.875
- avg_up: float32 [768, 3072], P(('dp', 'fsdp')), may hold values from -0.21875 to 0.21875
- avg_down: float32 [3072, 768], P(('dp', 'fsdp')), may hold values from -0.109375 to 0.109375
- avg_small: float32 [16, 768], P(None, ('dp', 'fsdp'))
- avg_position: float32 [512, 768], P(None, ('dp', 'fsdp')), may hold values from -0.4375 to 0.4375
Outputs:
- new_table: float32 [30592, 768], P(('dp', 'fsdp'))
- new_qkv: float32 [768, 2304], P(('dp', 'fsdp'))
- new_out: float32 [768, 768], P(('dp', 'fsdp'))
- new_up: float32 [768, 3072], P(('dp', 'fsdp'))
- new_down: float32 [3072, 768], P(('dp', 'fsdp'))
- new_small: float32 [16, 768], P(None, ('dp', 'fsdp'))
- new_position: float32 [512, 768], P(None, ('dp', 'fsdp'))
- moment_table: float32 [30592, 768], P(('dp', 'fsdp'))
- moment_qkv: float32 [768, 2304], P(('dp', 'fsdp'))
- moment_out: float32 [768, 768], P(('dp', 'fsdp'))
- moment_up: float32 [768, 3072], P(('dp', 'fsdp'))
- moment_down: float32 [3072, 768], P(('dp', 'fsdp'))
- moment_small: float32 [16, 768], P(None, ('dp', 'fsdp'))
- moment_position: float32 [512, 768], P(None, ('dp', 'fsdp'))
- average_table: float32 [30592, 768], P(('dp', 'fsdp'))
- average_qkv: float32 [768, 2304], P(('dp', 'fsdp'))
- average_out: float32 [768, 768], P(('dp', 'fsdp'))
- average_up: float32 [768, 3072], P(('dp', 'fsdp'))
- average_down: float32 [3072, 768], P(('dp', 'fsdp'))
- average_small: float32 [16, 768], P(None, ('dp', 'fsdp'))
- average_position: float32 [512, 768], P(None, ('dp', 'fsdp'))
- grad_norm: float32 [], replicated
- loss_value: float32 [], replicated
The draws below stay inside these ranges and needn't reach their ends.
Inputs may be any that keep to these rules, and one draw needn't show every extreme that they name: `seq_len`: A length of 0 marks an empty slot; the first of each device's 2 slots is never empty; some sequence has 512 tokens; live lengths are at least 256. `label_pos`: each labeled position lies from 1 to its slot's length minus one (is 1 in an empty slot). `segments`: each row is 0 up to some position from 1 to 511 and 1 from there on.
All inputs are finite; a program needn't handle non-finite values.
Results may differ from the reference program's by a relative error of at most 0.011.
Values may be sent and summed in bfloat16 or wider, within the bound.
A program may use at most 384 MiB of HBM per device.

```python
import math
import jax
import jax.numpy as jnp
import numpy as np
from jax import lax

D = 768
HD = 64
FF = 3072
V = 30592
S = 512
P_SIZE = 64
MB = 2
NS = 16
SEQS = 64
NPARAM = 30978048


def slot_lengths(key):
    inner = jax.random.fold_in(key, 7)
    first_key, second_key = jax.random.split(inner)
    length = jax.random.randint(first_key, (SEQS,), S // 2, S + 1)
    empty = jax.random.randint(second_key, (SEQS,), 0, 4) == 0
    slot = jnp.arange(SEQS) % MB
    length = jnp.where(empty & (slot > 0), 0, length)
    length = length.at[0].set(S)
    return length.astype(jnp.int32)


def draw_seq_len(key, part):
    return slot_lengths(key)


def draw_label_pos(key, part):
    length = slot_lengths(key)
    upper = jnp.maximum(length, 2)
    return jax.random.randint(jax.random.fold_in(key, 11), (SEQS, P_SIZE), 1, upper[:, None]).astype(jnp.int32)


def draw_segments(key, part):
    split = jax.random.randint(jax.random.fold_in(key, 13), (SEQS, 1), 1, S)
    return (jnp.arange(S)[None, :] >= split).astype(jnp.int32)


def small_rows(key):
    base = jnp.clip(jax.random.normal(key, (NS, D), jnp.float32), -3.0, 3.0)
    row = jnp.arange(NS)[:, None]
    gains = (row == 8) | (row == 10) | (row == 12)
    segment_rows = row >= 14
    scale = jnp.where(gains, 0.1, jnp.where(segment_rows, 0.3, 0.1))
    return jnp.where(gains, 1.0, 0.0) + scale * base


def draw_small(key, part):
    return small_rows(jax.random.fold_in(key, 21))


def draw_t_small(key, part):
    return small_rows(jax.random.fold_in(key, 23)).astype(jnp.bfloat16)


def draw_avg_small(key, part):
    return small_rows(jax.random.fold_in(key, 25))


def with_ends(drawn, stream_key, least, largest):
    shape = drawn.shape
    spot = [jax.random.randint(jax.random.fold_in(stream_key, axis), (), 0, shape[axis]) for axis in range(len(shape))]
    drawn = drawn.at[tuple(spot)].set(least)
    longest = shape.index(max(shape))
    spot[longest] = (spot[longest] + 1) % shape[longest]
    return drawn.at[tuple(spot)].set(largest)


def block_scale(rng, dims, pieces, least, largest):
    factor_of, own = 1.0, jax.random.fold_in(rng, 6)
    for dim, parts in pieces:
        heights = jnp.exp(jax.random.uniform(jax.random.fold_in(own, dim), (parts,), jnp.float32, least / len(pieces), largest / len(pieces)))
        factor_of = factor_of * jnp.repeat(heights, dims[dim] // parts).reshape([-1 if axis == dim else 1 for axis in range(len(dims))])
    return factor_of


def rank_bounds(amount, skew):
    loads = [(1 << 20) // math.isqrt(grade ** skew) + 1 for grade in range(1, amount + 1)]
    deviation = 1 + sum(loads) // (1 << 30)
    return np.cumsum(np.array([max(1, weight // deviation) for weight in loads]))


def ranked(own_key, dims, count, slope):
    listing = rank_bounds(count, slope)
    lot = jax.random.randint(jax.random.fold_in(own_key, 1), dims, 0, int(listing[count - 1]))
    grade = jnp.searchsorted(jnp.asarray(listing, jnp.int32), lot, side="right")
    return jax.random.permutation(jax.random.fold_in(own_key, 2), count)[grade].astype(jnp.int32)


def scatter_about(rng, shape, deviation, reach, cuts=(), kind=jnp.bfloat16):
    values = jax.random.normal(rng, shape, jnp.float32) * deviation
    if len(cuts) > 0:
        values = block_scale(rng, shape, cuts, -0.22, 0.18) * values
    return jnp.clip(values, min=-reach, max=reach).astype(kind)


def setup_inputs(seed: int = 0) -> dict:
    key_of = jax.random.split(jax.random.key(seed), 34)
    return {
        "tok_ids": with_ends(ranked(key_of[0], (SEQS, S), V, 2), jax.random.fold_in(key_of[0], 3), 0, V - 1).astype(jnp.int32),
        "segments": draw_segments(jax.random.fold_in(key_of[33], 71), 0),
        "seq_len": draw_seq_len(jax.random.fold_in(key_of[33], 71), 0),
        "label_pos": draw_label_pos(jax.random.fold_in(key_of[33], 71), 0),
        "label_ids": with_ends(ranked(key_of[4], (SEQS, P_SIZE), V, 2), jax.random.fold_in(key_of[4], 3), 0, V - 1).astype(jnp.int32),
        "table": scatter_about(key_of[5], (V, D), (D // 4) ** -0.5, 0.4375, ((0, 32),), jnp.float32),
        "w_qkv": scatter_about(key_of[6], (D, 3 * D), D ** -0.5, 0.21875, ((0, 32),), jnp.float32),
        "w_out": scatter_about(key_of[7], (D, D), (D // 16) ** -0.5, 0.875, ((0, 32),), jnp.float32),
        "w_up": scatter_about(key_of[8], (D, FF), D ** -0.5, 0.21875, ((0, 32),), jnp.float32),
        "w_down": scatter_about(key_of[9], (FF, D), FF ** -0.5, 0.109375, ((0, 32),), jnp.float32),
        "small": draw_small(jax.random.fold_in(key_of[33], 71), 0),
        "position": scatter_about(key_of[11], (S, D), (D // 4) ** -0.5, 0.4375, ((1, 32),), jnp.float32),
        "t_table": scatter_about(key_of[12], (V, D), (D // 4) ** -0.5, 0.4375, ((0, 32),)),
        "t_qkv": scatter_about(key_of[13], (D, 3 * D), D ** -0.5, 0.21875, ((0, 32),)),
        "t_out": scatter_about(key_of[14], (D, D), (D // 16) ** -0.5, 0.875, ((0, 32),)),
        "t_up": scatter_about(key_of[15], (D, FF), D ** -0.5, 0.21875, ((0, 32),)),
        "t_down": scatter_about(key_of[16], (FF, D), FF ** -0.5, 0.109375, ((0, 32),)),
        "t_small": draw_t_small(jax.random.fold_in(key_of[33], 71), 0),
        "t_position": scatter_about(key_of[18], (S, D), (D // 4) ** -0.5, 0.4375, ((1, 32),)),
        "mom_table": scatter_about(key_of[19], (V, D), (0.0002 * NPARAM ** -0.5), 2.086162567138672e-07, ((0, 32),), jnp.float32),
        "mom_qkv": scatter_about(key_of[20], (D, 3 * D), (0.0002 * NPARAM ** -0.5), 2.086162567138672e-07, ((0, 32),), jnp.float32),
        "mom_out": scatter_about(key_of[21], (D, D), (0.0002 * NPARAM ** -0.5), 2.086162567138672e-07, ((0, 32),), jnp.float32),
        "mom_up": scatter_about(key_of[22], (D, FF), (0.0002 * NPARAM ** -0.5), 2.086162567138672e-07, ((0, 32),), jnp.float32),
        "mom_down": scatter_about(key_of[23], (FF, D), (0.0002 * NPARAM ** -0.5), 2.086162567138672e-07, ((0, 32),), jnp.float32),
        "mom_small": scatter_about(key_of[24], (NS, D), (0.0002 * NPARAM ** -0.5), 2.086162567138672e-07, ((1, 32),), jnp.float32),
        "mom_position": scatter_about(key_of[25], (S, D), (0.0002 * NPARAM ** -0.5), 2.086162567138672e-07, ((1, 32),), jnp.float32),
        "avg_table": scatter_about(key_of[26], (V, D), (D // 4) ** -0.5, 0.4375, ((0, 32),), jnp.float32),
        "avg_qkv": scatter_about(key_of[27], (D, 3 * D), D ** -0.5, 0.21875, ((0, 32),), jnp.float32),
        "avg_out": scatter_about(key_of[28], (D, D), (D // 16) ** -0.5, 0.875, ((0, 32),), jnp.float32),
        "avg_up": scatter_about(key_of[29], (D, FF), D ** -0.5, 0.21875, ((0, 32),), jnp.float32),
        "avg_down": scatter_about(key_of[30], (FF, D), FF ** -0.5, 0.109375, ((0, 32),), jnp.float32),
        "avg_small": draw_avg_small(jax.random.fold_in(key_of[33], 71), 0),
        "avg_position": scatter_about(key_of[32], (S, D), (D // 4) ** -0.5, 0.4375, ((1, 32),), jnp.float32),
    }


SOFTMAX_HEAT = 2.0
SOFT_FRACTION = 0.5
PKD_WEIGHT = 10.0
MOMENTUM = 0.9
AVERAGE = 0.75
CLIP = 0.002
RATE_SCALE = 20.0
EPSILON = 1e-12
NEGATIVE = -1e+30
HIGHEST_PRECISION = lax.Precision.HIGHEST

@jax.custom_vjp
def low(v):
    return lax.optimization_barrier(v.astype(jnp.bfloat16)).astype(jnp.float32)

@jax.custom_vjp
def low_back(v):
    return v

def low_keep(v):
    return (low(v), None)

def low_pass(kept, grad):
    return (grad,)

def back_keep(v):
    return (v, None)

def back_low(kept, grad):
    return (low(grad),)
low.defvjp(low_keep, low_pass)
low_back.defvjp(back_keep, back_low)

def product(left, right):
    return jnp.dot(left, right, precision=HIGHEST_PRECISION, preferred_element_type=jnp.float32)

def layer_norm(value, gain, shift):
    mean = lax.optimization_barrier(jnp.mean(value, axis=-1, keepdims=True))
    centred = value - mean
    variance = lax.optimization_barrier(jnp.mean(centred * centred, axis=-1, keepdims=True))
    return centred * lax.rsqrt(variance + EPSILON) * gain + shift

def layer_forward(value, weights, length):
    w_qkv, w_out, w_up, w_down, small = weights
    rows, width = value.shape
    heads = width // HD
    value_low = low(value)
    bias = jnp.concatenate([small[0], jnp.zeros_like(small[0]), small[1]])
    joined = low(low_back(product(value_low, w_qkv) + bias)).reshape(rows, 3, heads, HD)
    raw = jnp.einsum('qhd,khd->hqk', joined[:, 0], joined[:, 1], precision=HIGHEST_PRECISION)
    keep = jnp.arange(rows) < jnp.maximum(length, 1)
    scores = low_back(jnp.where(keep[None, None, :], raw * 0.125, NEGATIVE))
    probs = low(jax.nn.softmax(scores, axis=-1))
    mixed = jnp.einsum('hqk,khd->qhd', probs, joined[:, 2], precision=HIGHEST_PRECISION)
    context = low(low_back(mixed.reshape(rows, width)))
    attn = low_back(product(context, w_out) + small[2])
    first = layer_norm(value + attn, small[8], small[9])
    upward = low_back(product(low(first), w_up) + small[3:7].reshape(-1))
    act = low(jax.nn.gelu(upward, approximate=False))
    down = low_back(product(act, w_down) + small[7])
    return layer_norm(first + down, small[10], small[11])

def run_model(params, ids, segment_ids, length):
    table_low, w_qkv, w_out, w_up, w_down, small, position = params
    tokens = low_back(table_low[ids])
    segment_rows = jnp.where(segment_ids[:, None] == 0, small[14], small[15])
    start = layer_norm(tokens + position + segment_rows, small[12], small[13])
    return layer_forward(start, (w_qkv, w_out, w_up, w_down, small), length)

def label_valid(lengths, labels, span):
    needed = (lengths * labels + span - 1) // span
    return (jnp.arange(labels)[None, :] < needed[:, None]).astype(jnp.float32)

def sequence_loss(student, teacher, data, label_count, count_seq):
    ids, segment_ids, length, places, targets, valid_mask = data
    student_out = run_model(student, ids, segment_ids, length)
    teacher_out = run_model(teacher, ids, segment_ids, length)
    student_rows = low(student_out[places])
    teacher_rows = low(teacher_out[places])
    student_scores = low_back(product(student_rows, student[0].T))
    teacher_scores = product(teacher_rows, teacher[0].T)
    plain = jax.nn.log_softmax(student_scores, axis=-1)
    cross_entropy = -jnp.take_along_axis(plain, targets[:, None], axis=1)[:, 0]
    student_soft_probs = jax.nn.log_softmax(student_scores / SOFTMAX_HEAT, axis=-1)
    teacher_soft_probs = jax.nn.log_softmax(teacher_scores / SOFTMAX_HEAT, axis=-1)
    divergence_loss = lax.optimization_barrier(jnp.sum(jnp.exp(teacher_soft_probs) * (teacher_soft_probs - student_soft_probs), axis=-1))
    label_loss_term = jnp.sum(valid_mask * ((1.0 - SOFT_FRACTION) * cross_entropy + SOFT_FRACTION * SOFTMAX_HEAT * SOFTMAX_HEAT * divergence_loss)) / label_count
    cls_student = student_out[0]
    cls_teacher = teacher_out[0]
    unit_student = cls_student * lax.rsqrt(jnp.sum(cls_student * cls_student) + 1e-06)
    unit_teacher = cls_teacher * lax.rsqrt(jnp.sum(cls_teacher * cls_teacher) + 1e-06)
    live = (length > 0).astype(jnp.float32)
    gap = unit_student - unit_teacher
    return label_loss_term + PKD_WEIGHT * live * jnp.sum(gap * gap) / count_seq

def reference(tok_ids, segments, seq_len, label_pos, label_ids, table, w_qkv, w_out, w_up, w_down, small, position, t_table, t_qkv, t_out, t_up, t_down, t_small, t_position, mom_table, mom_qkv, mom_out, mom_up, mom_down, mom_small, mom_position, avg_table, avg_qkv, avg_out, avg_up, avg_down, avg_small, avg_position):
    teacher = tuple((low(weight.astype(jnp.float32)) for weight in (t_table, t_qkv, t_out, t_up, t_down, t_small, t_position)))
    valid_mask = label_valid(seq_len, P_SIZE, S)
    label_count = jnp.sum(valid_mask)
    count_seq = jnp.sum((seq_len > 0).astype(jnp.float32))

    def total_loss(*params):
        lowed = tuple((low(weight) for weight in params))

        def one(carry, data):
            return (carry + sequence_loss(lowed, teacher, data, label_count, count_seq), None)
        total, unused = lax.scan(jax.checkpoint(one), jnp.float32(0.0), (tok_ids, segments, seq_len, label_pos, label_ids, valid_mask))
        return total
    params = (table, w_qkv, w_out, w_up, w_down, small, position)
    loss_value, pullback = jax.vjp(total_loss, *params)
    grads = pullback(jnp.ones((), jnp.float32))
    total_sq = jnp.float32(0.0)
    for grad in grads:
        total_sq = total_sq + jnp.sum(grad * grad)
    grad_norm = jnp.sqrt(total_sq)
    factor = CLIP / jnp.maximum(grad_norm, CLIP)
    rate = RATE_SCALE * math.sqrt(NPARAM)
    moms = (mom_table, mom_qkv, mom_out, mom_up, mom_down, mom_small, mom_position)
    avgs = (avg_table, avg_qkv, avg_out, avg_up, avg_down, avg_small, avg_position)
    news, moments, averages = ([], [], [])
    for weight, grad, momentum, average in zip(params, grads, moms, avgs):
        clipped = grad * factor
        moment = MOMENTUM * momentum + clipped
        fresh = weight - rate * (clipped + MOMENTUM * moment)
        news.append(fresh)
        moments.append(moment)
        averages.append(AVERAGE * average + (1.0 - AVERAGE) * fresh)
    return (news[0], news[1], news[2], news[3], news[4], news[5], news[6], moments[0], moments[1], moments[2], moments[3], moments[4], moments[5], moments[6], averages[0], averages[1], averages[2], averages[3], averages[4], averages[5], averages[6], grad_norm, loss_value)
```

```python
import math

import jax
import jax.numpy as jnp
from jax import lax
from jax.sharding import PartitionSpec as P

HD = 64
NPARAM = 30978048


SOFTMAX_HEAT = 2.0
SOFT_FRACTION = 0.5
PKD_WEIGHT = 10.0
MOMENTUM = 0.9
AVERAGE = 0.75
CLIP = 0.002
RATE_SCALE = 20.0
EPSILON = 1e-12
NEGATIVE = -1e30
BOTH = ("dp", "fsdp")
LOW = jnp.bfloat16


def product_of(form, left, right):
    return jnp.einsum(form, left, right, preferred_element_type=jnp.float32)


def owned(ids, share, padded, groups, own):
    block = ids // share
    inside = block % groups == own
    local = block // groups * padded + ids % share
    return (inside, jnp.where(inside, local, 0))


def layer_norm_keep(value, gain, shift):
    mean = jnp.mean(value, axis=-1, keepdims=True)
    centred = value - mean
    inverse = lax.rsqrt(jnp.mean(centred * centred, axis=-1, keepdims=True) + EPSILON)
    normed = centred * inverse
    return (normed * gain + shift, normed, inverse)


def layer_norm_back(grad, normed, inverse, gain):
    axes = tuple(range(grad.ndim - 1))
    gain_grad = jnp.sum(grad * normed, axis=axes)
    shift_grad = jnp.sum(grad, axis=axes)
    scaled = grad * gain
    centred = scaled - jnp.mean(scaled, axis=-1, keepdims=True)
    return (
        inverse * (centred - normed * jnp.mean(scaled * normed, axis=-1, keepdims=True)),
        gain_grad,
        shift_grad,
    )


def gelu_parts(upward):
    normal_cdf = 0.5 * (1.0 + lax.erf(upward * 0.7071067811865476))
    density = jnp.exp(-0.5 * upward * upward) * 0.3989422804014327
    return (upward * normal_cdf, normal_cdf + upward * density)


def label_valid(lengths, labels, span):
    needed = (lengths * labels + span - 1) // span
    return (jnp.arange(labels)[None, :] < needed[:, None]).astype(jnp.float32)


def masked_scores(queries, keys, lengths):
    raw = product_of("bqhd,bkhd->bhqk", queries, keys)
    keep = jnp.arange(keys.shape[1])[None, :] < jnp.maximum(lengths, 1)[:, None]
    return jnp.where(keep[:, None, None, :], raw * 0.125, NEGATIVE)


def pack_layer(weights, extra):
    w_qkv, w_out, w_up, w_down, small, position = (w.astype(LOW) for w in weights)
    rows = w_qkv.shape[0]
    parts = w_down.shape[0] // rows
    pieces = [w_qkv, w_out, w_up]
    pieces += [w_down[k * rows : (k + 1) * rows] for k in range(parts)]
    pieces += [position.T, small.T]
    filled = small.shape[0]
    if extra is not None:
        pieces.append(extra)
        filled += extra.shape[1]
    pieces.append(jnp.zeros((rows, -filled % 128), LOW))
    return jnp.concatenate(pieces, axis=1)


def unpack_layer(packed, devices, span, slots):
    width = packed.shape[0]
    ff = 4 * width
    edges = [3 * width, 4 * width, 4 * width + ff, 4 * width + 2 * ff]
    w_qkv = packed[:, : edges[0]]
    w_out = packed[:, edges[0] : edges[1]]
    w_up = packed[:, edges[1] : edges[2]]
    down = packed[:, edges[2] : edges[3]]
    w_down = (
        down.reshape(devices, width // devices, 4, width).transpose(0, 2, 1, 3).reshape(ff, width)
    )
    rest = packed[:, edges[3] :]
    position = rest[:, :span].T.astype(jnp.float32)
    small = rest[:, span : span + slots].T.astype(jnp.float32)
    return (w_qkv, w_out, w_up, w_down, small, position), rest[:, span + slots :]


def embed_forward(token_rows, weights, segment_ids):
    small, position = weights[4:]
    segment_rows = jnp.where(segment_ids[..., None] == 0, small[14], small[15])
    return layer_norm_keep(token_rows + position + segment_rows, small[12], small[13])


def layer_forward(value, weights, lengths):
    w_qkv, w_out, w_up, w_down, small = weights[:5]
    micro, span, width = value.shape
    heads = width // HD
    value_low = value.astype(LOW)
    bias = jnp.concatenate([small[0], jnp.zeros_like(small[0]), small[1]])
    joined = (product_of("bsd,df->bsf", value_low, w_qkv) + bias).astype(LOW)
    split = joined.reshape(micro, span, 3, heads, HD)
    scores = masked_scores(split[:, :, 0], split[:, :, 1], lengths)
    top = jnp.max(scores, axis=-1, keepdims=True)
    exponent = jnp.exp(scores - top)
    total = jnp.sum(exponent, axis=-1, keepdims=True)
    probs = (exponent / total).astype(LOW)
    logsum = top + jnp.log(total)
    context = (
        product_of("bhqk,bkhd->bqhd", probs, split[:, :, 2]).reshape(micro, span, width).astype(LOW)
    )
    attn = product_of("bsc,cd->bsd", context, w_out) + small[2]
    first, normed_first, inverse_first = layer_norm_keep(value + attn, small[8], small[9])
    first_low = first.astype(LOW)
    upward = product_of("bsd,df->bsf", first_low, w_up) + small[3:7].reshape(-1)
    act, slope = gelu_parts(upward)
    act_low = act.astype(LOW)
    down = product_of("bsf,fd->bsd", act_low, w_down) + small[7]
    out, normed_second, inverse_second = layer_norm_keep(first + down, small[10], small[11])
    return (
        out,
        (
            value_low,
            joined,
            logsum,
            context,
            normed_first,
            inverse_first,
            first_low,
            slope,
            act_low,
            normed_second,
            inverse_second,
        ),
    )


def layer_backward(grad, weights, kept, lengths):
    w_qkv, w_out, w_up, w_down, small = weights[:5]
    (
        value_low,
        joined,
        logsum,
        context,
        normed_first,
        inverse_first,
        first_low,
        slope,
        act_low,
        normed_second,
        inverse_second,
    ) = kept
    micro, span, width = value_low.shape
    heads = width // HD
    d_second, gain_second, shift_second = layer_norm_back(
        grad, normed_second, inverse_second, small[10]
    )
    d_down = d_second.astype(LOW)
    g_down = product_of("bsf,bsd->fd", act_low, d_down)
    d_up = (product_of("bsd,fd->bsf", d_down, w_down) * slope).astype(LOW)
    g_up = product_of("bsd,bsf->df", first_low, d_up)
    d_first = d_second + product_of("bsf,df->bsd", d_up, w_up)
    d_sum, gain_first, shift_first = layer_norm_back(d_first, normed_first, inverse_first, small[8])
    d_attn = d_sum.astype(LOW)
    g_out = product_of("bsc,bsd->cd", context, d_attn)
    d_context = (
        product_of("bsd,cd->bsc", d_attn, w_out).astype(LOW).reshape(micro, span, heads, HD)
    )
    split = joined.reshape(micro, span, 3, heads, HD)
    probs = jnp.exp(masked_scores(split[:, :, 0], split[:, :, 1], lengths) - logsum)
    g_values = product_of("bhqk,bqhd->bkhd", probs.astype(LOW), d_context)
    d_probs = product_of("bqhd,bkhd->bhqk", d_context, split[:, :, 2])
    d_scores = (probs * (d_probs - jnp.sum(probs * d_probs, axis=-1, keepdims=True))).astype(LOW)
    g_queries = product_of("bhqk,bkhd->bqhd", d_scores, split[:, :, 1]) * 0.125
    g_keys = product_of("bhqk,bqhd->bkhd", d_scores, split[:, :, 0]) * 0.125
    d_joined = (
        jnp.stack([g_queries, g_keys, g_values], axis=2)
        .reshape(micro, span, 3 * width)
        .astype(LOW)
    )
    g_qkv = product_of("bsd,bsf->df", value_low, d_joined)
    d_value = d_sum + product_of("bsf,df->bsd", d_joined, w_qkv)

    def column_sum(value):
        return jnp.sum(value.astype(jnp.float32), axis=(0, 1))

    joined_sum = column_sum(d_joined)
    rows_grad = jnp.concatenate(
        [
            joined_sum[:width][None],
            joined_sum[2 * width :][None],
            column_sum(d_attn)[None],
            column_sum(d_up).reshape(-1, width),
            column_sum(d_down)[None],
            gain_first[None],
            shift_first[None],
            gain_second[None],
            shift_second[None],
        ]
    )
    return ((g_qkv, g_out, g_up, g_down), rows_grad, d_value)


def label_head(
    student_out, teacher_out, places, tables, targets, valid_mask, own, share, padded, groups, count
):
    table_student, table_teacher = tables
    vocab_rows = table_student.shape[0]
    micro, span, width = student_out.shape
    mine = places.size
    pick = (places[..., None] == jnp.arange(span)).astype(LOW)
    rows = jnp.stack(
        [
            product_of("bps,bsd->bpd", pick, out.astype(LOW)).astype(LOW).reshape(mine, width)
            for out in (student_out, teacher_out)
        ]
    )
    rows_all = lax.all_gather(rows, "fsdp", axis=1, tiled=True)
    all_student = rows_all[0]
    all_teacher = rows_all[1]
    row_index = jnp.arange(vocab_rows)
    real = (row_index % padded < share)[None, :]
    inside, local_target = owned(targets, share, padded, groups, own)
    hit = (row_index[None, :] == local_target[:, None]) & inside[:, None]
    student = jnp.where(real, product_of("pd,vd->pv", all_student, table_student), NEGATIVE)
    teacher = jnp.where(real, product_of("pd,vd->pv", all_teacher, table_teacher), NEGATIVE)
    top_student = jnp.max(student, axis=1)
    top_teacher = jnp.max(teacher, axis=1)
    half = jnp.exp((student - top_student[:, None]) / SOFTMAX_HEAT)
    teacher_exp = jnp.exp((teacher - top_teacher[:, None]) / SOFTMAX_HEAT)
    stats = jnp.stack(
        [
            top_student,
            jnp.sum(half * half, axis=1),
            jnp.sum(half, axis=1),
            top_teacher,
            jnp.sum(teacher_exp, axis=1),
            jnp.sum(teacher_exp * ((teacher - student) / SOFTMAX_HEAT), axis=1),
            jnp.sum(jnp.where(hit, student, 0.0), axis=1),
            jnp.zeros_like(top_student),
        ]
    )
    stats = lax.all_gather(stats, "fsdp")
    peak_student = jnp.max(stats[:, 0], axis=0)
    peak_teacher = jnp.max(stats[:, 3], axis=0)
    fall_student = jnp.exp((stats[:, 0] - peak_student) / SOFTMAX_HEAT)
    fall_teacher = jnp.exp((stats[:, 3] - peak_teacher) / SOFTMAX_HEAT)
    sum_plain = jnp.sum(stats[:, 1] * fall_student * fall_student, axis=0)
    sum_soft = jnp.sum(stats[:, 2] * fall_student, axis=0)
    sum_teacher = jnp.sum(stats[:, 4] * fall_teacher, axis=0)
    cross = jnp.sum(stats[:, 5] * fall_teacher, axis=0)
    target_logit = jnp.sum(stats[:, 6], axis=0)
    lse_plain = peak_student + jnp.log(sum_plain)
    lse_soft = peak_student / SOFTMAX_HEAT + jnp.log(sum_soft)
    lse_teacher = peak_teacher / SOFTMAX_HEAT + jnp.log(sum_teacher)
    cross_entropy = lse_plain - target_logit
    divergence_loss = cross / sum_teacher - lse_teacher + lse_soft
    share_lab = valid_mask / count
    hard = jnp.exp(student - lse_plain[:, None]) - hit.astype(jnp.float32)
    soft = jnp.exp(student / SOFTMAX_HEAT - lse_soft[:, None]) - jnp.exp(
        teacher / SOFTMAX_HEAT - lse_teacher[:, None]
    )
    d_logits = (
        share_lab[:, None]
        * ((1.0 - SOFT_FRACTION) * hard + SOFT_FRACTION * SOFTMAX_HEAT * soft)
    ).astype(LOW)
    d_rows = lax.psum_scatter(
        product_of("pv,vd->pd", d_logits, table_student).astype(LOW),
        "fsdp",
        scatter_dimension=0,
        tiled=True,
    )
    table_term = product_of("pv,pd->vd", d_logits, all_student)
    terms = share_lab * (
        (1.0 - SOFT_FRACTION) * cross_entropy
        + SOFT_FRACTION * SOFTMAX_HEAT * SOFTMAX_HEAT * divergence_loss
    )
    local = lax.dynamic_slice_in_dim(terms, own * mine, mine)
    d_out = product_of("bps,bpd->bsd", pick, d_rows.reshape(micro, -1, width))
    return (d_out, table_term, jnp.sum(local))


def pack_grads(matrices, small_grad, position_grad, devices):
    g_qkv, g_out, g_up, g_down = (g.astype(LOW) for g in matrices)
    width = g_qkv.shape[0]
    ff = g_down.shape[0]
    parts = ff // width
    g_down = (
        g_down.reshape(devices, parts, width // devices, width)
        .transpose(0, 2, 1, 3)
        .reshape(width, ff)
    )
    pad = -small_grad.shape[0] % 128
    return jnp.concatenate(
        [
            g_qkv,
            g_out,
            g_up,
            g_down,
            position_grad.astype(LOW).T,
            jnp.pad(small_grad, ((0, pad), (0, 0))).astype(LOW).T,
        ],
        axis=1,
    )


def unpack_grads(packed, width, span, slots):
    ff = 4 * width
    packed = packed.astype(jnp.float32)
    edges = [3 * width, 4 * width, 4 * width + ff, 4 * width + 2 * ff]
    down = packed[:, edges[2] : edges[3]]
    g_down = jnp.concatenate([down[:, k * width : (k + 1) * width] for k in range(4)], axis=0)
    return (
        packed[:, : edges[0]],
        packed[:, edges[0] : edges[1]],
        packed[:, edges[1] : edges[2]],
        g_down,
        packed[:, edges[3] + span : edges[3] + span + slots].T,
        packed[:, edges[3] : edges[3] + span].T,
    )


def unit_of(cls):
    scale = lax.rsqrt(jnp.sum(cls * cls, axis=-1, keepdims=True) + 1e-06)
    return cls * scale, scale


def on_device(
    tok_ids,
    segments,
    seq_len,
    label_pos,
    label_ids,
    table,
    w_qkv,
    w_out,
    w_up,
    w_down,
    small,
    position,
    t_table,
    t_qkv,
    t_out,
    t_up,
    t_down,
    t_small,
    t_position,
    mom_table,
    mom_qkv,
    mom_out,
    mom_up,
    mom_down,
    mom_small,
    mom_position,
    avg_table,
    avg_qkv,
    avg_out,
    avg_up,
    avg_down,
    avg_small,
    avg_position,
):
    micro, span = tok_ids.shape
    labels = label_pos.shape[1]
    share, width = table.shape
    groups = lax.axis_size("fsdp")
    dp = lax.axis_size("dp")
    devices = groups * dp
    own = lax.axis_index("fsdp")
    pad = -share % 16
    padded = share + pad
    rows_own = w_qkv.shape[0]
    slots = small.shape[0]

    info = jnp.concatenate(
        [tok_ids, label_ids, jnp.broadcast_to(seq_len[:, None], (micro, labels))], axis=1
    )
    info = lax.all_gather(info, "fsdp", axis=0, tiled=True)
    ids_all = info[:, :span]
    targets_all = info[:, span : span + labels].reshape(-1)
    lengths_all = info[:, span + labels]
    student_table = lax.all_gather(
        jnp.pad(table.astype(LOW), ((0, pad), (0, 0))), "dp", axis=0, tiled=True
    )
    teacher_table = lax.all_gather(jnp.pad(t_table, ((0, pad), (0, 0))), "dp", axis=0, tiled=True)
    tables = (student_table, teacher_table)
    vocab_rows = student_table.shape[0]

    valid_local = label_valid(seq_len, labels, span)
    counts = jnp.stack([jnp.sum(valid_local), jnp.sum((seq_len > 0).astype(jnp.float32))])
    extra = jnp.broadcast_to(counts.astype(LOW)[None, :], (rows_own, 2))

    inside, safe_ids = owned(ids_all, share, padded, groups, own)
    blank = jnp.zeros((), LOW)
    picked_student = jnp.where(inside[..., None], student_table[safe_ids], blank)
    picked_teacher = jnp.where(inside[..., None], teacher_table[safe_ids], blank)
    tokens_student = lax.psum_scatter(
        picked_student, "fsdp", scatter_dimension=0, tiled=True
    ).astype(jnp.float32)
    tokens_teacher = lax.psum_scatter(
        picked_teacher, "fsdp", scatter_dimension=0, tiled=True
    ).astype(jnp.float32)

    packed_student = pack_layer((w_qkv, w_out, w_up, w_down, small, position), extra)
    packed_teacher = pack_layer((t_qkv, t_out, t_up, t_down, t_small, t_position), None)
    packed_student = lax.all_gather(packed_student, BOTH, axis=0, tiled=True)
    packed_teacher = lax.all_gather(packed_teacher, BOTH, axis=0, tiled=True)
    weights, rest = unpack_layer(packed_student, devices, span, slots)
    teacher, _ = unpack_layer(packed_teacher, devices, span, slots)
    counted = jnp.sum(rest[::rows_own, :2].astype(jnp.float32), axis=0)
    label_count, count_seq = counted[0], counted[1]

    start, normed_start, inverse_start = embed_forward(tokens_student, weights, segments)
    teacher_start = embed_forward(tokens_teacher, teacher, segments)[0]
    student_out, kept = layer_forward(start, weights, seq_len)
    teacher_out = layer_forward(teacher_start, teacher, seq_len)[0]
    valid_group = label_valid(lengths_all, labels, span).reshape(-1)
    d_out, table_grad, label_loss = label_head(
        student_out,
        teacher_out,
        label_pos,
        tables,
        targets_all,
        valid_group,
        own,
        share,
        padded,
        groups,
        label_count,
    )
    cls_student = student_out[:, 0]
    unit_student, scale_student = unit_of(cls_student)
    unit_teacher = unit_of(teacher_out[:, 0])[0]
    weight_pkd = (PKD_WEIGHT * (seq_len > 0).astype(jnp.float32) / count_seq)[:, None]
    gap = unit_student - unit_teacher
    d_unit = 2.0 * weight_pkd * gap
    d_cls = scale_student * d_unit - cls_student * scale_student**3 * jnp.sum(
        cls_student * d_unit, axis=-1, keepdims=True
    )
    first_row = (jnp.arange(span) == 0).astype(jnp.float32)[None, :, None]
    d_out = d_out + first_row * d_cls[:, None, :]
    loss_part = label_loss + jnp.sum(weight_pkd * gap * gap)

    matrices, rows_grad, d_start = layer_backward(d_out, weights, kept, seq_len)
    d_embed, gain_embed, shift_embed = layer_norm_back(
        d_start, normed_start, inverse_start, weights[4][12]
    )
    zero_segment = (segments == 0).astype(jnp.float32)[..., None]
    small_grad = jnp.concatenate(
        [
            rows_grad,
            gain_embed[None],
            shift_embed[None],
            jnp.sum(d_embed * zero_segment, axis=(0, 1))[None],
            jnp.sum(d_embed * (1.0 - zero_segment), axis=(0, 1))[None],
        ]
    )
    embed_grads = lax.all_gather(d_embed.astype(LOW), "fsdp", axis=0, tiled=True)
    packed_grads = pack_grads(matrices, small_grad, jnp.sum(d_embed, axis=0), devices)
    packed_grads = lax.psum_scatter(packed_grads, BOTH, scatter_dimension=0, tiled=True)
    flat = jnp.where(inside[..., None], embed_grads.astype(jnp.float32), 0.0).reshape(-1, width)
    table_grad = table_grad + jax.ops.segment_sum(
        flat, safe_ids.reshape(-1), num_segments=vocab_rows
    )
    table_shard = lax.psum_scatter(
        table_grad.astype(LOW), "dp", scatter_dimension=0, tiled=True
    ).astype(jnp.float32)[:share]
    grads = (table_shard,) + unpack_grads(packed_grads, width, span, slots)
    squares = jnp.zeros((), jnp.float32)
    for grad in grads:
        squares = squares + jnp.sum(grad * grad)
    sums = jnp.broadcast_to(jnp.stack([squares, loss_part])[:, None], (2, 128))
    sums = jnp.sum(lax.all_gather(sums, "dp"), axis=0)
    sums = jnp.sum(lax.all_gather(sums, "fsdp"), axis=0)
    total_sq, loss_value = sums[0, 0], sums[1, 0]
    grad_norm = jnp.sqrt(total_sq)
    factor = CLIP / jnp.maximum(grad_norm, CLIP)
    rate = RATE_SCALE * math.sqrt(NPARAM)
    params = (table, w_qkv, w_out, w_up, w_down, small, position)
    moms = (mom_table, mom_qkv, mom_out, mom_up, mom_down, mom_small, mom_position)
    avgs = (avg_table, avg_qkv, avg_out, avg_up, avg_down, avg_small, avg_position)
    news, moments, averages = ([], [], [])
    for weight, grad, momentum, average in zip(params, grads, moms, avgs):
        clipped = grad * factor
        moment = MOMENTUM * momentum + clipped
        fresh = weight - rate * (clipped + MOMENTUM * moment)
        news.append(fresh)
        moments.append(moment)
        averages.append(AVERAGE * average + (1.0 - AVERAGE) * fresh)
    return tuple(news) + tuple(moments) + tuple(averages) + (grad_norm, loss_value)


def solution(mesh):
    placed = (
        P(("dp", "fsdp"), None),
        P(("dp", "fsdp"), None),
        P(("dp", "fsdp")),
        P(("dp", "fsdp"), None),
        P(("dp", "fsdp"), None),
        P(("dp", "fsdp"), None),
        P(("dp", "fsdp"), None),
        P(("dp", "fsdp"), None),
        P(("dp", "fsdp"), None),
        P(("dp", "fsdp"), None),
        P(None, ("dp", "fsdp")),
        P(None, ("dp", "fsdp")),
        P(("dp", "fsdp"), None),
        P(("dp", "fsdp"), None),
        P(("dp", "fsdp"), None),
        P(("dp", "fsdp"), None),
        P(("dp", "fsdp"), None),
        P(None, ("dp", "fsdp")),
        P(None, ("dp", "fsdp")),
        P(("dp", "fsdp"), None),
        P(("dp", "fsdp"), None),
        P(("dp", "fsdp"), None),
        P(("dp", "fsdp"), None),
        P(("dp", "fsdp"), None),
        P(None, ("dp", "fsdp")),
        P(None, ("dp", "fsdp")),
        P(("dp", "fsdp"), None),
        P(("dp", "fsdp"), None),
        P(("dp", "fsdp"), None),
        P(("dp", "fsdp"), None),
        P(("dp", "fsdp"), None),
        P(None, ("dp", "fsdp")),
        P(None, ("dp", "fsdp")),
    )
    return jax.shard_map(
        on_device,
        mesh=mesh,
        in_specs=placed,
        out_specs=(
            P(("dp", "fsdp"), None),
            P(("dp", "fsdp"), None),
            P(("dp", "fsdp"), None),
            P(("dp", "fsdp"), None),
            P(("dp", "fsdp"), None),
            P(None, ("dp", "fsdp")),
            P(None, ("dp", "fsdp")),
            P(("dp", "fsdp"), None),
            P(("dp", "fsdp"), None),
            P(("dp", "fsdp"), None),
            P(("dp", "fsdp"), None),
            P(("dp", "fsdp"), None),
            P(None, ("dp", "fsdp")),
            P(None, ("dp", "fsdp")),
            P(("dp", "fsdp"), None),
            P(("dp", "fsdp"), None),
            P(("dp", "fsdp"), None),
            P(("dp", "fsdp"), None),
            P(("dp", "fsdp"), None),
            P(None, ("dp", "fsdp")),
            P(None, ("dp", "fsdp")),
            P(),
            P(),
        ),
        check_vma=False,
    )
```

```python
import functools
import math

import jax
import jax.numpy as jnp
from jax import lax
from jax.experimental import pallas as pl
from jax.experimental.pallas import tpu as pltpu
from jax.sharding import PartitionSpec as P

HD = 64
NPARAM = 30978048


SOFTMAX_HEAT = 2.0
SOFT_FRACTION = 0.5
PKD_WEIGHT = 10.0
MOMENTUM = 0.9
AVERAGE = 0.75
CLIP = 0.002
RATE_SCALE = 20.0
EPSILON = 1e-12
NEGATIVE = -1e30
BOTH = ("dp", "fsdp")
LOW = jnp.bfloat16
MIB = 1 << 20


def push(src, dst, send, recv, where):
    copy = pltpu.make_async_remote_copy(
        src_ref=src,
        dst_ref=dst,
        send_sem=send,
        recv_sem=recv,
        device_id=where,
        device_id_type=pl.DeviceIdType.MESH,
    )
    copy.start()
    return copy


def greet(peers):
    barrier = pltpu.get_barrier_semaphore()
    for peer in peers:
        pl.semaphore_signal(barrier, inc=1, device_id=peer, device_id_type=pl.DeviceIdType.MESH)
    pl.semaphore_wait(barrier, len(peers))


def flipped(index, bit):
    return index + bit - 2 * bit * (lax.div(index, bit) % 2)


def spread_body(dp, count, *refs):
    blocks, outs = refs[:count], refs[count : 2 * count]
    local, send, recv = refs[2 * count :]
    me = lax.axis_index("dp")
    own = [pltpu.make_async_copy(blocks[k], outs[k].at[me], local.at[k]) for k in range(count)]
    for copy in own:
        copy.start()
    if dp == 4:
        near = [flipped(me, 1), flipped(me, 2)]
        greet([{"dp": near[0]}, {"dp": near[1]}])
        first = []
        for k in range(count):
            for step in range(2):
                for link in range(2):
                    half = step if link == 0 else 1 - step
                    first.append(
                        push(
                            blocks[k].at[half],
                            outs[k].at[me, half],
                            send.at[k, link, half],
                            recv.at[k, link, half],
                            {"dp": near[link]},
                        )
                    )
        for k in range(count):
            for link in range(2):
                first[k * 4 + link].wait_recv()
                origin = near[link]
                other = 1 - link
                first.append(
                    push(
                        outs[k].at[origin, link],
                        outs[k].at[origin, link],
                        send.at[k, 2, other],
                        recv.at[k, 2, other],
                        {"dp": near[other]},
                    )
                )
        for place, copy in enumerate(first):
            if place >= 4 * count or place % 4 >= 2:
                copy.wait_recv()
        for copy in first:
            copy.wait_send()
    else:
        peers = [lax.rem(me + hop, dp) for hop in range(1, dp)]
        greet([{"dp": peer} for peer in peers])
        sent = []
        for k in range(count):
            for hop, peer in enumerate(peers):
                sent.append(
                    push(
                        blocks[k],
                        outs[k].at[me],
                        send.at[k, hop, 0],
                        recv.at[k, hop, 0],
                        {"dp": peer},
                    )
                )
        for copy in sent:
            copy.wait()
    for copy in own:
        copy.wait()


def spread_dp(blocks, dp, identity):
    count = len(blocks)
    rows, width = blocks[0].shape
    cut = [block.reshape(2, rows // 2, width) for block in blocks]
    outs = pl.pallas_call(
        functools.partial(spread_body, dp, count),
        out_shape=[jax.ShapeDtypeStruct((dp, 2, rows // 2, width), LOW)] * count,
        in_specs=[pl.BlockSpec(memory_space=pl.ANY)] * count,
        out_specs=[pl.BlockSpec(memory_space=pl.ANY)] * count,
        scratch_shapes=[
            pltpu.SemaphoreType.DMA((count,)),
            pltpu.SemaphoreType.DMA((count, max(3, dp - 1), 2)),
            pltpu.SemaphoreType.DMA((count, max(3, dp - 1), 2)),
        ],
        compiler_params=pltpu.CompilerParams(collective_id=identity, has_side_effects=True),
        name="spread_tables",
    )(*cut)
    return [out.reshape(dp * rows, width) for out in outs]


def fold_body(dp, pieces, g, out, near_buffer, far_buffer, last_buffer, sems):
    me = lax.axis_index("dp")
    half_rows = pieces
    if dp == 4:
        near = [flipped(me, 1), flipped(me, 2)]
        far = flipped(near[0], 2)
        greet([{"dp": near[0]}, {"dp": near[1]}])
        firsts = []
        seconds = []
        for i in range(pieces):
            for link in range(2):
                firsts.append(
                    push(
                        g.at[far, link, i],
                        far_buffer.at[link, i],
                        sems.at[0, 0, link, i],
                        sems.at[1, 0, link, i],
                        {"dp": near[link]},
                    )
                )
        for i in range(pieces):
            for link in range(2):
                firsts.append(
                    push(
                        g.at[near[link], link, i],
                        near_buffer.at[link, i],
                        sems.at[0, 1, link, i],
                        sems.at[1, 1, link, i],
                        {"dp": near[link]},
                    )
                )
        for i in range(pieces):
            for link in range(2):
                firsts[2 * i + link].wait_recv()
                far_buffer[link, i] = (
                    far_buffer[link, i].astype(jnp.float32)
                    + g[near[1 - link], link, i].astype(jnp.float32)
                ).astype(LOW)
                seconds.append(
                    push(
                        far_buffer.at[link, i],
                        last_buffer.at[link, i],
                        sems.at[0, 2, link, i],
                        sems.at[1, 2, link, i],
                        {"dp": near[1 - link]},
                    )
                )
        for i in range(pieces):
            for link in range(2):
                firsts[2 * pieces + 2 * i + link].wait_recv()
                seconds[2 * i + link].wait_recv()
                out[link, i] = (
                    g[me, link, i].astype(jnp.float32)
                    + near_buffer[link, i].astype(jnp.float32)
                    + last_buffer[link, i].astype(jnp.float32)
                )
        for copy in firsts + seconds:
            copy.wait_send()
    else:
        peers = [lax.rem(me + hop, dp) for hop in range(1, dp)]
        greet([{"dp": peer} for peer in peers])
        sent = []
        for hop, peer in enumerate(peers):
            sent.append(
                push(
                    g.at[peer],
                    near_buffer.at[hop],
                    sems.at[0, hop, 0, 0],
                    sems.at[1, hop, 0, 0],
                    {"dp": peer},
                )
            )
        out[...] = g[me].astype(jnp.float32)
        for hop in range(dp - 1):
            sent[hop].wait()
            out[...] = out[...] + near_buffer[hop].astype(jnp.float32)


def fold_dp(g, dp, pieces, identity):
    rows, width = g.shape[0] // dp, g.shape[1]
    piece = rows // (2 * pieces)
    g = g.reshape(dp, 2, pieces, piece, width)
    small = pltpu.VMEM((2, pieces, piece, width), LOW)
    first = small if dp == 4 else pltpu.VMEM((dp - 1, 2, pieces, piece, width), LOW)
    out = pl.pallas_call(
        functools.partial(fold_body, dp, pieces),
        out_shape=jax.ShapeDtypeStruct((2, pieces, piece, width), jnp.float32),
        in_specs=[pl.BlockSpec(memory_space=pltpu.VMEM)],
        out_specs=pl.BlockSpec(memory_space=pltpu.VMEM),
        scratch_shapes=[first, small, small, pltpu.SemaphoreType.DMA((2, max(3, dp - 1), 2, pieces))],
        compiler_params=pltpu.CompilerParams(
            collective_id=identity, has_side_effects=True, vmem_limit_bytes=56 * MIB
        ),
        name="fold_table",
    )(g)
    return out.reshape(rows, width)


def total_body(dp, groups, x, out, buffer, send, recv):
    steps = []
    bit = 1
    while bit < groups:
        steps.append({"fsdp": flipped(lax.axis_index("fsdp"), bit)})
        bit *= 2
    bit = 1
    while bit < dp:
        steps.append({"dp": flipped(lax.axis_index("dp"), bit)})
        bit *= 2
    greet(steps)
    buffer[0, 0] = x[...]
    for k, peer in enumerate(steps):
        copy = push(buffer.at[0, k], buffer.at[1, k], send.at[k], recv.at[k], peer)
        copy.wait()
        value = buffer[0, k] + buffer[1, k]
        if k + 1 < len(steps):
            buffer[0, k + 1] = value
        else:
            out[...] = value


def total_all(x, dp, groups, identity):
    count = (dp - 1).bit_length() + (groups - 1).bit_length()
    return pl.pallas_call(
        functools.partial(total_body, dp, groups),
        out_shape=jax.ShapeDtypeStruct((8, 128), jnp.float32),
        in_specs=[pl.BlockSpec(memory_space=pltpu.VMEM)],
        out_specs=pl.BlockSpec(memory_space=pltpu.VMEM),
        scratch_shapes=[
            pltpu.VMEM((2, count, 8, 128), jnp.float32),
            pltpu.SemaphoreType.DMA((count,)),
            pltpu.SemaphoreType.DMA((count,)),
        ],
        compiler_params=pltpu.CompilerParams(collective_id=identity, has_side_effects=True),
        name="total",
    )(x)


def product_of(form, left, right):
    return jnp.einsum(form, left, right, preferred_element_type=jnp.float32)


def owned(ids, share, padded, groups, own):
    block = ids // share
    inside = block % groups == own
    local = block // groups * padded + ids % share
    return (inside, jnp.where(inside, local, share))


def layer_norm_keep(value, gain, shift):
    mean = jnp.mean(value, axis=-1, keepdims=True)
    centred = value - mean
    inverse = lax.rsqrt(jnp.mean(centred * centred, axis=-1, keepdims=True) + EPSILON)
    normed = centred * inverse
    return (normed * gain + shift, normed, inverse)


def layer_norm_back(grad, normed, inverse, gain):
    axes = tuple(range(grad.ndim - 1))
    gain_grad = jnp.sum(grad * normed, axis=axes)
    shift_grad = jnp.sum(grad, axis=axes)
    scaled = grad * gain
    centred = scaled - jnp.mean(scaled, axis=-1, keepdims=True)
    return (
        inverse * (centred - normed * jnp.mean(scaled * normed, axis=-1, keepdims=True)),
        gain_grad,
        shift_grad,
    )


def gelu_parts(upward):
    normal_cdf = 0.5 * (1.0 + lax.erf(upward * 0.7071067811865476))
    density = jnp.exp(-0.5 * upward * upward) * 0.3989422804014327
    return (upward * normal_cdf, normal_cdf + upward * density)


def label_valid(lengths, labels, span):
    needed = (lengths * labels + span - 1) // span
    return (jnp.arange(labels)[None, :] < needed[:, None]).astype(jnp.float32)


def masked_scores(queries, keys, lengths):
    raw = product_of("bqhd,bkhd->bhqk", queries, keys)
    keep = jnp.arange(keys.shape[1])[None, :] < jnp.maximum(lengths, 1)[:, None]
    return jnp.where(keep[:, None, None, :], raw * 0.125, NEGATIVE)


def pack_layer(weights, extra):
    w_qkv, w_out, w_up, w_down, small, position = (w.astype(LOW) for w in weights)
    rows, width = w_out.shape
    pieces = [w_qkv[:, k * width : (k + 1) * width] for k in range(3)]
    pieces += [w_out]
    pieces += [w_up[:, k * width : (k + 1) * width] for k in range(w_up.shape[1] // width)]
    pieces += [w_down]
    rest = [position.T, small.T] + ([] if extra is None else [extra])
    rest = jnp.concatenate(rest, axis=1)
    pieces += [jnp.pad(rest, ((0, 0), (0, width - rest.shape[1])))]
    packed = jnp.concatenate(pieces, axis=0)
    return jnp.pad(packed, ((0, -packed.shape[0] % 32), (0, 0)))


def unpack_layer(packed, span, slots):
    devices, _, width = packed.shape
    rows = width // devices
    ff = 4 * width

    def part(first, count):
        return packed[:, first : first + count].reshape(devices * count, width)

    w_qkv = jnp.concatenate([part(k * rows, rows) for k in range(3)], axis=1)
    w_out = part(3 * rows, rows)
    w_up = jnp.concatenate([part((4 + k) * rows, rows) for k in range(4)], axis=1)
    w_down = part(8 * rows, ff // devices)
    rest = part(8 * rows + ff // devices, rows)
    position = rest[:, :span].T.astype(jnp.float32)
    small = rest[:, span : span + slots].T.astype(jnp.float32)
    return (w_qkv, w_out, w_up, w_down, small, position), rest[:, span + slots :]


def embed_forward(token_rows, weights, segment_ids):
    small, position = weights[4:]
    segment_rows = jnp.where(segment_ids[..., None] == 0, small[14], small[15])
    return layer_norm_keep(token_rows + position + segment_rows, small[12], small[13])


def layer_forward(value, weights, lengths):
    w_qkv, w_out, w_up, w_down, small = weights[:5]
    micro, span, width = value.shape
    heads = width // HD
    value_low = value.astype(LOW)
    bias = jnp.concatenate([small[0], jnp.zeros_like(small[0]), small[1]])
    joined = (product_of("bsd,df->bsf", value_low, w_qkv) + bias).astype(LOW)
    split = joined.reshape(micro, span, 3, heads, HD)
    scores = masked_scores(split[:, :, 0], split[:, :, 1], lengths)
    top = jnp.max(scores, axis=-1, keepdims=True)
    exponent = jnp.exp(scores - top)
    total = jnp.sum(exponent, axis=-1, keepdims=True)
    probs = (exponent / total).astype(LOW)
    logsum = top + jnp.log(total)
    context = (
        product_of("bhqk,bkhd->bqhd", probs, split[:, :, 2]).reshape(micro, span, width).astype(LOW)
    )
    attn = product_of("bsc,cd->bsd", context, w_out) + small[2]
    first, normed_first, inverse_first = layer_norm_keep(value + attn, small[8], small[9])
    first_low = first.astype(LOW)
    upward = product_of("bsd,df->bsf", first_low, w_up) + small[3:7].reshape(-1)
    act, slope = gelu_parts(upward)
    act_low = act.astype(LOW)
    down = product_of("bsf,fd->bsd", act_low, w_down) + small[7]
    out, normed_second, inverse_second = layer_norm_keep(first + down, small[10], small[11])
    return (
        out,
        (
            value_low,
            joined,
            logsum,
            context,
            normed_first,
            inverse_first,
            first_low,
            slope,
            act_low,
            normed_second,
            inverse_second,
        ),
    )


def layer_backward(grad, weights, kept, lengths):
    w_qkv, w_out, w_up, w_down, small = weights[:5]
    (
        value_low,
        joined,
        logsum,
        context,
        normed_first,
        inverse_first,
        first_low,
        slope,
        act_low,
        normed_second,
        inverse_second,
    ) = kept
    micro, span, width = value_low.shape
    heads = width // HD
    d_second, gain_second, shift_second = layer_norm_back(
        grad, normed_second, inverse_second, small[10]
    )
    d_down = d_second.astype(LOW)
    g_down = product_of("bsf,bsd->fd", act_low, d_down)
    d_up = (product_of("bsd,fd->bsf", d_down, w_down) * slope).astype(LOW)
    g_up = product_of("bsd,bsf->df", first_low, d_up)
    d_first = d_second + product_of("bsf,df->bsd", d_up, w_up)
    d_sum, gain_first, shift_first = layer_norm_back(d_first, normed_first, inverse_first, small[8])
    d_attn = d_sum.astype(LOW)
    g_out = product_of("bsc,bsd->cd", context, d_attn)
    d_context = (
        product_of("bsd,cd->bsc", d_attn, w_out).astype(LOW).reshape(micro, span, heads, HD)
    )
    split = joined.reshape(micro, span, 3, heads, HD)
    probs = jnp.exp(masked_scores(split[:, :, 0], split[:, :, 1], lengths) - logsum)
    g_values = product_of("bhqk,bqhd->bkhd", probs.astype(LOW), d_context)
    d_probs = product_of("bqhd,bkhd->bhqk", d_context, split[:, :, 2])
    d_scores = (probs * (d_probs - jnp.sum(probs * d_probs, axis=-1, keepdims=True))).astype(LOW)
    g_queries = product_of("bhqk,bkhd->bqhd", d_scores, split[:, :, 1]) * 0.125
    g_keys = product_of("bhqk,bqhd->bkhd", d_scores, split[:, :, 0]) * 0.125
    d_joined = (
        jnp.stack([g_queries, g_keys, g_values], axis=2)
        .reshape(micro, span, 3 * width)
        .astype(LOW)
    )
    g_qkv = product_of("bsd,bsf->df", value_low, d_joined)
    d_value = d_sum + product_of("bsf,df->bsd", d_joined, w_qkv)

    def column_sum(value):
        return jnp.sum(value.astype(jnp.float32), axis=(0, 1))

    joined_sum = column_sum(d_joined)
    rows_grad = jnp.concatenate(
        [
            joined_sum[:width][None],
            joined_sum[2 * width :][None],
            column_sum(d_attn)[None],
            column_sum(d_up).reshape(-1, width),
            column_sum(d_down)[None],
            gain_first[None],
            shift_first[None],
            gain_second[None],
            shift_second[None],
        ]
    )
    return ((g_qkv, g_out, g_up, g_down), rows_grad, d_value)


def label_head(
    student_out, teacher_out, places, tables, targets, valid_mask, own, share, padded, groups, count
):
    table_student, table_teacher = tables
    vocab_rows = table_student.shape[0]
    micro, span, width = student_out.shape
    mine = places.size
    pick = (places[..., None] == jnp.arange(span)).astype(LOW)
    rows = jnp.stack(
        [
            product_of("bps,bsd->bpd", pick, out.astype(LOW)).astype(LOW).reshape(mine, width)
            for out in (student_out, teacher_out)
        ]
    )
    rows_all = lax.all_gather(rows, "fsdp", axis=1, tiled=True)
    all_student = rows_all[0]
    all_teacher = rows_all[1]
    row_index = jnp.arange(vocab_rows)
    real = (row_index % padded < share)[None, :]
    inside, local_target = owned(targets, share, padded, groups, own)
    hit = (row_index[None, :] == local_target[:, None]) & inside[:, None]
    student = jnp.where(real, product_of("pd,vd->pv", all_student, table_student), NEGATIVE)
    teacher = jnp.where(real, product_of("pd,vd->pv", all_teacher, table_teacher), NEGATIVE)
    top_student = jnp.max(student, axis=1)
    top_teacher = jnp.max(teacher, axis=1)
    half = jnp.exp((student - top_student[:, None]) / SOFTMAX_HEAT)
    teacher_exp = jnp.exp((teacher - top_teacher[:, None]) / SOFTMAX_HEAT)
    stats = jnp.stack(
        [
            top_student,
            jnp.sum(half * half, axis=1),
            jnp.sum(half, axis=1),
            top_teacher,
            jnp.sum(teacher_exp, axis=1),
            jnp.sum(teacher_exp * ((teacher - student) / SOFTMAX_HEAT), axis=1),
            jnp.sum(jnp.where(hit, student, 0.0), axis=1),
            jnp.zeros_like(top_student),
        ]
    )
    stats = lax.all_gather(stats, "fsdp")
    peak_student = jnp.max(stats[:, 0], axis=0)
    peak_teacher = jnp.max(stats[:, 3], axis=0)
    fall_student = jnp.exp((stats[:, 0] - peak_student) / SOFTMAX_HEAT)
    fall_teacher = jnp.exp((stats[:, 3] - peak_teacher) / SOFTMAX_HEAT)
    sum_plain = jnp.sum(stats[:, 1] * fall_student * fall_student, axis=0)
    sum_soft = jnp.sum(stats[:, 2] * fall_student, axis=0)
    sum_teacher = jnp.sum(stats[:, 4] * fall_teacher, axis=0)
    cross = jnp.sum(stats[:, 5] * fall_teacher, axis=0)
    target_logit = jnp.sum(stats[:, 6], axis=0)
    lse_plain = peak_student + jnp.log(sum_plain)
    lse_soft = peak_student / SOFTMAX_HEAT + jnp.log(sum_soft)
    lse_teacher = peak_teacher / SOFTMAX_HEAT + jnp.log(sum_teacher)
    cross_entropy = lse_plain - target_logit
    divergence_loss = cross / sum_teacher - lse_teacher + lse_soft
    share_lab = valid_mask / count
    hard = jnp.exp(student - lse_plain[:, None]) - hit.astype(jnp.float32)
    soft = jnp.exp(student / SOFTMAX_HEAT - lse_soft[:, None]) - jnp.exp(
        teacher / SOFTMAX_HEAT - lse_teacher[:, None]
    )
    d_logits = (
        share_lab[:, None]
        * ((1.0 - SOFT_FRACTION) * hard + SOFT_FRACTION * SOFTMAX_HEAT * soft)
    ).astype(LOW)
    d_rows = lax.psum_scatter(
        product_of("pv,vd->pd", d_logits, table_student).astype(LOW),
        "fsdp",
        scatter_dimension=0,
        tiled=True,
    )
    table_term = product_of("pv,pd->vd", d_logits, all_student)
    terms = share_lab * (
        (1.0 - SOFT_FRACTION) * cross_entropy
        + SOFT_FRACTION * SOFTMAX_HEAT * SOFTMAX_HEAT * divergence_loss
    )
    local = lax.dynamic_slice_in_dim(terms, own * mine, mine)
    d_out = product_of("bps,bpd->bsd", pick, d_rows.reshape(micro, -1, width))
    return (d_out, table_term, jnp.sum(local))


def pack_grads(matrices, small_grad, position_grad, devices):
    g_qkv, g_out, g_up, g_down = (g.astype(LOW) for g in matrices)
    width = g_qkv.shape[0]
    ff = g_down.shape[0]
    parts = ff // width
    g_down = (
        g_down.reshape(devices, parts, width // devices, width)
        .transpose(0, 2, 1, 3)
        .reshape(width, ff)
    )
    pad = -small_grad.shape[0] % 128
    return jnp.concatenate(
        [
            g_qkv,
            g_out,
            g_up,
            g_down,
            position_grad.astype(LOW).T,
            jnp.pad(small_grad, ((0, pad), (0, 0))).astype(LOW).T,
        ],
        axis=1,
    )


def unpack_grads(packed, width, span, slots):
    ff = 4 * width
    packed = packed.astype(jnp.float32)
    edges = [3 * width, 4 * width, 4 * width + ff, 4 * width + 2 * ff]
    down = packed[:, edges[2] : edges[3]]
    g_down = jnp.concatenate([down[:, k * width : (k + 1) * width] for k in range(4)], axis=0)
    return (
        packed[:, : edges[0]],
        packed[:, edges[0] : edges[1]],
        packed[:, edges[1] : edges[2]],
        g_down,
        packed[:, edges[3] + span : edges[3] + span + slots].T,
        packed[:, edges[3] : edges[3] + span].T,
    )


def unit_of(cls):
    scale = lax.rsqrt(jnp.sum(cls * cls, axis=-1, keepdims=True) + 1e-06)
    return cls * scale, scale


def on_device(
    tok_ids,
    segments,
    seq_len,
    label_pos,
    label_ids,
    table,
    w_qkv,
    w_out,
    w_up,
    w_down,
    small,
    position,
    t_table,
    t_qkv,
    t_out,
    t_up,
    t_down,
    t_small,
    t_position,
    mom_table,
    mom_qkv,
    mom_out,
    mom_up,
    mom_down,
    mom_small,
    mom_position,
    avg_table,
    avg_qkv,
    avg_out,
    avg_up,
    avg_down,
    avg_small,
    avg_position,
):
    micro, span = tok_ids.shape
    labels = label_pos.shape[1]
    share, width = table.shape
    groups = lax.axis_size("fsdp")
    dp = lax.axis_size("dp")
    devices = groups * dp
    own = lax.axis_index("fsdp")
    padded = (share // 32 + 1) * 32
    pad = padded - share
    rows_own = w_qkv.shape[0]
    slots = small.shape[0]

    info = jnp.concatenate(
        [tok_ids, label_ids, jnp.broadcast_to(seq_len[:, None], (micro, labels))], axis=1
    )
    info = lax.all_gather(info, "fsdp", axis=0, tiled=True)
    ids_all = info[:, :span]
    targets_all = info[:, span : span + labels].reshape(-1)
    lengths_all = info[:, span + labels]
    student_table = spread_dp([jnp.pad(table.astype(LOW), ((0, pad), (0, 0)))], dp, 1)[0]
    teacher_table = spread_dp([jnp.pad(t_table, ((0, pad), (0, 0)))], dp, 2)[0]
    tables = (student_table, teacher_table)
    vocab_rows = student_table.shape[0]

    valid_local = label_valid(seq_len, labels, span)
    counts = jnp.stack([jnp.sum(valid_local), jnp.sum((seq_len > 0).astype(jnp.float32))])
    extra = jnp.broadcast_to(counts.astype(LOW)[None, :], (rows_own, 2))

    safe_ids = owned(ids_all, share, padded, groups, own)[1]
    tokens_student = lax.psum_scatter(
        student_table[safe_ids], "fsdp", scatter_dimension=0, tiled=True
    ).astype(jnp.float32)
    tokens_teacher = lax.psum_scatter(
        teacher_table[safe_ids], "fsdp", scatter_dimension=0, tiled=True
    ).astype(jnp.float32)

    packed_student = pack_layer((w_qkv, w_out, w_up, w_down, small, position), extra)
    packed_teacher = pack_layer((t_qkv, t_out, t_up, t_down, t_small, t_position), None)
    packed_student = lax.all_gather(packed_student, BOTH)
    packed_teacher = lax.all_gather(packed_teacher, BOTH)
    weights, rest = unpack_layer(packed_student, span, slots)
    teacher, _ = unpack_layer(packed_teacher, span, slots)
    counted = jnp.sum(rest[::rows_own, :2].astype(jnp.float32), axis=0)
    label_count, count_seq = counted[0], counted[1]

    start, normed_start, inverse_start = embed_forward(tokens_student, weights, segments)
    teacher_start = embed_forward(tokens_teacher, teacher, segments)[0]
    student_out, kept = layer_forward(start, weights, seq_len)
    teacher_out = layer_forward(teacher_start, teacher, seq_len)[0]
    valid_group = label_valid(lengths_all, labels, span).reshape(-1)
    d_out, table_grad, label_loss = label_head(
        student_out,
        teacher_out,
        label_pos,
        tables,
        targets_all,
        valid_group,
        own,
        share,
        padded,
        groups,
        label_count,
    )
    cls_student = student_out[:, 0]
    unit_student, scale_student = unit_of(cls_student)
    unit_teacher = unit_of(teacher_out[:, 0])[0]
    weight_pkd = (PKD_WEIGHT * (seq_len > 0).astype(jnp.float32) / count_seq)[:, None]
    gap = unit_student - unit_teacher
    d_unit = 2.0 * weight_pkd * gap
    d_cls = scale_student * d_unit - cls_student * scale_student**3 * jnp.sum(
        cls_student * d_unit, axis=-1, keepdims=True
    )
    first_row = (jnp.arange(span) == 0).astype(jnp.float32)[None, :, None]
    d_out = d_out + first_row * d_cls[:, None, :]
    loss_part = label_loss + jnp.sum(weight_pkd * gap * gap)

    matrices, rows_grad, d_start = layer_backward(d_out, weights, kept, seq_len)
    d_embed, gain_embed, shift_embed = layer_norm_back(
        d_start, normed_start, inverse_start, weights[4][12]
    )
    zero_segment = (segments == 0).astype(jnp.float32)[..., None]
    small_grad = jnp.concatenate(
        [
            rows_grad,
            gain_embed[None],
            shift_embed[None],
            jnp.sum(d_embed * zero_segment, axis=(0, 1))[None],
            jnp.sum(d_embed * (1.0 - zero_segment), axis=(0, 1))[None],
        ]
    )
    embed_grads = lax.all_gather(d_embed.astype(LOW), "fsdp", axis=0, tiled=True)
    packed_grads = pack_grads(matrices, small_grad, jnp.sum(d_embed, axis=0), devices)
    packed_grads = lax.psum_scatter(packed_grads, BOTH, scatter_dimension=0, tiled=True)
    table_grad = table_grad + jax.ops.segment_sum(
        embed_grads.astype(jnp.float32).reshape(-1, width),
        safe_ids.reshape(-1),
        num_segments=vocab_rows,
    )
    table_shard = fold_dp(table_grad.astype(LOW), dp, 1, 3)[:share]
    grads = (table_shard,) + unpack_grads(packed_grads, width, span, slots)
    squares = jnp.zeros((), jnp.float32)
    for grad in grads:
        squares = squares + jnp.sum(grad * grad)
    column = jnp.arange(128)[None, :]
    sums = jnp.where(column == 0, squares, jnp.where(column == 1, loss_part, 0.0))
    sums = total_all(jnp.broadcast_to(sums, (8, 128)), dp, groups, 4)
    total_sq, loss_value = sums[0, 0], sums[0, 1]
    grad_norm = jnp.sqrt(total_sq)
    factor = CLIP / jnp.maximum(grad_norm, CLIP)
    rate = RATE_SCALE * math.sqrt(NPARAM)
    params = (table, w_qkv, w_out, w_up, w_down, small, position)
    moms = (mom_table, mom_qkv, mom_out, mom_up, mom_down, mom_small, mom_position)
    avgs = (avg_table, avg_qkv, avg_out, avg_up, avg_down, avg_small, avg_position)
    news, moments, averages = ([], [], [])
    for weight, grad, momentum, average in zip(params, grads, moms, avgs):
        clipped = grad * factor
        moment = MOMENTUM * momentum + clipped
        fresh = weight - rate * (clipped + MOMENTUM * moment)
        news.append(fresh)
        moments.append(moment)
        averages.append(AVERAGE * average + (1.0 - AVERAGE) * fresh)
    return tuple(news) + tuple(moments) + tuple(averages) + (grad_norm, loss_value)


def solution(mesh):
    placed = (
        P(("dp", "fsdp"), None),
        P(("dp", "fsdp"), None),
        P(("dp", "fsdp")),
        P(("dp", "fsdp"), None),
        P(("dp", "fsdp"), None),
        P(("dp", "fsdp"), None),
        P(("dp", "fsdp"), None),
        P(("dp", "fsdp"), None),
        P(("dp", "fsdp"), None),
        P(("dp", "fsdp"), None),
        P(None, ("dp", "fsdp")),
        P(None, ("dp", "fsdp")),
        P(("dp", "fsdp"), None),
        P(("dp", "fsdp"), None),
        P(("dp", "fsdp"), None),
        P(("dp", "fsdp"), None),
        P(("dp", "fsdp"), None),
        P(None, ("dp", "fsdp")),
        P(None, ("dp", "fsdp")),
        P(("dp", "fsdp"), None),
        P(("dp", "fsdp"), None),
        P(("dp", "fsdp"), None),
        P(("dp", "fsdp"), None),
        P(("dp", "fsdp"), None),
        P(None, ("dp", "fsdp")),
        P(None, ("dp", "fsdp")),
        P(("dp", "fsdp"), None),
        P(("dp", "fsdp"), None),
        P(("dp", "fsdp"), None),
        P(("dp", "fsdp"), None),
        P(("dp", "fsdp"), None),
        P(None, ("dp", "fsdp")),
        P(None, ("dp", "fsdp")),
    )
    return jax.shard_map(
        on_device,
        mesh=mesh,
        in_specs=placed,
        out_specs=(
            P(("dp", "fsdp"), None),
            P(("dp", "fsdp"), None),
            P(("dp", "fsdp"), None),
            P(("dp", "fsdp"), None),
            P(("dp", "fsdp"), None),
            P(None, ("dp", "fsdp")),
            P(None, ("dp", "fsdp")),
            P(("dp", "fsdp"), None),
            P(("dp", "fsdp"), None),
            P(("dp", "fsdp"), None),
            P(("dp", "fsdp"), None),
            P(("dp", "fsdp"), None),
            P(None, ("dp", "fsdp")),
            P(None, ("dp", "fsdp")),
            P(("dp", "fsdp"), None),
            P(("dp", "fsdp"), None),
            P(("dp", "fsdp"), None),
            P(("dp", "fsdp"), None),
            P(("dp", "fsdp"), None),
            P(None, ("dp", "fsdp")),
            P(None, ("dp", "fsdp")),
            P(),
            P(),
        ),
        check_vma=False,
    )
```

```python
import functools
import math

import jax
import jax.numpy as jnp
from jax import lax
from jax.experimental import pallas as pl
from jax.experimental.pallas import tpu as pltpu
from jax.sharding import PartitionSpec as P

HD = 64
NPARAM = 30978048


SOFTMAX_HEAT = 2.0
SOFT_FRACTION = 0.5
PKD_WEIGHT = 10.0
MOMENTUM = 0.9
AVERAGE = 0.75
CLIP = 0.002
RATE_SCALE = 20.0
EPSILON = 1e-12
NEGATIVE = -1e30
BOTH = ("dp", "fsdp")
LOW = jnp.bfloat16
MIB = 1 << 20
CHUNK = 512


def push(src, dst, send, recv, where):
    copy = pltpu.make_async_remote_copy(
        src_ref=src,
        dst_ref=dst,
        send_sem=send,
        recv_sem=recv,
        device_id=where,
        device_id_type=pl.DeviceIdType.MESH,
    )
    copy.start()
    return copy


def greet(peers):
    barrier = pltpu.get_barrier_semaphore()
    for peer in peers:
        pl.semaphore_signal(barrier, inc=1, device_id=peer, device_id_type=pl.DeviceIdType.MESH)
    pl.semaphore_wait(barrier, len(peers))


def flipped(index, bit):
    return index + bit - 2 * bit * (lax.div(index, bit) % 2)


def spread_body(dp, count, *refs):
    blocks, outs = refs[:count], refs[count : 2 * count]
    local, send, recv = refs[2 * count :]
    me = lax.axis_index("dp")
    own = [pltpu.make_async_copy(blocks[k], outs[k].at[me], local.at[k]) for k in range(count)]
    for copy in own:
        copy.start()
    if dp == 4:
        near = [flipped(me, 1), flipped(me, 2)]
        greet([{"dp": near[0]}, {"dp": near[1]}])
        first = []
        for k in range(count):
            for step in range(2):
                for link in range(2):
                    half = step if link == 0 else 1 - step
                    first.append(
                        push(
                            blocks[k].at[half],
                            outs[k].at[me, half],
                            send.at[k, link, half],
                            recv.at[k, link, half],
                            {"dp": near[link]},
                        )
                    )
        for k in range(count):
            for link in range(2):
                first[k * 4 + link].wait_recv()
                origin = near[link]
                other = 1 - link
                first.append(
                    push(
                        outs[k].at[origin, link],
                        outs[k].at[origin, link],
                        send.at[k, 2, other],
                        recv.at[k, 2, other],
                        {"dp": near[other]},
                    )
                )
        for place, copy in enumerate(first):
            if place >= 4 * count or place % 4 >= 2:
                copy.wait_recv()
        for copy in first:
            copy.wait_send()
    else:
        peers = [lax.rem(me + hop, dp) for hop in range(1, dp)]
        greet([{"dp": peer} for peer in peers])
        sent = []
        for k in range(count):
            for hop, peer in enumerate(peers):
                sent.append(
                    push(
                        blocks[k],
                        outs[k].at[me],
                        send.at[k, hop, 0],
                        recv.at[k, hop, 0],
                        {"dp": peer},
                    )
                )
        for copy in sent:
            copy.wait()
    for copy in own:
        copy.wait()


def spread_dp(blocks, dp, identity):
    count = len(blocks)
    rows, width = blocks[0].shape
    cut = [block.reshape(2, rows // 2, width) for block in blocks]
    outs = pl.pallas_call(
        functools.partial(spread_body, dp, count),
        out_shape=[jax.ShapeDtypeStruct((dp, 2, rows // 2, width), LOW)] * count,
        in_specs=[pl.BlockSpec(memory_space=pl.ANY)] * count,
        out_specs=[pl.BlockSpec(memory_space=pl.ANY)] * count,
        scratch_shapes=[
            pltpu.SemaphoreType.DMA((count,)),
            pltpu.SemaphoreType.DMA((count, max(3, dp - 1), 2)),
            pltpu.SemaphoreType.DMA((count, max(3, dp - 1), 2)),
        ],
        compiler_params=pltpu.CompilerParams(collective_id=identity, has_side_effects=True),
        name="spread_tables",
    )(*cut)
    return [out.reshape(dp * rows, width) for out in outs]


def ways_of(me, dp):
    if dp == 4:
        return [flipped(me, 1), flipped(me, 2)]
    return [lax.rem(me + hop, dp) for hop in range(1, dp)]


def sources_of(me, dp):
    if dp == 4:
        return [flipped(me, 1), flipped(me, 2)]
    return [lax.rem(me + dp - hop, dp) for hop in range(1, dp)]


def gather_body(dp, n, count, *refs):
    blocks, outs = refs[:count], refs[count : 2 * count]
    local, z_send, z_recv, way_send, way_recv, far_send, far_recv, core_send, core_recv = refs[
        2 * count :
    ]
    me = lax.axis_index("fsdp")
    row = lax.axis_index("dp")
    p = lax.div(me, 2)
    c = lax.rem(me, 2)
    partner = me + 1 - 2 * c
    ways = ways_of(row, dp)
    sources = sources_of(row, dp)
    barrier = pltpu.get_barrier_semaphore()

    def hello(where):
        pl.semaphore_signal(barrier, inc=1, device_id=where, device_id_type=pl.DeviceIdType.MESH)

    hello({"fsdp": partner})
    for way in ways:
        hello({"dp": way})

    @pl.when(p > 0)
    def _():
        hello({"fsdp": me - 2})

    @pl.when(p < n - 1)
    def _():
        hello({"fsdp": me + 2})

    @pl.when((p > 0) & (p < n - 1))
    def _():
        pl.semaphore_wait(barrier, 3 + len(ways))

    @pl.when((p == 0) | (p == n - 1))
    def _():
        pl.semaphore_wait(barrier, 2 + len(ways))

    def remote(src, dst, send, recv, where):
        return pltpu.make_async_remote_copy(
            src_ref=src,
            dst_ref=dst,
            send_sem=send,
            recv_sem=recv,
            device_id=where,
            device_id_type=pl.DeviceIdType.MESH,
        )

    def line(m, q, side):
        shard = outs[m].at[row, 2 * q + c]
        where = {"fsdp": me + 2 - 4 * side}
        return remote(shard, shard, z_send.at[m, side, q], z_recv.at[m, q], where)

    def way_copy(m, w, half, q):
        shard = outs[m].at[row, 2 * q + c, half]
        return remote(
            shard, shard, way_send.at[m, w, half, q], way_recv.at[m, w, half, q], {"dp": ways[w]}
        )

    def far_copy(m, w, q):
        shard = outs[m].at[sources[w], 2 * q + c, w]
        return remote(
            shard, shard, far_send.at[m, w, q], far_recv.at[m, w, q], {"dp": ways[1 - w]}
        )

    def core_copy(m, j, q, half):
        shard = outs[m].at[j, 2 * q + c, half]
        return remote(
            shard,
            shard,
            core_send.at[m, j, q, half],
            core_recv.at[m, j, q, half],
            {"fsdp": partner},
        )

    def onward(m, q):
        for half in range(2):
            for w in range(len(ways)):
                way_copy(m, w, half if w == 0 else 1 - half, q).start()
        for half in range(2):
            core_copy(m, row, q, half).start()

    def landed(m, q):
        for half in range(2):
            for w in range(len(ways)):
                part = half if w == 0 else 1 - half
                way_copy(m, w, part, q).wait_recv()
                if dp == 4 and part == w:
                    far_copy(m, w, q).start()
                core_copy(m, sources[w], q, part).start()

    def far_landed(m, q):
        if dp == 4:
            for w in range(2):
                far_copy(m, w, q).wait_recv()
                core_copy(m, dp - 1 - row, q, w).start()

    def each(distance, act):
        if distance == 0:
            act(p)
            return

        @pl.when(p >= distance)
        def _():
            act(p - distance)

        @pl.when(p + distance < n)
        def _():
            act(p + distance)

    for m in range(count):
        copy = pltpu.make_async_copy(blocks[m], outs[m].at[row, me], local.at[m])
        copy.start()
        copy.wait()

        @pl.when(p < n - 1)
        def _():
            line(m, p, 0).start()

        @pl.when(p > 0)
        def _():
            line(m, p, 1).start()

        onward(m, p)
    for distance in range(1, n + 2):
        for m in range(count):
            if distance < n:

                @pl.when(p >= distance)
                def _():
                    line(m, p - distance, 0).wait_recv()

                    @pl.when(p < n - 1)
                    def _():
                        line(m, p - distance, 0).start()

                    onward(m, p - distance)

                @pl.when(p + distance < n)
                def _():
                    line(m, p + distance, 1).wait_recv()

                    @pl.when(p > 0)
                    def _():
                        line(m, p + distance, 1).start()

                    onward(m, p + distance)

            if distance <= n:
                each(distance - 1, functools.partial(landed, m))
            if distance >= 2:
                each(distance - 2, functools.partial(far_landed, m))

    def settle(q, carry):
        for m in range(count):

            @pl.when((q <= p) & (p < n - 1))
            def _():
                line(m, q, 0).wait_send()

            @pl.when((q >= p) & (p > 0))
            def _():
                line(m, q, 1).wait_send()

            for half in range(2):
                for w in range(len(ways)):
                    way_copy(m, w, half, q).wait_send()
                if dp == 4:
                    far_copy(m, half, q).wait_send()
                for j in range(dp):
                    core_copy(m, j, q, half).wait()
        return carry

    lax.fori_loop(0, n, settle, 0)


def gather_weights(blocks, dp, groups, identity):
    count = len(blocks)
    rows, width = blocks[0].shape
    n = groups // 2
    cut = [block.reshape(2, rows // 2, width) for block in blocks]
    ways = 2 if dp == 4 else dp - 1
    dma = pltpu.SemaphoreType.DMA
    outs = pl.pallas_call(
        functools.partial(gather_body, dp, n, count),
        out_shape=[jax.ShapeDtypeStruct((dp, groups, 2, rows // 2, width), LOW)] * count,
        in_specs=[pl.BlockSpec(memory_space=pl.ANY)] * count,
        out_specs=[pl.BlockSpec(memory_space=pl.ANY)] * count,
        scratch_shapes=[
            dma((count,)),
            dma((count, 2, n)),
            dma((count, n)),
            dma((count, ways, 2, n)),
            dma((count, ways, 2, n)),
            dma((count, 2, n)),
            dma((count, 2, n)),
            dma((count, dp, n, 2)),
            dma((count, dp, n, 2)),
        ],
        compiler_params=pltpu.CompilerParams(collective_id=identity, has_side_effects=True),
        name="gather_weights",
    )(*cut)
    return [out.reshape(dp * groups, rows, width) for out in outs]


def fold_body(dp, pieces, g, out, near_buffer, far_buffer, last_buffer, sems):
    me = lax.axis_index("dp")
    half_rows = pieces
    if dp == 4:
        near = [flipped(me, 1), flipped(me, 2)]
        far = flipped(near[0], 2)
        greet([{"dp": near[0]}, {"dp": near[1]}])
        firsts = []
        seconds = []
        for i in range(pieces):
            for link in range(2):
                firsts.append(
                    push(
                        g.at[far, link, i],
                        far_buffer.at[link, i],
                        sems.at[0, 0, link, i],
                        sems.at[1, 0, link, i],
                        {"dp": near[link]},
                    )
                )
        for i in range(pieces):
            for link in range(2):
                firsts.append(
                    push(
                        g.at[near[link], link, i],
                        near_buffer.at[link, i],
                        sems.at[0, 1, link, i],
                        sems.at[1, 1, link, i],
                        {"dp": near[link]},
                    )
                )
        for i in range(pieces):
            for link in range(2):
                firsts[2 * i + link].wait_recv()
                far_buffer[link, i] = (
                    far_buffer[link, i].astype(jnp.float32)
                    + g[near[1 - link], link, i].astype(jnp.float32)
                ).astype(LOW)
                seconds.append(
                    push(
                        far_buffer.at[link, i],
                        last_buffer.at[link, i],
                        sems.at[0, 2, link, i],
                        sems.at[1, 2, link, i],
                        {"dp": near[1 - link]},
                    )
                )
        for i in range(pieces):
            for link in range(2):
                firsts[2 * pieces + 2 * i + link].wait_recv()
                seconds[2 * i + link].wait_recv()
                out[link, i] = (
                    g[me, link, i].astype(jnp.float32)
                    + near_buffer[link, i].astype(jnp.float32)
                    + last_buffer[link, i].astype(jnp.float32)
                )
        for copy in firsts + seconds:
            copy.wait_send()
    else:
        peers = [lax.rem(me + hop, dp) for hop in range(1, dp)]
        greet([{"dp": peer} for peer in peers])
        sent = []
        for hop, peer in enumerate(peers):
            sent.append(
                push(
                    g.at[peer],
                    near_buffer.at[hop],
                    sems.at[0, hop, 0, 0],
                    sems.at[1, hop, 0, 0],
                    {"dp": peer},
                )
            )
        out[...] = g[me].astype(jnp.float32)
        for hop in range(dp - 1):
            sent[hop].wait()
            out[...] = out[...] + near_buffer[hop].astype(jnp.float32)


def fold_dp(g, dp, pieces, identity):
    rows, width = g.shape[0] // dp, g.shape[1]
    piece = rows // (2 * pieces)
    g = g.reshape(dp, 2, pieces, piece, width)
    small = pltpu.VMEM((2, pieces, piece, width), LOW)
    first = small if dp == 4 else pltpu.VMEM((dp - 1, 2, pieces, piece, width), LOW)
    out = pl.pallas_call(
        functools.partial(fold_body, dp, pieces),
        out_shape=jax.ShapeDtypeStruct((2, pieces, piece, width), jnp.float32),
        in_specs=[pl.BlockSpec(memory_space=pltpu.VMEM)],
        out_specs=pl.BlockSpec(memory_space=pltpu.VMEM),
        scratch_shapes=[first, small, small, pltpu.SemaphoreType.DMA((2, max(3, dp - 1), 2, pieces))],
        compiler_params=pltpu.CompilerParams(
            collective_id=identity, has_side_effects=True, vmem_limit_bytes=56 * MIB
        ),
        name="fold_table",
    )(g)
    return out.reshape(rows, width)


def total_body(dp, groups, x, out, buffer, send, recv):
    steps = []
    bit = 1
    while bit < groups:
        steps.append({"fsdp": flipped(lax.axis_index("fsdp"), bit)})
        bit *= 2
    bit = 1
    while bit < dp:
        steps.append({"dp": flipped(lax.axis_index("dp"), bit)})
        bit *= 2
    greet(steps)
    buffer[0, 0] = x[...]
    for k, peer in enumerate(steps):
        copy = push(buffer.at[0, k], buffer.at[1, k], send.at[k], recv.at[k], peer)
        copy.wait()
        value = buffer[0, k] + buffer[1, k]
        if k + 1 < len(steps):
            buffer[0, k + 1] = value
        else:
            out[...] = value


def total_all(x, dp, groups, identity):
    count = (dp - 1).bit_length() + (groups - 1).bit_length()
    return pl.pallas_call(
        functools.partial(total_body, dp, groups),
        out_shape=jax.ShapeDtypeStruct((8, 128), jnp.float32),
        in_specs=[pl.BlockSpec(memory_space=pltpu.VMEM)],
        out_specs=pl.BlockSpec(memory_space=pltpu.VMEM),
        scratch_shapes=[
            pltpu.VMEM((2, count, 8, 128), jnp.float32),
            pltpu.SemaphoreType.DMA((count,)),
            pltpu.SemaphoreType.DMA((count,)),
        ],
        compiler_params=pltpu.CompilerParams(collective_id=identity, has_side_effects=True),
        name="total",
    )(x)


def dot_over(left, right, left_dim, right_dim):
    return lax.dot_general(
        left, right, (((left_dim,), (right_dim,)), ((), ())), preferred_element_type=jnp.float32
    )


def attend_body(lengths, q_ref, k_ref, v_ref, out_ref):
    live = jnp.maximum(lengths[pl.program_id(0)], 1)
    span = q_ref.shape[1]
    k, v = k_ref[0], v_ref[0]
    keep = lax.broadcasted_iota(jnp.int32, (span, CHUNK), 0) < live
    low_lane = lax.broadcasted_iota(jnp.int32, (CHUNK, 2 * HD), 1) < HD
    for first in range(0, span, CHUNK):
        q = q_ref[0, first : first + CHUNK, :]
        parts = []
        for head in range(2):
            mine = low_lane if head == 0 else jnp.logical_not(low_lane)
            scores = dot_over(k, jnp.where(mine, q, jnp.zeros_like(q)), 1, 1)
            scores = jnp.where(keep, scores * 0.125, NEGATIVE)
            exponent = jnp.exp(scores - jnp.max(scores, axis=0, keepdims=True))
            scale = 1.0 / jnp.sum(exponent, axis=0, keepdims=True)
            parts.append(dot_over((exponent * scale).astype(LOW), v, 0, 0))
        out_ref[0, first : first + CHUNK, :] = jnp.where(low_lane, parts[0], parts[1]).astype(LOW)


def attend(joined, lengths):
    micro, span, wide = joined.shape
    width = wide // 3
    pairs = width // (2 * HD)

    def place(third):
        return pl.BlockSpec((1, span, 2 * HD), lambda b, h, _: (b, 0, third * pairs + h))

    return pl.pallas_call(
        attend_body,
        grid_spec=pltpu.PrefetchScalarGridSpec(
            num_scalar_prefetch=1,
            grid=(micro, pairs),
            in_specs=[place(0), place(1), place(2)],
            out_specs=pl.BlockSpec((1, span, 2 * HD), lambda b, h, _: (b, 0, h)),
        ),
        out_shape=jax.ShapeDtypeStruct((micro, span, width), LOW),
        cost_estimate=pl.CostEstimate(
            flops=4 * micro * span * span * width,
            bytes_accessed=8 * micro * span * width,
            transcendentals=micro * span * span * width // HD,
        ),
        name="attend",
    )(lengths, joined, joined, joined)


def attend_back_body(lengths, q_ref, k_ref, v_ref, d_ref, out_ref, g_keys, g_values):
    live = jnp.maximum(lengths[pl.program_id(0)], 1)
    span = q_ref.shape[1]
    k, v = k_ref[0], v_ref[0]
    keep = lax.broadcasted_iota(jnp.int32, (span, CHUNK), 0) < live
    low_lane = lax.broadcasted_iota(jnp.int32, (CHUNK, 2 * HD), 1) < HD
    low_wide = lax.broadcasted_iota(jnp.int32, (span, 2 * HD), 1) < HD
    for first in range(0, span, CHUNK):
        q = q_ref[0, first : first + CHUNK, :]
        d = d_ref[0, first : first + CHUNK, :]
        parts = []
        for head in range(2):
            mine = low_lane if head == 0 else jnp.logical_not(low_lane)
            scores = dot_over(k, jnp.where(mine, q, jnp.zeros_like(q)), 1, 1)
            scores = jnp.where(keep, scores * 0.125, NEGATIVE)
            exponent = jnp.exp(scores - jnp.max(scores, axis=0, keepdims=True))
            probs = exponent * (1.0 / jnp.sum(exponent, axis=0, keepdims=True))
            d_probs = dot_over(v, jnp.where(mine, d, jnp.zeros_like(d)), 1, 1)
            inner = jnp.sum(probs * d_probs, axis=0, keepdims=True)
            d_scores = (probs * (d_probs - inner)).astype(LOW)
            value_part = dot_over(probs.astype(LOW), d, 1, 0)
            key_part = dot_over(d_scores, q, 1, 0)
            if first == 0:
                g_values[head] = value_part
                g_keys[head] = key_part
            else:
                g_values[head] += value_part
                g_keys[head] += key_part
            parts.append(dot_over(d_scores, k, 0, 0))
        out_ref[0, 0, first : first + CHUNK, :] = (
            jnp.where(low_lane, parts[0], parts[1]) * 0.125
        ).astype(LOW)
    out_ref[1, 0] = (jnp.where(low_wide, g_keys[0], g_keys[1]) * 0.125).astype(LOW)
    out_ref[2, 0] = jnp.where(low_wide, g_values[0], g_values[1]).astype(LOW)


def attend_back(joined, d_context, lengths):
    micro, span, width = d_context.shape
    pairs = width // (2 * HD)

    def place(third):
        return pl.BlockSpec((1, span, 2 * HD), lambda b, h, _: (b, 0, third * pairs + h))

    return pl.pallas_call(
        attend_back_body,
        grid_spec=pltpu.PrefetchScalarGridSpec(
            num_scalar_prefetch=1,
            grid=(micro, pairs),
            in_specs=[place(0), place(1), place(2), place(0)],
            out_specs=pl.BlockSpec((3, 1, span, 2 * HD), lambda b, h, _: (0, b, 0, h)),
            scratch_shapes=[
                pltpu.VMEM((2, span, 2 * HD), jnp.float32),
                pltpu.VMEM((2, span, 2 * HD), jnp.float32),
            ],
        ),
        out_shape=jax.ShapeDtypeStruct((3, micro, span, width), LOW),
        cost_estimate=pl.CostEstimate(
            flops=10 * micro * span * span * width,
            bytes_accessed=14 * micro * span * width,
            transcendentals=micro * span * span * width // HD,
        ),
        name="attend_back",
    )(lengths, joined, joined, joined, d_context)


def product_of(form, left, right):
    return jnp.einsum(form, left, right, preferred_element_type=jnp.float32)


def owned(ids, share, padded, groups, own):
    block = ids // share
    inside = block % groups == own
    local = block // groups * padded + ids % share
    return (inside, jnp.where(inside, local, share))


def layer_norm_keep(value, gain, shift):
    mean = jnp.mean(value, axis=-1, keepdims=True)
    centred = value - mean
    inverse = lax.rsqrt(jnp.mean(centred * centred, axis=-1, keepdims=True) + EPSILON)
    normed = centred * inverse
    return (normed * gain + shift, normed, inverse)


def layer_norm_back(grad, normed, inverse, gain):
    axes = tuple(range(grad.ndim - 1))
    gain_grad = jnp.sum(grad * normed, axis=axes)
    shift_grad = jnp.sum(grad, axis=axes)
    scaled = grad * gain
    centred = scaled - jnp.mean(scaled, axis=-1, keepdims=True)
    return (
        inverse * (centred - normed * jnp.mean(scaled * normed, axis=-1, keepdims=True)),
        gain_grad,
        shift_grad,
    )


def gelu_parts(upward):
    normal_cdf = 0.5 * (1.0 + lax.erf(upward * 0.7071067811865476))
    density = jnp.exp(-0.5 * upward * upward) * 0.3989422804014327
    return (upward * normal_cdf, normal_cdf + upward * density)


def label_valid(lengths, labels, span):
    needed = (lengths * labels + span - 1) // span
    return (jnp.arange(labels)[None, :] < needed[:, None]).astype(jnp.float32)


def pack_layer(weights, extra):
    w_qkv, w_out, w_up, w_down, small, position = (w.astype(LOW) for w in weights)
    rows, width = w_out.shape
    pieces = [w_qkv[:, k * width : (k + 1) * width] for k in range(3)]
    pieces += [w_out]
    pieces += [w_up[:, k * width : (k + 1) * width] for k in range(w_up.shape[1] // width)]
    pieces += [w_down]
    rest = [position.T, small.T] + ([] if extra is None else [extra])
    rest = jnp.concatenate(rest, axis=1)
    pieces += [jnp.pad(rest, ((0, 0), (0, width - rest.shape[1])))]
    packed = jnp.concatenate(pieces, axis=0)
    return jnp.pad(packed, ((0, -packed.shape[0] % 32), (0, 0)))


def unpack_layer(packed, span, slots):
    devices, _, width = packed.shape
    rows = width // devices
    ff = 4 * width

    def part(first, count):
        return packed[:, first : first + count].reshape(devices * count, width)

    w_qkv = jnp.concatenate([part(k * rows, rows) for k in range(3)], axis=1)
    w_out = part(3 * rows, rows)
    w_up = jnp.concatenate([part((4 + k) * rows, rows) for k in range(4)], axis=1)
    w_down = part(8 * rows, ff // devices)
    rest = part(8 * rows + ff // devices, rows)
    position = rest[:, :span].T.astype(jnp.float32)
    small = rest[:, span : span + slots].T.astype(jnp.float32)
    return (w_qkv, w_out, w_up, w_down, small, position), rest[:, span + slots :]


def embed_forward(token_rows, weights, segment_ids):
    small, position = weights[4:]
    segment_rows = jnp.where(segment_ids[..., None] == 0, small[14], small[15])
    return layer_norm_keep(token_rows + position + segment_rows, small[12], small[13])


def layer_forward(value, weights, lengths):
    w_qkv, w_out, w_up, w_down, small = weights[:5]
    micro, span, width = value.shape
    value_low = value.astype(LOW)
    bias = jnp.concatenate([small[0], jnp.zeros_like(small[0]), small[1]])
    joined = (product_of("bsd,df->bsf", value_low, w_qkv) + bias).astype(LOW)
    context = attend(joined, lengths)
    attn = product_of("bsc,cd->bsd", context, w_out) + small[2]
    first, normed_first, inverse_first = layer_norm_keep(value + attn, small[8], small[9])
    first_low = first.astype(LOW)
    upward = product_of("bsd,df->bsf", first_low, w_up) + small[3:7].reshape(-1)
    act, slope = gelu_parts(upward)
    act_low = act.astype(LOW)
    down = product_of("bsf,fd->bsd", act_low, w_down) + small[7]
    out, normed_second, inverse_second = layer_norm_keep(first + down, small[10], small[11])
    return (
        out,
        (
            value_low,
            joined,
            context,
            normed_first,
            inverse_first,
            first_low,
            slope,
            act_low,
            normed_second,
            inverse_second,
        ),
    )


def layer_backward(grad, weights, kept, lengths, devices):
    w_qkv, w_out, w_up, w_down, small = weights[:5]
    (
        value_low,
        joined,
        context,
        normed_first,
        inverse_first,
        first_low,
        slope,
        act_low,
        normed_second,
        inverse_second,
    ) = kept
    micro, span, width = value_low.shape
    d_second, gain_second, shift_second = layer_norm_back(
        grad, normed_second, inverse_second, small[10]
    )
    d_down = d_second.astype(LOW)
    g_down = product_of("bsf,bsd->fd", act_low, d_down)
    d_up = (product_of("bsd,fd->bsf", d_down, w_down) * slope).astype(LOW)
    g_up = product_of("bsd,bsf->df", first_low, d_up)
    d_first = d_second + product_of("bsf,df->bsd", d_up, w_up)
    wide = pack_wide(g_up, g_down, devices)
    d_first, wide = lax.optimization_barrier((d_first, wide))
    wide = lax.psum_scatter(wide, BOTH, scatter_dimension=0, tiled=True)
    d_sum, gain_first, shift_first = layer_norm_back(d_first, normed_first, inverse_first, small[8])
    d_attn = d_sum.astype(LOW)
    d_context = product_of("bsd,cd->bsc", d_attn, w_out).astype(LOW)
    d_joined = jnp.concatenate(list(attend_back(joined, d_context, lengths)), axis=-1)
    d_value = d_sum + product_of("bsf,df->bsd", d_joined, w_qkv)

    def column_sum(value):
        return jnp.sum(value.astype(jnp.float32), axis=(0, 1))

    joined_sum = column_sum(d_joined)
    rows_grad = jnp.concatenate(
        [
            joined_sum[:width][None],
            joined_sum[2 * width :][None],
            column_sum(d_attn)[None],
            column_sum(d_up).reshape(-1, width),
            column_sum(d_down)[None],
            gain_first[None],
            shift_first[None],
            gain_second[None],
            shift_second[None],
        ]
    )
    return wide, (value_low, d_joined, context, d_attn), rows_grad, d_value


def label_rows(pick, out):
    micro, labels, _ = pick.shape
    rows = product_of("bps,bsd->bpd", pick, out.astype(LOW)).astype(LOW)
    return rows.reshape(micro * labels, out.shape[-1])


def label_head(
    all_student, all_teacher, pick, tables, targets, valid_mask, own, share, padded, groups, count
):
    table_student, table_teacher = tables
    vocab_rows = table_student.shape[0]
    micro, labels, span = pick.shape
    width = all_student.shape[1]
    mine = micro * labels
    row_index = jnp.arange(vocab_rows)
    real = (row_index % padded < share)[None, :]
    inside, local_target = owned(targets, share, padded, groups, own)
    hit = (row_index[None, :] == local_target[:, None]) & inside[:, None]
    student = jnp.where(real, product_of("pd,vd->pv", all_student, table_student), NEGATIVE)
    teacher = jnp.where(real, product_of("pd,vd->pv", all_teacher, table_teacher), NEGATIVE)
    top_student = jnp.max(student, axis=1)
    top_teacher = jnp.max(teacher, axis=1)
    half = jnp.exp((student - top_student[:, None]) / SOFTMAX_HEAT)
    teacher_exp = jnp.exp((teacher - top_teacher[:, None]) / SOFTMAX_HEAT)
    stats = jnp.stack(
        [
            top_student,
            jnp.sum(half * half, axis=1),
            jnp.sum(half, axis=1),
            top_teacher,
            jnp.sum(teacher_exp, axis=1),
            jnp.sum(teacher_exp * ((teacher - student) / SOFTMAX_HEAT), axis=1),
            jnp.sum(jnp.where(hit, student, 0.0), axis=1),
            jnp.zeros_like(top_student),
        ]
    )
    stats = lax.all_gather(stats, "fsdp")
    peak_student = jnp.max(stats[:, 0], axis=0)
    peak_teacher = jnp.max(stats[:, 3], axis=0)
    fall_student = jnp.exp((stats[:, 0] - peak_student) / SOFTMAX_HEAT)
    fall_teacher = jnp.exp((stats[:, 3] - peak_teacher) / SOFTMAX_HEAT)
    sum_plain = jnp.sum(stats[:, 1] * fall_student * fall_student, axis=0)
    sum_soft = jnp.sum(stats[:, 2] * fall_student, axis=0)
    sum_teacher = jnp.sum(stats[:, 4] * fall_teacher, axis=0)
    cross = jnp.sum(stats[:, 5] * fall_teacher, axis=0)
    target_logit = jnp.sum(stats[:, 6], axis=0)
    lse_plain = peak_student + jnp.log(sum_plain)
    lse_soft = peak_student / SOFTMAX_HEAT + jnp.log(sum_soft)
    lse_teacher = peak_teacher / SOFTMAX_HEAT + jnp.log(sum_teacher)
    cross_entropy = lse_plain - target_logit
    divergence_loss = cross / sum_teacher - lse_teacher + lse_soft
    share_lab = valid_mask / count
    hard = jnp.exp(student - lse_plain[:, None]) - hit.astype(jnp.float32)
    soft = jnp.exp(student / SOFTMAX_HEAT - lse_soft[:, None]) - jnp.exp(
        teacher / SOFTMAX_HEAT - lse_teacher[:, None]
    )
    d_logits = (
        share_lab[:, None]
        * ((1.0 - SOFT_FRACTION) * hard + SOFT_FRACTION * SOFTMAX_HEAT * soft)
    ).astype(LOW)
    d_rows = lax.psum_scatter(
        product_of("pv,vd->pd", d_logits, table_student).astype(LOW),
        "fsdp",
        scatter_dimension=0,
        tiled=True,
    )
    table_term = product_of("pv,pd->vd", d_logits, all_student)
    d_rows, table_term = lax.optimization_barrier((d_rows, table_term))
    terms = share_lab * (
        (1.0 - SOFT_FRACTION) * cross_entropy
        + SOFT_FRACTION * SOFTMAX_HEAT * SOFTMAX_HEAT * divergence_loss
    )
    local = lax.dynamic_slice_in_dim(terms, own * mine, mine)
    d_out = product_of("bps,bpd->bsd", pick, d_rows.reshape(micro, -1, width))
    return (d_out, table_term, jnp.sum(local))


def pack_wide(g_up, g_down, devices):
    width = g_up.shape[0]
    ff = g_down.shape[0]
    g_down = (
        g_down.astype(LOW)
        .reshape(devices, ff // width, width // devices, width)
        .transpose(0, 2, 1, 3)
        .reshape(width, ff)
    )
    return jnp.concatenate([g_up.astype(LOW), g_down], axis=1)


def pack_narrow(g_qkv, g_out, small_grad, position_grad):
    pad = -small_grad.shape[0] % 128
    return jnp.concatenate(
        [
            g_qkv.astype(LOW),
            g_out.astype(LOW),
            position_grad.astype(LOW).T,
            jnp.pad(small_grad, ((0, pad), (0, 0))).astype(LOW).T,
        ],
        axis=1,
    )


def unpack_grads(wide, narrow, width, span, slots):
    ff = 4 * width
    wide = wide.astype(jnp.float32)
    narrow = narrow.astype(jnp.float32)
    down = wide[:, ff:]
    g_down = jnp.concatenate([down[:, k * width : (k + 1) * width] for k in range(4)], axis=0)
    return (
        narrow[:, : 3 * width],
        narrow[:, 3 * width : 4 * width],
        wide[:, :ff],
        g_down,
        narrow[:, 4 * width + span : 4 * width + span + slots].T,
        narrow[:, 4 * width : 4 * width + span].T,
    )


def unit_of(cls):
    scale = lax.rsqrt(jnp.sum(cls * cls, axis=-1, keepdims=True) + 1e-06)
    return cls * scale, scale


def on_device(
    tok_ids,
    segments,
    seq_len,
    label_pos,
    label_ids,
    table,
    w_qkv,
    w_out,
    w_up,
    w_down,
    small,
    position,
    t_table,
    t_qkv,
    t_out,
    t_up,
    t_down,
    t_small,
    t_position,
    mom_table,
    mom_qkv,
    mom_out,
    mom_up,
    mom_down,
    mom_small,
    mom_position,
    avg_table,
    avg_qkv,
    avg_out,
    avg_up,
    avg_down,
    avg_small,
    avg_position,
):
    micro, span = tok_ids.shape
    labels = label_pos.shape[1]
    share, width = table.shape
    groups = lax.axis_size("fsdp")
    dp = lax.axis_size("dp")
    devices = groups * dp
    own = lax.axis_index("fsdp")
    padded = (share // 32 + 1) * 32
    pad = padded - share
    rows_own = w_qkv.shape[0]
    slots = small.shape[0]

    info = jnp.concatenate(
        [tok_ids, label_ids, jnp.broadcast_to(seq_len[:, None], (micro, labels))], axis=1
    )
    info = lax.all_gather(info, "fsdp", axis=0, tiled=True)
    ids_all = info[:, :span]
    targets_all = info[:, span : span + labels].reshape(-1)
    lengths_all = info[:, span + labels]
    student_table = spread_dp([jnp.pad(table.astype(LOW), ((0, pad), (0, 0)))], dp, 1)[0]
    valid_local = label_valid(seq_len, labels, span)
    counts = jnp.stack([jnp.sum(valid_local), jnp.sum((seq_len > 0).astype(jnp.float32))])
    extra = jnp.broadcast_to(counts.astype(LOW)[None, :], (rows_own, 2))

    safe_ids = owned(ids_all, share, padded, groups, own)[1]
    packed_teacher = pack_layer((t_qkv, t_out, t_up, t_down, t_small, t_position), None)
    packed_teacher = lax.all_gather(packed_teacher, BOTH)
    safe_flat = safe_ids.reshape(-1)
    student_hits = student_table[safe_flat].reshape(groups * micro, span, width)
    student_hits, t_table = lax.optimization_barrier((student_hits, t_table))
    teacher_table = spread_dp([jnp.pad(t_table, ((0, pad), (0, 0)))], dp, 2)[0]
    tokens_student = lax.psum_scatter(
        student_hits,
        "fsdp",
        scatter_dimension=0,
        tiled=True,
    ).astype(jnp.float32)
    teacher_hits = teacher_table[safe_flat].reshape(groups * micro, span, width)
    s_weights, teacher_hits, packed_teacher = lax.optimization_barrier(
        ((w_qkv, w_out, w_up, w_down, small, position), teacher_hits, packed_teacher)
    )
    tokens_teacher = lax.psum_scatter(teacher_hits, "fsdp", scatter_dimension=0, tiled=True)
    packed_student = gather_weights([pack_layer(s_weights, extra)], dp, groups, 5)[0]
    weights, rest = unpack_layer(packed_student, span, slots)
    counted = jnp.sum(rest[::rows_own, :2].astype(jnp.float32), axis=0)
    label_count, count_seq = counted[0], counted[1]

    tables = (student_table, teacher_table)
    vocab_rows = student_table.shape[0]
    start, normed_start, inverse_start = embed_forward(tokens_student, weights, segments)
    student_out, kept = layer_forward(start, weights, seq_len)
    pick = (label_pos[..., None] == jnp.arange(span)).astype(LOW)
    student_rows = label_rows(pick, student_out)
    student_rows, tokens_teacher, packed_teacher = lax.optimization_barrier(
        (student_rows, tokens_teacher, packed_teacher)
    )
    teacher, _ = unpack_layer(packed_teacher, span, slots)
    student_rows = lax.all_gather(student_rows, "fsdp", axis=0, tiled=True)
    teacher_start = embed_forward(tokens_teacher.astype(jnp.float32), teacher, segments)[0]
    teacher_out = layer_forward(teacher_start, teacher, seq_len)[0]
    teacher_rows = label_rows(pick, teacher_out)
    teacher_rows = lax.all_gather(teacher_rows, "fsdp", axis=0, tiled=True)
    valid_group = label_valid(lengths_all, labels, span).reshape(-1)
    d_out, table_grad, label_loss = label_head(
        student_rows,
        teacher_rows,
        pick,
        tables,
        targets_all,
        valid_group,
        own,
        share,
        padded,
        groups,
        label_count,
    )
    cls_student = student_out[:, 0]
    unit_student, scale_student = unit_of(cls_student)
    unit_teacher = unit_of(teacher_out[:, 0])[0]
    weight_pkd = (PKD_WEIGHT * (seq_len > 0).astype(jnp.float32) / count_seq)[:, None]
    gap = unit_student - unit_teacher
    d_unit = 2.0 * weight_pkd * gap
    d_cls = scale_student * d_unit - cls_student * scale_student**3 * jnp.sum(
        cls_student * d_unit, axis=-1, keepdims=True
    )
    first_row = (jnp.arange(span) == 0).astype(jnp.float32)[None, :, None]
    d_out = d_out + first_row * d_cls[:, None, :]
    loss_part = label_loss + jnp.sum(weight_pkd * gap * gap)

    wide, factors, rows_grad, d_start = layer_backward(d_out, weights, kept, seq_len, devices)
    d_embed, gain_embed, shift_embed = layer_norm_back(
        d_start, normed_start, inverse_start, weights[4][12]
    )
    zero_segment = (segments == 0).astype(jnp.float32)[..., None]
    small_grad = jnp.concatenate(
        [
            rows_grad,
            gain_embed[None],
            shift_embed[None],
            jnp.sum(d_embed * zero_segment, axis=(0, 1))[None],
            jnp.sum(d_embed * (1.0 - zero_segment), axis=(0, 1))[None],
        ]
    )
    position_grad = jnp.sum(d_embed, axis=0)
    d_embed_low, factors = lax.optimization_barrier((d_embed.astype(LOW), factors))
    embed_grads = lax.all_gather(d_embed_low, "fsdp", axis=0, tiled=True)
    value_low, d_joined, context, d_attn = factors
    g_qkv = product_of("bsd,bsf->df", value_low, d_joined)
    g_out = product_of("bsc,bsd->cd", context, d_attn)
    narrow = pack_narrow(g_qkv, g_out, small_grad, position_grad)
    narrow, wide = lax.optimization_barrier((narrow, wide))
    narrow = lax.psum_scatter(narrow, BOTH, scatter_dimension=0, tiled=True)
    chosen = (safe_flat[:, None] == jnp.arange(vocab_rows)[None, :]).astype(LOW)
    table_grad = table_grad + product_of("tv,td->vd", chosen, embed_grads.reshape(-1, width))
    table_low, wide, narrow = lax.optimization_barrier((table_grad.astype(LOW), wide, narrow))
    table_shard = fold_dp(table_low, dp, 1, 3)[:share]
    grads = (table_shard,) + unpack_grads(wide, narrow, width, span, slots)
    squares = jnp.zeros((), jnp.float32)
    for grad in grads:
        squares = squares + jnp.sum(grad * grad)
    column = jnp.arange(128)[None, :]
    sums = jnp.where(column == 0, squares, jnp.where(column == 1, loss_part, 0.0))
    sums = total_all(jnp.broadcast_to(sums, (8, 128)), dp, groups, 4)
    total_sq, loss_value = sums[0, 0], sums[0, 1]
    grad_norm = jnp.sqrt(total_sq)
    factor = CLIP / jnp.maximum(grad_norm, CLIP)
    rate = RATE_SCALE * math.sqrt(NPARAM)
    params = (table, w_qkv, w_out, w_up, w_down, small, position)
    moms = (mom_table, mom_qkv, mom_out, mom_up, mom_down, mom_small, mom_position)
    avgs = (avg_table, avg_qkv, avg_out, avg_up, avg_down, avg_small, avg_position)
    news, moments, averages = ([], [], [])
    for weight, grad, momentum, average in zip(params, grads, moms, avgs):
        clipped = grad * factor
        moment = MOMENTUM * momentum + clipped
        fresh = weight - rate * (clipped + MOMENTUM * moment)
        news.append(fresh)
        moments.append(moment)
        averages.append(AVERAGE * average + (1.0 - AVERAGE) * fresh)
    return tuple(news) + tuple(moments) + tuple(averages) + (grad_norm, loss_value)


def solution(mesh):
    placed = (
        P(("dp", "fsdp"), None),
        P(("dp", "fsdp"), None),
        P(("dp", "fsdp")),
        P(("dp", "fsdp"), None),
        P(("dp", "fsdp"), None),
        P(("dp", "fsdp"), None),
        P(("dp", "fsdp"), None),
        P(("dp", "fsdp"), None),
        P(("dp", "fsdp"), None),
        P(("dp", "fsdp"), None),
        P(None, ("dp", "fsdp")),
        P(None, ("dp", "fsdp")),
        P(("dp", "fsdp"), None),
        P(("dp", "fsdp"), None),
        P(("dp", "fsdp"), None),
        P(("dp", "fsdp"), None),
        P(("dp", "fsdp"), None),
        P(None, ("dp", "fsdp")),
        P(None, ("dp", "fsdp")),
        P(("dp", "fsdp"), None),
        P(("dp", "fsdp"), None),
        P(("dp", "fsdp"), None),
        P(("dp", "fsdp"), None),
        P(("dp", "fsdp"), None),
        P(None, ("dp", "fsdp")),
        P(None, ("dp", "fsdp")),
        P(("dp", "fsdp"), None),
        P(("dp", "fsdp"), None),
        P(("dp", "fsdp"), None),
        P(("dp", "fsdp"), None),
        P(("dp", "fsdp"), None),
        P(None, ("dp", "fsdp")),
        P(None, ("dp", "fsdp")),
    )
    return jax.shard_map(
        on_device,
        mesh=mesh,
        in_specs=placed,
        out_specs=(
            P(("dp", "fsdp"), None),
            P(("dp", "fsdp"), None),
            P(("dp", "fsdp"), None),
            P(("dp", "fsdp"), None),
            P(("dp", "fsdp"), None),
            P(None, ("dp", "fsdp")),
            P(None, ("dp", "fsdp")),
            P(("dp", "fsdp"), None),
            P(("dp", "fsdp"), None),
            P(("dp", "fsdp"), None),
            P(("dp", "fsdp"), None),
            P(("dp", "fsdp"), None),
            P(None, ("dp", "fsdp")),
            P(None, ("dp", "fsdp")),
            P(("dp", "fsdp"), None),
            P(("dp", "fsdp"), None),
            P(("dp", "fsdp"), None),
            P(("dp", "fsdp"), None),
            P(("dp", "fsdp"), None),
            P(None, ("dp", "fsdp")),
            P(None, ("dp", "fsdp")),
            P(),
            P(),
        ),
        check_vma=False,
    )
```

```python
import functools
import math

import jax
import jax.numpy as jnp
from jax import lax
from jax.experimental import pallas as pl
from jax.experimental.pallas import tpu as pltpu
from jax.sharding import PartitionSpec as P

HD = 64
NPARAM = 30978048


SOFTMAX_HEAT = 2.0
SOFT_FRACTION = 0.5
PKD_WEIGHT = 10.0
MOMENTUM = 0.9
AVERAGE = 0.75
CLIP = 0.002
RATE_SCALE = 20.0
EPSILON = 1e-12
NEGATIVE = -1e30
BOTH = ("dp", "fsdp")
LOW = jnp.bfloat16
MIB = 1 << 20
CHUNK = 512


def push(src, dst, send, recv, where):
    copy = pltpu.make_async_remote_copy(
        src_ref=src,
        dst_ref=dst,
        send_sem=send,
        recv_sem=recv,
        device_id=where,
        device_id_type=pl.DeviceIdType.MESH,
    )
    copy.start()
    return copy


def greet(peers):
    barrier = pltpu.get_barrier_semaphore()
    for peer in peers:
        pl.semaphore_signal(barrier, inc=1, device_id=peer, device_id_type=pl.DeviceIdType.MESH)
    pl.semaphore_wait(barrier, len(peers))


def flipped(index, bit):
    return index + bit - 2 * bit * (lax.div(index, bit) % 2)


def spread_body(dp, count, *refs):
    blocks, outs = refs[:count], refs[count : 2 * count]
    local, send, recv = refs[2 * count :]
    me = lax.axis_index("dp")
    own = [pltpu.make_async_copy(blocks[k], outs[k].at[me], local.at[k]) for k in range(count)]
    for copy in own:
        copy.start()
    if dp == 4:
        near = [flipped(me, 1), flipped(me, 2)]
        greet([{"dp": near[0]}, {"dp": near[1]}])
        first = []
        for k in range(count):
            for step in range(2):
                for link in range(2):
                    half = step if link == 0 else 1 - step
                    first.append(
                        push(
                            blocks[k].at[half],
                            outs[k].at[me, half],
                            send.at[k, link, half],
                            recv.at[k, link, half],
                            {"dp": near[link]},
                        )
                    )
        for k in range(count):
            for link in range(2):
                first[k * 4 + link].wait_recv()
                origin = near[link]
                other = 1 - link
                first.append(
                    push(
                        outs[k].at[origin, link],
                        outs[k].at[origin, link],
                        send.at[k, 2, other],
                        recv.at[k, 2, other],
                        {"dp": near[other]},
                    )
                )
        for place, copy in enumerate(first):
            if place >= 4 * count or place % 4 >= 2:
                copy.wait_recv()
        for copy in first:
            copy.wait_send()
    else:
        peers = [lax.rem(me + hop, dp) for hop in range(1, dp)]
        greet([{"dp": peer} for peer in peers])
        sent = []
        for k in range(count):
            for hop, peer in enumerate(peers):
                sent.append(
                    push(
                        blocks[k],
                        outs[k].at[me],
                        send.at[k, hop, 0],
                        recv.at[k, hop, 0],
                        {"dp": peer},
                    )
                )
        for copy in sent:
            copy.wait()
    for copy in own:
        copy.wait()


def spread_dp(blocks, dp, identity):
    count = len(blocks)
    rows, width = blocks[0].shape
    cut = [block.reshape(2, rows // 2, width) for block in blocks]
    outs = pl.pallas_call(
        functools.partial(spread_body, dp, count),
        out_shape=[jax.ShapeDtypeStruct((dp, 2, rows // 2, width), LOW)] * count,
        in_specs=[pl.BlockSpec(memory_space=pl.ANY)] * count,
        out_specs=[pl.BlockSpec(memory_space=pl.ANY)] * count,
        scratch_shapes=[
            pltpu.SemaphoreType.DMA((count,)),
            pltpu.SemaphoreType.DMA((count, max(3, dp - 1), 2)),
            pltpu.SemaphoreType.DMA((count, max(3, dp - 1), 2)),
        ],
        compiler_params=pltpu.CompilerParams(collective_id=identity, has_side_effects=True),
        name="spread_tables",
    )(*cut)
    return [out.reshape(dp * rows, width) for out in outs]


def ways_of(me, dp):
    if dp == 4:
        return [flipped(me, 1), flipped(me, 2)]
    return [lax.rem(me + hop, dp) for hop in range(1, dp)]


def sources_of(me, dp):
    if dp == 4:
        return [flipped(me, 1), flipped(me, 2)]
    return [lax.rem(me + dp - hop, dp) for hop in range(1, dp)]


def gather_body(dp, n, count, *refs):
    blocks, outs = refs[:count], refs[count : 2 * count]
    local, z_send, z_recv, way_send, way_recv, far_send, far_recv, core_send, core_recv = refs[
        2 * count :
    ]
    me = lax.axis_index("fsdp")
    row = lax.axis_index("dp")
    p = lax.div(me, 2)
    c = lax.rem(me, 2)
    partner = me + 1 - 2 * c
    ways = ways_of(row, dp)
    sources = sources_of(row, dp)
    barrier = pltpu.get_barrier_semaphore()

    def hello(where):
        pl.semaphore_signal(barrier, inc=1, device_id=where, device_id_type=pl.DeviceIdType.MESH)

    hello({"fsdp": partner})
    for way in ways:
        hello({"dp": way})

    @pl.when(p > 0)
    def _():
        hello({"fsdp": me - 2})

    @pl.when(p < n - 1)
    def _():
        hello({"fsdp": me + 2})

    @pl.when((p > 0) & (p < n - 1))
    def _():
        pl.semaphore_wait(barrier, 3 + len(ways))

    @pl.when((p == 0) | (p == n - 1))
    def _():
        pl.semaphore_wait(barrier, 2 + len(ways))

    def remote(src, dst, send, recv, where):
        return pltpu.make_async_remote_copy(
            src_ref=src,
            dst_ref=dst,
            send_sem=send,
            recv_sem=recv,
            device_id=where,
            device_id_type=pl.DeviceIdType.MESH,
        )

    def line(m, q, side):
        shard = outs[m].at[row, 2 * q + c]
        where = {"fsdp": me + 2 - 4 * side}
        return remote(shard, shard, z_send.at[m, side, q], z_recv.at[m, q], where)

    def way_copy(m, w, half, q):
        shard = outs[m].at[row, 2 * q + c, half]
        return remote(
            shard, shard, way_send.at[m, w, half, q], way_recv.at[m, w, half, q], {"dp": ways[w]}
        )

    def far_copy(m, w, q):
        shard = outs[m].at[sources[w], 2 * q + c, w]
        return remote(
            shard, shard, far_send.at[m, w, q], far_recv.at[m, w, q], {"dp": ways[1 - w]}
        )

    def core_copy(m, j, q, half):
        shard = outs[m].at[j, 2 * q + c, half]
        return remote(
            shard,
            shard,
            core_send.at[m, j, q, half],
            core_recv.at[m, j, q, half],
            {"fsdp": partner},
        )

    def onward(m, q):
        for half in range(2):
            for w in range(len(ways)):
                way_copy(m, w, half if w == 0 else 1 - half, q).start()
        for half in range(2):
            core_copy(m, row, q, half).start()

    def landed(m, q):
        for half in range(2):
            for w in range(len(ways)):
                part = half if w == 0 else 1 - half
                way_copy(m, w, part, q).wait_recv()
                if dp == 4 and part == w:
                    far_copy(m, w, q).start()
                core_copy(m, sources[w], q, part).start()

    def far_landed(m, q):
        if dp == 4:
            for w in range(2):
                far_copy(m, w, q).wait_recv()
                core_copy(m, dp - 1 - row, q, w).start()

    def each(distance, act):
        if distance == 0:
            act(p)
            return

        @pl.when(p >= distance)
        def _():
            act(p - distance)

        @pl.when(p + distance < n)
        def _():
            act(p + distance)

    for m in range(count):
        copy = pltpu.make_async_copy(blocks[m], outs[m].at[row, me], local.at[m])
        copy.start()
        copy.wait()

        @pl.when(p < n - 1)
        def _():
            line(m, p, 0).start()

        @pl.when(p > 0)
        def _():
            line(m, p, 1).start()

        onward(m, p)
    for distance in range(1, n + 2):
        for m in range(count):
            if distance < n:

                @pl.when(p >= distance)
                def _():
                    line(m, p - distance, 0).wait_recv()

                    @pl.when(p < n - 1)
                    def _():
                        line(m, p - distance, 0).start()

                    onward(m, p - distance)

                @pl.when(p + distance < n)
                def _():
                    line(m, p + distance, 1).wait_recv()

                    @pl.when(p > 0)
                    def _():
                        line(m, p + distance, 1).start()

                    onward(m, p + distance)

            if distance <= n:
                each(distance - 1, functools.partial(landed, m))
            if distance >= 2:
                each(distance - 2, functools.partial(far_landed, m))

    def settle(q, carry):
        for m in range(count):

            @pl.when((q <= p) & (p < n - 1))
            def _():
                line(m, q, 0).wait_send()

            @pl.when((q >= p) & (p > 0))
            def _():
                line(m, q, 1).wait_send()

            for half in range(2):
                for w in range(len(ways)):
                    way_copy(m, w, half, q).wait_send()
                if dp == 4:
                    far_copy(m, half, q).wait_send()
                for j in range(dp):
                    core_copy(m, j, q, half).wait()
        return carry

    lax.fori_loop(0, n, settle, 0)


def gather_weights(blocks, dp, groups, identity):
    count = len(blocks)
    rows, width = blocks[0].shape
    n = groups // 2
    cut = [block.reshape(2, rows // 2, width) for block in blocks]
    ways = 2 if dp == 4 else dp - 1
    dma = pltpu.SemaphoreType.DMA
    outs = pl.pallas_call(
        functools.partial(gather_body, dp, n, count),
        out_shape=[jax.ShapeDtypeStruct((dp, groups, 2, rows // 2, width), LOW)] * count,
        in_specs=[pl.BlockSpec(memory_space=pl.ANY)] * count,
        out_specs=[pl.BlockSpec(memory_space=pl.ANY)] * count,
        scratch_shapes=[
            dma((count,)),
            dma((count, 2, n)),
            dma((count, n)),
            dma((count, ways, 2, n)),
            dma((count, ways, 2, n)),
            dma((count, 2, n)),
            dma((count, 2, n)),
            dma((count, dp, n, 2)),
            dma((count, dp, n, 2)),
        ],
        compiler_params=pltpu.CompilerParams(collective_id=identity, has_side_effects=True),
        name="gather_weights",
    )(*cut)
    return [out.reshape(dp * groups, rows, width) for out in outs]


def dot_over(left, right, left_dim, right_dim):
    return lax.dot_general(
        left, right, (((left_dim,), (right_dim,)), ((), ())), preferred_element_type=jnp.float32
    )


def added(*values):
    total = values[0].astype(jnp.float32)
    for value in values[1:]:
        total = total + value.astype(jnp.float32)
    return total


def reduce_body(dp, n, g, out, core, far, near, last, right, left, core_sem, far_sem, near_sem,
                last_sem, line_sem):
    me = lax.axis_index("fsdp")
    row = lax.axis_index("dp")
    p = lax.div(me, 2)
    c = lax.rem(me, 2)
    partner = me + 1 - 2 * c
    ways = ways_of(row, dp)
    opposite = dp - 1 - row
    barrier = pltpu.get_barrier_semaphore()
    order = []
    for k in range((n + 1) // 2):
        order += [n - 1 - k] + ([k] if k != n - 1 - k else [])

    def hello(where):
        pl.semaphore_signal(barrier, inc=1, device_id=where, device_id_type=pl.DeviceIdType.MESH)

    hello({"fsdp": partner})
    for way in ways:
        hello({"dp": way})

    @pl.when(p > 0)
    def _():
        hello({"fsdp": me - 2})

    @pl.when(p < n - 1)
    def _():
        hello({"fsdp": me + 2})

    @pl.when((p > 0) & (p < n - 1))
    def _():
        pl.semaphore_wait(barrier, 3 + len(ways))

    @pl.when((p == 0) | (p == n - 1))
    def _():
        pl.semaphore_wait(barrier, 2 + len(ways))

    def remote(src, dst, sems, index, where):
        return pltpu.make_async_remote_copy(
            src_ref=src,
            dst_ref=dst,
            send_sem=sems.at[(0,) + index],
            recv_sem=sems.at[(1,) + index],
            device_id=where,
            device_id_type=pl.DeviceIdType.MESH,
        )

    def core_copy(j, q, half):
        return remote(
            g.at[j, 2 * q + 1 - c, half],
            core.at[j, q, half],
            core_sem,
            (j, q, half),
            {"fsdp": partner},
        )

    def far_copy(q, w):
        return remote(
            core.at[opposite, q, w], far.at[q, w], far_sem, (q, w), {"dp": ways[w]}
        )

    def near_copy(q, w):
        return remote(
            core.at[ways[w], q, w], near.at[q, w], near_sem, (q, w, 0), {"dp": ways[w]}
        )

    def last_copy(q, w):
        return remote(
            far.at[q, w], last.at[q, w], last_sem, (q, w), {"dp": ways[1 - w]}
        )

    def direct_copy(hop, q, half):
        return remote(
            core.at[ways[hop], q, half],
            near.at[hop, q, half],
            near_sem,
            (q, half, hop),
            {"dp": ways[hop]},
        )

    def line_copy(buffer, q, side):
        return remote(
            buffer.at[q], buffer.at[q], line_sem, (q, side), {"fsdp": me + 2 - 4 * side}
        )

    for q in order:
        for j in [opposite, *ways, row] if dp == 4 else range(dp):
            for half in range(2):
                core_copy(j, q, half).start()

    def pair(j, q, half):
        core_copy(j, q, half).wait_recv()
        core[j, q, half] = added(core[j, q, half], g[j, 2 * q + c, half]).astype(LOW)

    for q in order:
        if dp == 4:
            for w in range(2):
                pair(opposite, q, w)
                far_copy(q, w).start()
            for w in range(2):
                pair(ways[w], q, w)
                near_copy(q, w).start()
            for w in range(2):
                pair(ways[w], q, 1 - w)
                pair(row, q, w)
        else:
            for half in range(2):
                for j in range(dp):
                    pair(j, q, half)
                for hop in range(dp - 1):
                    direct_copy(hop, q, half).start()
    if dp == 4:
        for q in order:
            for w in range(2):
                far_copy(q, w).wait_recv()
                far[q, w] = added(far[q, w], core[ways[1 - w], q, w]).astype(LOW)
                last_copy(q, w).start()

    def total(q, half):
        if dp == 4:
            near_copy(q, half).wait_recv()
            last_copy(q, half).wait_recv()
            return added(core[row, q, half], near[q, half], last[q, half])
        parts = [core[row, q, half]]
        for hop in range(dp - 1):
            direct_copy(hop, q, half).wait_recv()
            parts.append(near[hop, q, half])
        return added(*parts)

    for q in order:
        sums = [total(q, half) for half in range(2)]

        def store(buffer, side, first):
            for half in range(2):
                if first:
                    buffer[q, half] = sums[half].astype(LOW)
                else:
                    buffer[q, half] = added(sums[half], buffer[q, half]).astype(LOW)
            line_copy(buffer, q, side).start()

        if q > 0:

            @pl.when((p > 0) & (p < q))
            def _():
                line_copy(right, q, 0).wait_recv()
                store(right, 0, False)

            @pl.when((p == 0) & (p < q))
            def _():
                store(right, 0, True)

        if q < n - 1:

            @pl.when((p < n - 1) & (p > q))
            def _():
                line_copy(left, q, 1).wait_recv()
                store(left, 1, False)

            @pl.when((p == n - 1) & (p > q))
            def _():
                store(left, 1, True)

        @pl.when(p == q)
        def _():
            for half in range(2):
                out[half] = sums[half]

    @pl.when(p > 0)
    def _():
        line_copy(right, p, 0).wait_recv()
        out[...] = added(out[...], right[p])

    @pl.when(p < n - 1)
    def _():
        line_copy(left, p, 1).wait_recv()
        out[...] = added(out[...], left[p])

    for q in order:
        for half in range(2):
            for j in range(dp):
                core_copy(j, q, half).wait_send()
            if dp == 4:
                far_copy(q, half).wait_send()
                near_copy(q, half).wait_send()
                last_copy(q, half).wait_send()
            else:
                for hop in range(dp - 1):
                    direct_copy(hop, q, half).wait_send()

        @pl.when(p < q)
        def _():
            line_copy(right, q, 0).wait_send()

        @pl.when(p > q)
        def _():
            line_copy(left, q, 1).wait_send()


def reduce_weights(g, dp, groups, identity):
    devices, rows, width = g.shape
    n = groups // 2
    half = rows // 2
    g = g.reshape(dp, groups, 2, half, width)
    dma = pltpu.SemaphoreType.DMA
    block = pltpu.VMEM((n, 2, half, width), LOW)
    near = block if dp == 4 else pltpu.VMEM((dp - 1, n, 2, half, width), LOW)
    out = pl.pallas_call(
        functools.partial(reduce_body, dp, n),
        out_shape=jax.ShapeDtypeStruct((2, half, width), jnp.float32),
        in_specs=[pl.BlockSpec(memory_space=pltpu.VMEM)],
        out_specs=pl.BlockSpec(memory_space=pltpu.VMEM),
        scratch_shapes=[
            pltpu.VMEM((dp, n, 2, half, width), LOW),
            block,
            near,
            block,
            block,
            block,
            dma((2, dp, n, 2)),
            dma((2, n, 2)),
            dma((2, n, 2, max(1, dp - 1))),
            dma((2, n, 2)),
            dma((2, n, 2)),
        ],
        compiler_params=pltpu.CompilerParams(
            collective_id=identity, has_side_effects=True, vmem_limit_bytes=56 * MIB
        ),
        name="reduce_weights",
    )(g)
    return out.reshape(rows, width)


def fold_body(dp, step, share, ids, rows, base, out, squares, g, near_buffer, far_buffer, last_buffer, sems):
    me = lax.axis_index("dp")
    half_rows = base.shape[2]
    tokens = rows.shape[0]

    def fill(dest, half):
        first = (dest * 2 + half) * half_rows
        vocab = lax.broadcasted_iota(jnp.int32, (half_rows, step), 0) + first

        def turn(k, total):
            chosen = (vocab == ids[k]).astype(jnp.float32).astype(LOW)
            start = pl.multiple_of(k * step, step)
            return total + dot_over(chosen, rows[pl.ds(start, step), :], 1, 0)

        return lax.fori_loop(0, tokens // step, turn, base[dest, half])

    if dp == 4:
        near = [flipped(me, 1), flipped(me, 2)]
        far = dp - 1 - me
        greet([{"dp": near[0]}, {"dp": near[1]}])

        def send(kind, w, src, dst, way):
            return push(src, dst, sems.at[0, kind, w], sems.at[1, kind, w], {"dp": near[way]})

        first, second, third = [], [], []
        for w in range(2):
            g[far, w] = fill(far, w).astype(LOW)
            first.append(send(0, w, g.at[far, w], far_buffer.at[w], w))
        for w in range(2):
            g[near[w], w] = fill(near[w], w).astype(LOW)
            second.append(send(1, w, g.at[near[w], w], near_buffer.at[w], w))
        for w in range(2):
            part = fill(near[1 - w], w)
            first[w].wait_recv()
            far_buffer[w] = (part + far_buffer[w].astype(jnp.float32)).astype(LOW)
            third.append(send(2, w, far_buffer.at[w], last_buffer.at[w], 1 - w))
        for w in range(2):
            out[w] = fill(me, w)
        for w in range(2):
            second[w].wait_recv()
            third[w].wait_recv()
            out[w] = (
                out[w]
                + near_buffer[w].astype(jnp.float32)
                + last_buffer[w].astype(jnp.float32)
            )
        for copy in first + second + third:
            copy.wait_send()
    else:
        peers = [lax.rem(me + hop, dp) for hop in range(1, dp)]
        greet([{"dp": peer} for peer in peers])
        sent = []
        for hop, peer in enumerate(peers):
            for half in range(2):
                g[peer, half] = fill(peer, half).astype(LOW)
            sent.append(
                push(
                    g.at[peer],
                    near_buffer.at[hop],
                    sems.at[0, hop, 0],
                    sems.at[1, hop, 0],
                    {"dp": peer},
                )
            )
        for half in range(2):
            out[half] = fill(me, half)
        for hop in range(dp - 1):
            sent[hop].wait()
            out[...] = out[...] + near_buffer[hop].astype(jnp.float32)
    total = jnp.zeros((1, out.shape[2]), jnp.float32)
    for half in range(2):
        index = lax.broadcasted_iota(jnp.int32, (half_rows, 1), 0) + half * half_rows
        value = jnp.where(index < share, out[half], 0.0)
        total = total + jnp.sum(value * value, axis=0, keepdims=True)
    squares[...] = total


def fold_dp(ids, rows, base, dp, share, step, identity):
    tokens, width = rows.shape
    padded = base.shape[0] // dp
    half = padded // 2
    block = pltpu.VMEM((2, half, width), LOW)
    first = block if dp == 4 else pltpu.VMEM((dp - 1, 2, half, width), LOW)
    vmem = pl.BlockSpec(memory_space=pltpu.VMEM)
    out, squares = pl.pallas_call(
        functools.partial(fold_body, dp, step, share),
        out_shape=[
            jax.ShapeDtypeStruct((2, half, width), jnp.float32),
            jax.ShapeDtypeStruct((1, width), jnp.float32),
        ],
        in_specs=[vmem, vmem, vmem],
        out_specs=[vmem, vmem],
        scratch_shapes=[
            pltpu.VMEM((dp, 2, half, width), LOW),
            first,
            block,
            block,
            pltpu.SemaphoreType.DMA((2, max(3, dp - 1), 2)),
        ],
        compiler_params=pltpu.CompilerParams(
            collective_id=identity, has_side_effects=True, vmem_limit_bytes=58 * MIB
        ),
        name="fold_table",
    )(ids.reshape(tokens // step, 1, step), rows, base.reshape(dp, 2, half, width))
    return out.reshape(padded, width), squares


def share_body(groups, x, out, send, recv):
    me = lax.axis_index("fsdp")
    peers = [lax.rem(me + hop, groups) for hop in range(1, groups)]
    greet([{"fsdp": peer} for peer in peers])
    sent = []
    for hop, peer in enumerate(peers):
        sent.append(push(x, out.at[me], send.at[hop], recv.at[hop], {"fsdp": peer}))
    out[me] = x[...]
    for copy in sent:
        copy.wait()


def share_small(x, groups, identity):
    return pl.pallas_call(
        functools.partial(share_body, groups),
        out_shape=jax.ShapeDtypeStruct((groups,) + x.shape, x.dtype),
        in_specs=[pl.BlockSpec(memory_space=pltpu.VMEM)],
        out_specs=pl.BlockSpec(memory_space=pltpu.VMEM),
        scratch_shapes=[pltpu.SemaphoreType.DMA((groups - 1,))] * 2,
        compiler_params=pltpu.CompilerParams(collective_id=identity, has_side_effects=True),
        name="share_small",
    )(x)


def total_body(dp, groups, x, out, fsdp_parts, dp_value, dp_parts, send, recv):
    me = lax.axis_index("fsdp")
    row = lax.axis_index("dp")
    peers = [lax.rem(me + hop, groups) for hop in range(1, groups)]
    rows = [lax.rem(row + hop, dp) for hop in range(1, dp)]
    greet([{"fsdp": peer} for peer in peers] + [{"dp": peer} for peer in rows])
    sent = []
    for hop, peer in enumerate(peers):
        sent.append(push(x, fsdp_parts.at[me], send.at[hop], recv.at[hop], {"fsdp": peer}))
    fsdp_parts[me] = x[...]
    for copy in sent:
        copy.wait()
    value = fsdp_parts[0]
    for k in range(1, groups):
        value = value + fsdp_parts[k]
    dp_value[...] = value
    dp_parts[row] = value
    sent = []
    for hop, peer in enumerate(rows):
        place = groups - 1 + hop
        sent.append(
            push(dp_value, dp_parts.at[row], send.at[place], recv.at[place], {"dp": peer})
        )
    for copy in sent:
        copy.wait()
    value = dp_parts[0]
    for k in range(1, dp):
        value = value + dp_parts[k]
    out[...] = value


def total_all(x, dp, groups, identity):
    count = dp + groups - 2
    tile = (8, 128)
    return pl.pallas_call(
        functools.partial(total_body, dp, groups),
        out_shape=jax.ShapeDtypeStruct(tile, jnp.float32),
        in_specs=[pl.BlockSpec(memory_space=pltpu.VMEM)],
        out_specs=pl.BlockSpec(memory_space=pltpu.VMEM),
        scratch_shapes=[
            pltpu.VMEM((groups,) + tile, jnp.float32),
            pltpu.VMEM(tile, jnp.float32),
            pltpu.VMEM((dp,) + tile, jnp.float32),
            pltpu.SemaphoreType.DMA((count,)),
            pltpu.SemaphoreType.DMA((count,)),
        ],
        compiler_params=pltpu.CompilerParams(collective_id=identity, has_side_effects=True),
        name="total",
    )(x)


def block_rows(ref_rows, share):
    block = pl.program_id(0)
    index = lax.broadcasted_iota(jnp.int32, (ref_rows, 1), 0)
    real = index + lax.rem(block, 2) * ref_rows < share
    return index + block * ref_rows, real


def student_logits_body(share, rows, table, target, logits, stats):
    index, real = block_rows(table.shape[0], share)
    value = jnp.where(real, dot_over(table[...], rows[...], 1, 1), NEGATIVE)
    logits[...] = value
    top = jnp.max(value, axis=0, keepdims=True)
    hit = jnp.sum(jnp.where(index == target[...], value, 0.0), axis=0, keepdims=True)

    @pl.when(pl.program_id(0) == 0)
    def _():
        half = jnp.exp((value - top) / SOFTMAX_HEAT)
        stats[0:1] = top
        stats[1:2] = jnp.sum(half * half, axis=0, keepdims=True)
        stats[2:3] = jnp.sum(half, axis=0, keepdims=True)
        stats[3:4] = hit

    @pl.when(pl.program_id(0) > 0)
    def _():
        before = stats[0:1]
        peak = jnp.maximum(before, top)
        fall = jnp.exp((before - peak) / SOFTMAX_HEAT)
        half = jnp.exp((value - peak) / SOFTMAX_HEAT)
        stats[0:1] = peak
        stats[1:2] = stats[1:2] * fall * fall + jnp.sum(half * half, axis=0, keepdims=True)
        stats[2:3] = stats[2:3] * fall + jnp.sum(half, axis=0, keepdims=True)
        stats[3:4] = stats[3:4] + hit


def teacher_logits_body(share, rows, table, student, logits, stats):
    _, real = block_rows(table.shape[0], share)
    value = jnp.where(real, dot_over(table[...], rows[...], 1, 1), NEGATIVE)
    logits[...] = value
    top = jnp.max(value, axis=0, keepdims=True)
    gap = (value - student[...]) / SOFTMAX_HEAT

    @pl.when(pl.program_id(0) == 0)
    def _():
        exponent = jnp.exp((value - top) / SOFTMAX_HEAT)
        stats[0:1] = top
        stats[1:2] = jnp.sum(exponent, axis=0, keepdims=True)
        stats[2:3] = jnp.sum(exponent * gap, axis=0, keepdims=True)
        stats[3:4] = jnp.zeros_like(top)

    @pl.when(pl.program_id(0) > 0)
    def _():
        before = stats[0:1]
        peak = jnp.maximum(before, top)
        fall = jnp.exp((before - peak) / SOFTMAX_HEAT)
        exponent = jnp.exp((value - peak) / SOFTMAX_HEAT)
        stats[0:1] = peak
        stats[1:2] = stats[1:2] * fall + jnp.sum(exponent, axis=0, keepdims=True)
        stats[2:3] = stats[2:3] * fall + jnp.sum(exponent * gap, axis=0, keepdims=True)


def logits_call(body, rows, table, other, block, name):
    count, width = rows.shape
    vocab = table.shape[0]
    wide = pl.BlockSpec((block, count), lambda v: (v, 0))
    whole = pl.BlockSpec(memory_space=pltpu.VMEM)
    return pl.pallas_call(
        body,
        grid=(vocab // block,),
        in_specs=[
            whole,
            pl.BlockSpec((block, width), lambda v: (v, 0)),
            wide if other.shape[0] == vocab else whole,
        ],
        out_specs=[wide, pl.BlockSpec((4, count), lambda v: (0, 0))],
        out_shape=[
            jax.ShapeDtypeStruct((vocab, count), jnp.float32),
            jax.ShapeDtypeStruct((4, count), jnp.float32),
        ],
        compiler_params=pltpu.CompilerParams(vmem_limit_bytes=40 * MIB),
        cost_estimate=pl.CostEstimate(
            flops=2 * vocab * count * width,
            bytes_accessed=4 * vocab * count + 2 * vocab * width,
            transcendentals=vocab * count,
        ),
        name=name,
    )(rows, table, other)


def logits_back_body(student, teacher, table, consts, target, d_logits, d_rows, total):
    index = lax.broadcasted_iota(jnp.int32, (table.shape[0], 1), 0)
    index = index + pl.program_id(0) * table.shape[0]
    value = student[...]
    hard = jnp.exp(value - consts[0:1]) - (index == target[...]).astype(jnp.float32)
    soft = jnp.exp(value / SOFTMAX_HEAT - consts[1:2]) - jnp.exp(
        teacher[...] / SOFTMAX_HEAT - consts[2:3]
    )
    mixed = consts[3:4] * (
        (1.0 - SOFT_FRACTION) * hard + SOFT_FRACTION * SOFTMAX_HEAT * soft
    )
    low = mixed.astype(LOW)
    d_logits[...] = low
    part = dot_over(low, table[...], 0, 0)

    @pl.when(pl.program_id(0) == 0)
    def _():
        total[...] = part

    @pl.when(pl.program_id(0) > 0)
    def _():
        total[...] += part

    @pl.when(pl.program_id(0) == pl.num_programs(0) - 1)
    def _():
        d_rows[...] = total[...].astype(LOW)


def logits_back(student, teacher, table, consts, target, block):
    vocab, count = student.shape
    width = table.shape[1]
    wide = pl.BlockSpec((block, count), lambda v: (v, 0))
    whole = pl.BlockSpec(memory_space=pltpu.VMEM)
    return pl.pallas_call(
        logits_back_body,
        grid=(vocab // block,),
        in_specs=[wide, wide, pl.BlockSpec((block, width), lambda v: (v, 0)), whole, whole],
        out_specs=[wide, pl.BlockSpec((count, width), lambda v: (0, 0))],
        out_shape=[
            jax.ShapeDtypeStruct((vocab, count), LOW),
            jax.ShapeDtypeStruct((count, width), LOW),
        ],
        scratch_shapes=[pltpu.VMEM((count, width), jnp.float32)],
        compiler_params=pltpu.CompilerParams(vmem_limit_bytes=48 * MIB),
        cost_estimate=pl.CostEstimate(
            flops=2 * vocab * count * width,
            bytes_accessed=10 * vocab * count + 2 * vocab * width,
            transcendentals=3 * vocab * count,
        ),
        name="logits_back",
    )(student, teacher, table, consts, target)


def attend_body(lengths, q_ref, k_ref, v_ref, out_ref):
    live = jnp.maximum(lengths[pl.program_id(0)], 1)
    span = q_ref.shape[1]
    k, v = k_ref[0], v_ref[0]
    keep = lax.broadcasted_iota(jnp.int32, (span, CHUNK), 0) < live
    low_lane = lax.broadcasted_iota(jnp.int32, (CHUNK, 2 * HD), 1) < HD
    for first in range(0, span, CHUNK):
        q = q_ref[0, first : first + CHUNK, :]
        parts = []
        for head in range(2):
            mine = low_lane if head == 0 else jnp.logical_not(low_lane)
            scores = dot_over(k, jnp.where(mine, q, jnp.zeros_like(q)), 1, 1)
            scores = jnp.where(keep, scores * 0.125, NEGATIVE)
            exponent = jnp.exp(scores - jnp.max(scores, axis=0, keepdims=True))
            scale = 1.0 / jnp.sum(exponent, axis=0, keepdims=True)
            parts.append(dot_over((exponent * scale).astype(LOW), v, 0, 0))
        out_ref[0, first : first + CHUNK, :] = jnp.where(low_lane, parts[0], parts[1]).astype(LOW)


def attend(joined, lengths):
    micro, span, wide = joined.shape
    width = wide // 3
    pairs = width // (2 * HD)

    def place(third):
        return pl.BlockSpec((1, span, 2 * HD), lambda b, h, _: (b, 0, third * pairs + h))

    return pl.pallas_call(
        attend_body,
        grid_spec=pltpu.PrefetchScalarGridSpec(
            num_scalar_prefetch=1,
            grid=(micro, pairs),
            in_specs=[place(0), place(1), place(2)],
            out_specs=pl.BlockSpec((1, span, 2 * HD), lambda b, h, _: (b, 0, h)),
        ),
        out_shape=jax.ShapeDtypeStruct((micro, span, width), LOW),
        cost_estimate=pl.CostEstimate(
            flops=4 * micro * span * span * width,
            bytes_accessed=8 * micro * span * width,
            transcendentals=micro * span * span * width // HD,
        ),
        name="attend",
    )(lengths, joined, joined, joined)


def attend_back_body(lengths, q_ref, k_ref, v_ref, d_ref, out_ref, g_keys, g_values):
    live = jnp.maximum(lengths[pl.program_id(0)], 1)
    span = q_ref.shape[1]
    k, v = k_ref[0], v_ref[0]
    keep = lax.broadcasted_iota(jnp.int32, (span, CHUNK), 0) < live
    low_lane = lax.broadcasted_iota(jnp.int32, (CHUNK, 2 * HD), 1) < HD
    low_wide = lax.broadcasted_iota(jnp.int32, (span, 2 * HD), 1) < HD
    for first in range(0, span, CHUNK):
        q = q_ref[0, first : first + CHUNK, :]
        d = d_ref[0, first : first + CHUNK, :]
        parts = []
        for head in range(2):
            mine = low_lane if head == 0 else jnp.logical_not(low_lane)
            scores = dot_over(k, jnp.where(mine, q, jnp.zeros_like(q)), 1, 1)
            scores = jnp.where(keep, scores * 0.125, NEGATIVE)
            exponent = jnp.exp(scores - jnp.max(scores, axis=0, keepdims=True))
            probs = exponent * (1.0 / jnp.sum(exponent, axis=0, keepdims=True))
            d_probs = dot_over(v, jnp.where(mine, d, jnp.zeros_like(d)), 1, 1)
            inner = jnp.sum(probs * d_probs, axis=0, keepdims=True)
            d_scores = (probs * (d_probs - inner)).astype(LOW)
            value_part = dot_over(probs.astype(LOW), d, 1, 0)
            key_part = dot_over(d_scores, q, 1, 0)
            if first == 0:
                g_values[head] = value_part
                g_keys[head] = key_part
            else:
                g_values[head] += value_part
                g_keys[head] += key_part
            parts.append(dot_over(d_scores, k, 0, 0))
        out_ref[0, 0, first : first + CHUNK, :] = (
            jnp.where(low_lane, parts[0], parts[1]) * 0.125
        ).astype(LOW)
    out_ref[1, 0] = (jnp.where(low_wide, g_keys[0], g_keys[1]) * 0.125).astype(LOW)
    out_ref[2, 0] = jnp.where(low_wide, g_values[0], g_values[1]).astype(LOW)


def attend_back(joined, d_context, lengths):
    micro, span, width = d_context.shape
    pairs = width // (2 * HD)

    def place(third):
        return pl.BlockSpec((1, span, 2 * HD), lambda b, h, _: (b, 0, third * pairs + h))

    return pl.pallas_call(
        attend_back_body,
        grid_spec=pltpu.PrefetchScalarGridSpec(
            num_scalar_prefetch=1,
            grid=(micro, pairs),
            in_specs=[place(0), place(1), place(2), place(0)],
            out_specs=pl.BlockSpec((3, 1, span, 2 * HD), lambda b, h, _: (0, b, 0, h)),
            scratch_shapes=[
                pltpu.VMEM((2, span, 2 * HD), jnp.float32),
                pltpu.VMEM((2, span, 2 * HD), jnp.float32),
            ],
        ),
        out_shape=jax.ShapeDtypeStruct((3, micro, span, width), LOW),
        cost_estimate=pl.CostEstimate(
            flops=10 * micro * span * span * width,
            bytes_accessed=14 * micro * span * width,
            transcendentals=micro * span * span * width // HD,
        ),
        name="attend_back",
    )(lengths, joined, joined, joined, d_context)


def product_of(form, left, right):
    return jnp.einsum(form, left, right, preferred_element_type=jnp.float32)


def owned(ids, share, padded, groups, own):
    block = ids // share
    inside = block % groups == own
    local = block // groups * padded + ids % share
    return (inside, jnp.where(inside, local, share))


def layer_norm_keep(value, gain, shift):
    mean = jnp.mean(value, axis=-1, keepdims=True)
    centred = value - mean
    inverse = lax.rsqrt(jnp.mean(centred * centred, axis=-1, keepdims=True) + EPSILON)
    normed = centred * inverse
    return (normed * gain + shift, normed, inverse)


def layer_norm_back(grad, normed, inverse, gain):
    axes = tuple(range(grad.ndim - 1))
    gain_grad = jnp.sum(grad * normed, axis=axes)
    shift_grad = jnp.sum(grad, axis=axes)
    scaled = grad * gain
    centred = scaled - jnp.mean(scaled, axis=-1, keepdims=True)
    return (
        inverse * (centred - normed * jnp.mean(scaled * normed, axis=-1, keepdims=True)),
        gain_grad,
        shift_grad,
    )


def gelu_parts(upward):
    normal_cdf = 0.5 * (1.0 + lax.erf(upward * 0.7071067811865476))
    density = jnp.exp(-0.5 * upward * upward) * 0.3989422804014327
    return (upward * normal_cdf, normal_cdf + upward * density)


def label_valid(lengths, labels, span):
    needed = (lengths * labels + span - 1) // span
    return (jnp.arange(labels)[None, :] < needed[:, None]).astype(jnp.float32)


def pack_layer(weights, extra):
    w_qkv, w_out, w_up, w_down, small, position = (w.astype(LOW) for w in weights)
    rows, width = w_out.shape
    pieces = [w_qkv[:, k * width : (k + 1) * width] for k in range(3)]
    pieces += [w_out]
    pieces += [w_up[:, k * width : (k + 1) * width] for k in range(w_up.shape[1] // width)]
    pieces += [w_down]
    rest = [position.T, small.T] + ([] if extra is None else [extra])
    rest = jnp.concatenate(rest, axis=1)
    pieces += [jnp.pad(rest, ((0, 0), (0, width - rest.shape[1])))]
    packed = jnp.concatenate(pieces, axis=0)
    return jnp.pad(packed, ((0, -packed.shape[0] % 32), (0, 0)))


def unpack_layer(packed, span, slots):
    devices, _, width = packed.shape
    rows = width // devices
    ff = 4 * width

    def part(first, count):
        return packed[:, first : first + count].reshape(devices * count, width)

    w_qkv = jnp.concatenate([part(k * rows, rows) for k in range(3)], axis=1)
    w_out = part(3 * rows, rows)
    w_up = jnp.concatenate([part((4 + k) * rows, rows) for k in range(4)], axis=1)
    w_down = part(8 * rows, ff // devices)
    rest = part(8 * rows + ff // devices, rows)
    position = rest[:, :span].T.astype(jnp.float32)
    small = rest[:, span : span + slots].T.astype(jnp.float32)
    return (w_qkv, w_out, w_up, w_down, small, position), rest[:, span + slots :]


def embed_forward(token_rows, weights, segment_ids):
    small, position = weights[4:]
    segment_rows = jnp.where(segment_ids[..., None] == 0, small[14], small[15])
    return layer_norm_keep(token_rows + position + segment_rows, small[12], small[13])


def layer_forward(value, weights, lengths):
    w_qkv, w_out, w_up, w_down, small = weights[:5]
    micro, span, width = value.shape
    value_low = value.astype(LOW)
    bias = jnp.concatenate([small[0], jnp.zeros_like(small[0]), small[1]])
    joined = (product_of("bsd,df->bsf", value_low, w_qkv) + bias).astype(LOW)
    context = attend(joined, lengths)
    attn = product_of("bsc,cd->bsd", context, w_out) + small[2]
    first, normed_first, inverse_first = layer_norm_keep(value + attn, small[8], small[9])
    first_low = first.astype(LOW)
    upward = product_of("bsd,df->bsf", first_low, w_up) + small[3:7].reshape(-1)
    act, slope = gelu_parts(upward)
    act_low = act.astype(LOW)
    down = product_of("bsf,fd->bsd", act_low, w_down) + small[7]
    out, normed_second, inverse_second = layer_norm_keep(first + down, small[10], small[11])
    return (
        out,
        (
            value_low,
            joined,
            context,
            normed_first,
            inverse_first,
            first_low,
            slope,
            act_low,
            normed_second,
            inverse_second,
        ),
    )


def layer_backward(grad, weights, kept, lengths):
    w_qkv, w_out, w_up, w_down, small = weights[:5]
    (
        value_low,
        joined,
        context,
        normed_first,
        inverse_first,
        first_low,
        slope,
        act_low,
        normed_second,
        inverse_second,
    ) = kept
    micro, span, width = value_low.shape
    d_second, gain_second, shift_second = layer_norm_back(
        grad, normed_second, inverse_second, small[10]
    )
    d_down = d_second.astype(LOW)
    d_up = (product_of("bsd,fd->bsf", d_down, w_down) * slope).astype(LOW)
    d_first = d_second + product_of("bsf,df->bsd", d_up, w_up)
    d_sum, gain_first, shift_first = layer_norm_back(d_first, normed_first, inverse_first, small[8])
    d_attn = d_sum.astype(LOW)
    d_context = product_of("bsd,cd->bsc", d_attn, w_out).astype(LOW)
    d_joined = jnp.concatenate(list(attend_back(joined, d_context, lengths)), axis=-1)
    d_value = d_sum + product_of("bsf,df->bsd", d_joined, w_qkv)

    def column_sum(value):
        return jnp.sum(value.astype(jnp.float32), axis=(0, 1))

    joined_sum = column_sum(d_joined)
    rows_grad = jnp.concatenate(
        [
            joined_sum[:width][None],
            joined_sum[2 * width :][None],
            column_sum(d_attn)[None],
            column_sum(d_up).reshape(-1, width),
            column_sum(d_down)[None],
            gain_first[None],
            shift_first[None],
            gain_second[None],
            shift_second[None],
        ]
    )
    factors = (
        (value_low, d_joined),
        (context, d_attn),
        (first_low, d_up),
        (act_low, d_down),
    )
    return factors, rows_grad, d_value


def label_rows(pick, out):
    micro, labels, _ = pick.shape
    rows = product_of("bps,bsd->bpd", pick, out.astype(LOW)).astype(LOW)
    return rows.reshape(micro * labels, out.shape[-1])


def label_head(
    all_student, all_teacher, pick, tables, targets, valid_mask, own, share, padded, groups, count
):
    table_student, table_teacher = tables
    vocab_rows = table_student.shape[0]
    micro, labels, span = pick.shape
    width = all_student.shape[1]
    mine = micro * labels
    inside, local_target = owned(targets, share, padded, groups, own)
    target = jnp.where(inside, local_target, -1)[None, :]
    block = padded // 2
    student, student_stats = logits_call(
        functools.partial(student_logits_body, share),
        all_student,
        table_student,
        target,
        block,
        "student_logits",
    )
    teacher, teacher_stats = logits_call(
        functools.partial(teacher_logits_body, share),
        all_teacher,
        table_teacher,
        student,
        block,
        "teacher_logits",
    )
    stats = share_small(jnp.concatenate([student_stats, teacher_stats]), groups, 8)
    peak_student = jnp.max(stats[:, 0], axis=0)
    peak_teacher = jnp.max(stats[:, 4], axis=0)
    fall_student = jnp.exp((stats[:, 0] - peak_student) / SOFTMAX_HEAT)
    fall_teacher = jnp.exp((stats[:, 4] - peak_teacher) / SOFTMAX_HEAT)
    sum_plain = jnp.sum(stats[:, 1] * fall_student * fall_student, axis=0)
    sum_soft = jnp.sum(stats[:, 2] * fall_student, axis=0)
    sum_teacher = jnp.sum(stats[:, 5] * fall_teacher, axis=0)
    cross = jnp.sum(stats[:, 6] * fall_teacher, axis=0)
    target_logit = jnp.sum(stats[:, 3], axis=0)
    lse_plain = peak_student + jnp.log(sum_plain)
    lse_soft = peak_student / SOFTMAX_HEAT + jnp.log(sum_soft)
    lse_teacher = peak_teacher / SOFTMAX_HEAT + jnp.log(sum_teacher)
    cross_entropy = lse_plain - target_logit
    divergence_loss = cross / sum_teacher - lse_teacher + lse_soft
    share_lab = valid_mask / count
    consts = jnp.stack([lse_plain, lse_soft, lse_teacher, share_lab])
    d_logits, d_rows = logits_back(student, teacher, table_student, consts, target, block)
    d_rows = lax.psum_scatter(d_rows, "fsdp", scatter_dimension=0, tiled=True)
    table_term = product_of("vp,pd->vd", d_logits, all_student)
    d_rows, table_term = lax.optimization_barrier((d_rows, table_term))
    terms = share_lab * (
        (1.0 - SOFT_FRACTION) * cross_entropy
        + SOFT_FRACTION * SOFTMAX_HEAT * SOFTMAX_HEAT * divergence_loss
    )
    local = lax.dynamic_slice_in_dim(terms, own * mine, mine)
    d_out = product_of("bps,bpd->bsd", pick, d_rows.reshape(micro, -1, width))
    return (d_out, table_term, jnp.sum(local))


def pack_grads(g_qkv, g_out, g_up, g_down, small_grad, position_grad, devices):
    width = g_out.shape[0]
    rows = width // devices

    def shards(grad):
        return grad.astype(LOW).reshape(devices, -1, width)

    pieces = [shards(g_qkv[:, k * width : (k + 1) * width]) for k in range(3)]
    pieces += [shards(g_out)]
    pieces += [shards(g_up[:, k * width : (k + 1) * width]) for k in range(4)]
    pieces += [shards(g_down)]
    rest = jnp.concatenate([position_grad, small_grad], axis=0)
    rest = jnp.pad(rest, ((0, width - rest.shape[0]), (0, 0))).T
    pieces += [shards(rest)]
    filled = 8 * rows + g_down.shape[0] // devices + rows
    pad = -filled % 32
    if pad:
        pieces += [jnp.zeros((devices, pad, width), LOW)]
    return jnp.concatenate(pieces, axis=1)


def unpack_grads(packed, rows, span, slots):
    width = packed.shape[1]
    down = packed.shape[1] * 4 * rows // width
    low = 8 * rows

    def part(first):
        return packed[first * rows : (first + 1) * rows]

    rest = packed[low + down : low + down + rows]
    return (
        jnp.concatenate([part(k) for k in range(3)], axis=1),
        part(3),
        jnp.concatenate([part(4 + k) for k in range(4)], axis=1),
        packed[low : low + down],
        rest[:, span : span + slots].T,
        rest[:, :span].T,
    )


def unit_of(cls):
    scale = lax.rsqrt(jnp.sum(cls * cls, axis=-1, keepdims=True) + 1e-06)
    return cls * scale, scale


def on_device(
    tok_ids,
    segments,
    seq_len,
    label_pos,
    label_ids,
    table,
    w_qkv,
    w_out,
    w_up,
    w_down,
    small,
    position,
    t_table,
    t_qkv,
    t_out,
    t_up,
    t_down,
    t_small,
    t_position,
    mom_table,
    mom_qkv,
    mom_out,
    mom_up,
    mom_down,
    mom_small,
    mom_position,
    avg_table,
    avg_qkv,
    avg_out,
    avg_up,
    avg_down,
    avg_small,
    avg_position,
):
    micro, span = tok_ids.shape
    labels = label_pos.shape[1]
    share, width = table.shape
    groups = lax.axis_size("fsdp")
    dp = lax.axis_size("dp")
    devices = groups * dp
    own = lax.axis_index("fsdp")
    padded = (share // 32 + 1) * 32
    pad = padded - share
    rows_own = w_qkv.shape[0]
    slots = small.shape[0]

    info = jnp.concatenate(
        [tok_ids, label_ids, jnp.broadcast_to(seq_len[:, None], (micro, labels))], axis=1
    )
    info = jnp.pad(info, ((0, -micro % 8), (0, 0)))
    info = share_small(info, groups, 7)[:, :micro].reshape(groups * micro, span + 2 * labels)
    ids_all = info[:, :span]
    targets_all = info[:, span : span + labels].reshape(-1)
    lengths_all = info[:, span + labels]
    student_table = spread_dp([jnp.pad(table.astype(LOW), ((0, pad), (0, 0)))], dp, 1)[0]
    valid_local = label_valid(seq_len, labels, span)
    counts = jnp.stack([jnp.sum(valid_local), jnp.sum((seq_len > 0).astype(jnp.float32))])
    extra = jnp.broadcast_to(counts.astype(LOW)[None, :], (rows_own, 2))

    safe_ids = owned(ids_all, share, padded, groups, own)[1]
    t_weights, student_table = lax.optimization_barrier(
        ((t_qkv, t_out, t_up, t_down, t_small, t_position), student_table)
    )
    packed_teacher = pack_layer(t_weights, None)
    packed_teacher = lax.all_gather(packed_teacher, BOTH)
    safe_flat = safe_ids.reshape(-1)
    student_hits = student_table[safe_flat].reshape(groups * micro, span, width)
    student_hits, t_table = lax.optimization_barrier((student_hits, t_table))
    teacher_table = spread_dp([jnp.pad(t_table, ((0, pad), (0, 0)))], dp, 2)[0]
    tokens_student = lax.psum_scatter(
        student_hits,
        "fsdp",
        scatter_dimension=0,
        tiled=True,
    ).astype(jnp.float32)
    teacher_hits = teacher_table[safe_flat].reshape(groups * micro, span, width)
    s_weights, teacher_hits, packed_teacher = lax.optimization_barrier(
        ((w_qkv, w_out, w_up, w_down, small, position), teacher_hits, packed_teacher)
    )
    tokens_teacher = lax.psum_scatter(teacher_hits, "fsdp", scatter_dimension=0, tiled=True)
    packed_student = gather_weights([pack_layer(s_weights, extra)], dp, groups, 5)[0]
    weights, rest = unpack_layer(packed_student, span, slots)
    counted = jnp.sum(rest[::rows_own, :2].astype(jnp.float32), axis=0)
    label_count, count_seq = counted[0], counted[1]

    tables = (student_table, teacher_table)
    vocab_rows = student_table.shape[0]
    start, normed_start, inverse_start = embed_forward(tokens_student, weights, segments)
    student_out, kept = layer_forward(start, weights, seq_len)
    pick = (label_pos[..., None] == jnp.arange(span)).astype(LOW)
    student_rows = label_rows(pick, student_out)
    student_rows, tokens_teacher, packed_teacher = lax.optimization_barrier(
        (student_rows, tokens_teacher, packed_teacher)
    )
    teacher, _ = unpack_layer(packed_teacher, span, slots)
    student_rows = lax.all_gather(student_rows, "fsdp", axis=0, tiled=True)
    teacher_start = embed_forward(tokens_teacher.astype(jnp.float32), teacher, segments)[0]
    teacher_out = layer_forward(teacher_start, teacher, seq_len)[0]
    teacher_rows = label_rows(pick, teacher_out)
    teacher_rows = lax.all_gather(teacher_rows, "fsdp", axis=0, tiled=True)
    valid_group = label_valid(lengths_all, labels, span).reshape(-1)
    d_out, table_grad, label_loss = label_head(
        student_rows,
        teacher_rows,
        pick,
        tables,
        targets_all,
        valid_group,
        own,
        share,
        padded,
        groups,
        label_count,
    )
    cls_student = student_out[:, 0]
    unit_student, scale_student = unit_of(cls_student)
    unit_teacher = unit_of(teacher_out[:, 0])[0]
    weight_pkd = (PKD_WEIGHT * (seq_len > 0).astype(jnp.float32) / count_seq)[:, None]
    gap = unit_student - unit_teacher
    d_unit = 2.0 * weight_pkd * gap
    d_cls = scale_student * d_unit - cls_student * scale_student**3 * jnp.sum(
        cls_student * d_unit, axis=-1, keepdims=True
    )
    first_row = (jnp.arange(span) == 0).astype(jnp.float32)[None, :, None]
    d_out = d_out + first_row * d_cls[:, None, :]
    loss_part = label_loss + jnp.sum(weight_pkd * gap * gap)

    factors, rows_grad, d_start = layer_backward(d_out, weights, kept, seq_len)
    d_embed, gain_embed, shift_embed = layer_norm_back(
        d_start, normed_start, inverse_start, weights[4][12]
    )
    zero_segment = (segments == 0).astype(jnp.float32)[..., None]
    small_grad = jnp.concatenate(
        [
            rows_grad,
            gain_embed[None],
            shift_embed[None],
            jnp.sum(d_embed * zero_segment, axis=(0, 1))[None],
            jnp.sum(d_embed * (1.0 - zero_segment), axis=(0, 1))[None],
        ]
    )
    position_grad = jnp.sum(d_embed, axis=0)
    d_embed_low, factors = lax.optimization_barrier((d_embed.astype(LOW), factors))
    embed_grads = lax.all_gather(d_embed_low, "fsdp", axis=0, tiled=True)
    matrices = [
        product_of("bsd,bsf->df", left, right) for left, right in factors
    ]
    packed_grads = pack_grads(*matrices, small_grad, position_grad, devices)
    packed_grads = reduce_weights(packed_grads, dp, groups, 6)
    layer_squares = jnp.sum(packed_grads * packed_grads)
    table_grad, embed_grads, packed_grads, layer_squares = lax.optimization_barrier(
        (table_grad, embed_grads, packed_grads, layer_squares)
    )
    table_shard, table_squares = fold_dp(
        safe_flat, embed_grads.reshape(-1, width), table_grad, dp, share, 2048, 3
    )
    table_shard = table_shard[:share]
    grads = (table_shard,) + unpack_grads(packed_grads, rows_own, span, slots)
    squares = layer_squares + jnp.sum(table_squares)
    column = jnp.arange(128)[None, :]
    sums = jnp.where(column == 0, squares, jnp.where(column == 1, loss_part, 0.0))
    sums = total_all(jnp.broadcast_to(sums, (8, 128)), dp, groups, 4)
    total_sq, loss_value = sums[0, 0], sums[0, 1]
    grad_norm = jnp.sqrt(total_sq)
    factor = CLIP / jnp.maximum(grad_norm, CLIP)
    rate = RATE_SCALE * math.sqrt(NPARAM)
    params = (table, w_qkv, w_out, w_up, w_down, small, position)
    moms = (mom_table, mom_qkv, mom_out, mom_up, mom_down, mom_small, mom_position)
    avgs = (avg_table, avg_qkv, avg_out, avg_up, avg_down, avg_small, avg_position)
    news, moments, averages = ([], [], [])
    for weight, grad, momentum, average in zip(params, grads, moms, avgs):
        clipped = grad * factor
        moment = MOMENTUM * momentum + clipped
        fresh = weight - rate * (clipped + MOMENTUM * moment)
        news.append(fresh)
        moments.append(moment)
        averages.append(AVERAGE * average + (1.0 - AVERAGE) * fresh)
    return tuple(news) + tuple(moments) + tuple(averages) + (grad_norm, loss_value)


def solution(mesh):
    placed = (
        P(("dp", "fsdp"), None),
        P(("dp", "fsdp"), None),
        P(("dp", "fsdp")),
        P(("dp", "fsdp"), None),
        P(("dp", "fsdp"), None),
        P(("dp", "fsdp"), None),
        P(("dp", "fsdp"), None),
        P(("dp", "fsdp"), None),
        P(("dp", "fsdp"), None),
        P(("dp", "fsdp"), None),
        P(None, ("dp", "fsdp")),
        P(None, ("dp", "fsdp")),
        P(("dp", "fsdp"), None),
        P(("dp", "fsdp"), None),
        P(("dp", "fsdp"), None),
        P(("dp", "fsdp"), None),
        P(("dp", "fsdp"), None),
        P(None, ("dp", "fsdp")),
        P(None, ("dp", "fsdp")),
        P(("dp", "fsdp"), None),
        P(("dp", "fsdp"), None),
        P(("dp", "fsdp"), None),
        P(("dp", "fsdp"), None),
        P(("dp", "fsdp"), None),
        P(None, ("dp", "fsdp")),
        P(None, ("dp", "fsdp")),
        P(("dp", "fsdp"), None),
        P(("dp", "fsdp"), None),
        P(("dp", "fsdp"), None),
        P(("dp", "fsdp"), None),
        P(("dp", "fsdp"), None),
        P(None, ("dp", "fsdp")),
        P(None, ("dp", "fsdp")),
    )
    return jax.shard_map(
        on_device,
        mesh=mesh,
        in_specs=placed,
        out_specs=(
            P(("dp", "fsdp"), None),
            P(("dp", "fsdp"), None),
            P(("dp", "fsdp"), None),
            P(("dp", "fsdp"), None),
            P(("dp", "fsdp"), None),
            P(None, ("dp", "fsdp")),
            P(None, ("dp", "fsdp")),
            P(("dp", "fsdp"), None),
            P(("dp", "fsdp"), None),
            P(("dp", "fsdp"), None),
            P(("dp", "fsdp"), None),
            P(("dp", "fsdp"), None),
            P(None, ("dp", "fsdp")),
            P(None, ("dp", "fsdp")),
            P(("dp", "fsdp"), None),
            P(("dp", "fsdp"), None),
            P(("dp", "fsdp"), None),
            P(("dp", "fsdp"), None),
            P(("dp", "fsdp"), None),
            P(None, ("dp", "fsdp")),
            P(None, ("dp", "fsdp")),
            P(),
            P(),
        ),
        check_vma=False,
    )
```

```python
import functools
import math

import jax
import jax.numpy as jnp
from jax import lax
from jax.experimental import pallas as pl
from jax.experimental.pallas import tpu as pltpu
from jax.sharding import PartitionSpec as P

HD = 64
NPARAM = 30978048


SOFTMAX_HEAT = 2.0
SOFT_FRACTION = 0.5
PKD_WEIGHT = 10.0
MOMENTUM = 0.9
AVERAGE = 0.75
CLIP = 0.002
RATE_SCALE = 20.0
EPSILON = 1e-12
NEGATIVE = -1e30
BOTH = ("dp", "fsdp")
LOW = jnp.bfloat16
MIB = 1 << 20
CHUNK = 512


def push(src, dst, send, recv, where):
    copy = pltpu.make_async_remote_copy(
        src_ref=src,
        dst_ref=dst,
        send_sem=send,
        recv_sem=recv,
        device_id=where,
        device_id_type=pl.DeviceIdType.MESH,
    )
    copy.start()
    return copy


def greet(peers):
    barrier = pltpu.get_barrier_semaphore()
    for peer in peers:
        pl.semaphore_signal(barrier, inc=1, device_id=peer, device_id_type=pl.DeviceIdType.MESH)
    pl.semaphore_wait(barrier, len(peers))


def flipped(index, bit):
    return index + bit - 2 * bit * (lax.div(index, bit) % 2)


def spread_body(dp, count, groups, *refs):
    blocks, outs = refs[:count], refs[count : 2 * count]
    local, send, recv = refs[2 * count : 2 * count + 3]
    extra = refs[2 * count + 3 :]
    shared = []
    friends = []
    if groups:
        spot = lax.axis_index("fsdp")
        friends = [{"fsdp": lax.rem(spot + hop, groups)} for hop in range(1, groups)]

    def share_info():
        if groups:
            note, notes, note_send, note_recv = extra
            for hop, friend in enumerate(friends):
                shared.append(
                    push(note, notes.at[spot], note_send.at[hop], note_recv.at[hop], friend)
                )
            notes[spot] = note[...]

    me = lax.axis_index("dp")
    own = [pltpu.make_async_copy(blocks[k], outs[k].at[me], local.at[k]) for k in range(count)]
    for copy in own:
        copy.start()
    if dp == 4:
        near = [flipped(me, 1), flipped(me, 2)]
        greet([{"dp": near[0]}, {"dp": near[1]}] + friends)
        share_info()
        first = []
        for k in range(count):
            for step in range(2):
                for link in range(2):
                    half = step if link == 0 else 1 - step
                    first.append(
                        push(
                            blocks[k].at[half],
                            outs[k].at[me, half],
                            send.at[k, link, half],
                            recv.at[k, link, half],
                            {"dp": near[link]},
                        )
                    )
        for k in range(count):
            for link in range(2):
                first[k * 4 + link].wait_recv()
                origin = near[link]
                other = 1 - link
                first.append(
                    push(
                        outs[k].at[origin, link],
                        outs[k].at[origin, link],
                        send.at[k, 2, other],
                        recv.at[k, 2, other],
                        {"dp": near[other]},
                    )
                )
        for place, copy in enumerate(first):
            if place >= 4 * count or place % 4 >= 2:
                copy.wait_recv()
        for copy in first:
            copy.wait_send()
    else:
        peers = [lax.rem(me + hop, dp) for hop in range(1, dp)]
        greet([{"dp": peer} for peer in peers] + friends)
        share_info()
        sent = []
        for k in range(count):
            for hop, peer in enumerate(peers):
                sent.append(
                    push(
                        blocks[k],
                        outs[k].at[me],
                        send.at[k, hop, 0],
                        recv.at[k, hop, 0],
                        {"dp": peer},
                    )
                )
        for copy in sent:
            copy.wait()
    for copy in own:
        copy.wait()
    for copy in shared:
        copy.wait()


def spread_dp(blocks, dp, identity, info=None, groups=0):
    count = len(blocks)
    rows, width = blocks[0].shape
    cut = [block.reshape(2, rows // 2, width) for block in blocks]
    anywhere = pl.BlockSpec(memory_space=pl.ANY)
    vmem = pl.BlockSpec(memory_space=pltpu.VMEM)
    dma = pltpu.SemaphoreType.DMA
    out_shape = [jax.ShapeDtypeStruct((dp, 2, rows // 2, width), LOW)] * count
    in_specs, out_specs = [anywhere] * count, [anywhere] * count
    scratch = [
        dma((count,)),
        dma((count, max(3, dp - 1), 2)),
        dma((count, max(3, dp - 1), 2)),
    ]
    body = functools.partial(spread_body, dp, count, 0)
    if info is not None:
        cut.append(info)
        in_specs.append(vmem)
        out_shape.append(jax.ShapeDtypeStruct((groups,) + info.shape, info.dtype))
        out_specs.append(vmem)
        scratch += [dma((groups - 1,)), dma((groups - 1,))]

        def body(*refs):
            size = count + 1
            ins, outs, rest = refs[:size], refs[size : 2 * size], refs[2 * size :]
            spread_body(
                dp,
                count,
                groups,
                *ins[:count],
                *outs[:count],
                *rest[:3],
                ins[count],
                outs[count],
                *rest[3:],
            )

    outs = pl.pallas_call(
        body,
        out_shape=out_shape,
        in_specs=in_specs,
        out_specs=out_specs,
        scratch_shapes=scratch,
        compiler_params=pltpu.CompilerParams(collective_id=identity, has_side_effects=True),
        name="spread_tables",
    )(*cut)
    return [out.reshape(dp * rows, width) for out in outs[:count]] + list(outs[count:])


def ways_of(me, dp):
    if dp == 4:
        return [flipped(me, 1), flipped(me, 2)]
    return [lax.rem(me + hop, dp) for hop in range(1, dp)]


def sources_of(me, dp):
    if dp == 4:
        return [flipped(me, 1), flipped(me, 2)]
    return [lax.rem(me + dp - hop, dp) for hop in range(1, dp)]


def gather_body(dp, n, count, *refs):
    blocks, outs = refs[:count], refs[count : 2 * count]
    local, z_send, z_recv, way_send, way_recv, far_send, far_recv, core_send, core_recv = refs[
        2 * count :
    ]
    me = lax.axis_index("fsdp")
    row = lax.axis_index("dp")
    p = lax.div(me, 2)
    c = lax.rem(me, 2)
    partner = me + 1 - 2 * c
    ways = ways_of(row, dp)
    sources = sources_of(row, dp)
    barrier = pltpu.get_barrier_semaphore()

    def hello(where):
        pl.semaphore_signal(barrier, inc=1, device_id=where, device_id_type=pl.DeviceIdType.MESH)

    hello({"fsdp": partner})
    for way in ways:
        hello({"dp": way})

    @pl.when(p > 0)
    def _():
        hello({"fsdp": me - 2})

    @pl.when(p < n - 1)
    def _():
        hello({"fsdp": me + 2})

    @pl.when((p > 0) & (p < n - 1))
    def _():
        pl.semaphore_wait(barrier, 3 + len(ways))

    @pl.when((p == 0) | (p == n - 1))
    def _():
        pl.semaphore_wait(barrier, 2 + len(ways))

    def remote(src, dst, send, recv, where):
        return pltpu.make_async_remote_copy(
            src_ref=src,
            dst_ref=dst,
            send_sem=send,
            recv_sem=recv,
            device_id=where,
            device_id_type=pl.DeviceIdType.MESH,
        )

    def line(m, q, side):
        shard = outs[m].at[row, 2 * q + c]
        where = {"fsdp": me + 2 - 4 * side}
        return remote(shard, shard, z_send.at[m, side, q], z_recv.at[m, q], where)

    def way_copy(m, w, half, q):
        shard = outs[m].at[row, 2 * q + c, half]
        return remote(
            shard, shard, way_send.at[m, w, half, q], way_recv.at[m, w, half, q], {"dp": ways[w]}
        )

    def far_copy(m, w, q):
        shard = outs[m].at[sources[w], 2 * q + c, w]
        return remote(
            shard, shard, far_send.at[m, w, q], far_recv.at[m, w, q], {"dp": ways[1 - w]}
        )

    def core_copy(m, j, q, half):
        shard = outs[m].at[j, 2 * q + c, half]
        return remote(
            shard,
            shard,
            core_send.at[m, j, q, half],
            core_recv.at[m, j, q, half],
            {"fsdp": partner},
        )

    def onward(m, q):
        for half in range(2):
            for w in range(len(ways)):
                way_copy(m, w, half if w == 0 else 1 - half, q).start()
        for half in range(2):
            core_copy(m, row, q, half).start()

    def landed(m, q):
        for half in range(2):
            for w in range(len(ways)):
                part = half if w == 0 else 1 - half
                way_copy(m, w, part, q).wait_recv()
                if dp == 4 and part == w:
                    far_copy(m, w, q).start()
                core_copy(m, sources[w], q, part).start()

    def far_landed(m, q):
        if dp == 4:
            for w in range(2):
                far_copy(m, w, q).wait_recv()
                core_copy(m, dp - 1 - row, q, w).start()

    def each(distance, act):
        if distance == 0:
            act(p)
            return

        @pl.when(p >= distance)
        def _():
            act(p - distance)

        @pl.when(p + distance < n)
        def _():
            act(p + distance)

    for m in range(count):
        copy = pltpu.make_async_copy(blocks[m], outs[m].at[row, me], local.at[m])
        copy.start()
        copy.wait()

        @pl.when(p < n - 1)
        def _():
            line(m, p, 0).start()

        @pl.when(p > 0)
        def _():
            line(m, p, 1).start()

        onward(m, p)
    for distance in range(1, n + 2):
        for m in range(count):
            if distance < n:

                @pl.when(p >= distance)
                def _():
                    line(m, p - distance, 0).wait_recv()

                    @pl.when(p < n - 1)
                    def _():
                        line(m, p - distance, 0).start()

                    onward(m, p - distance)

                @pl.when(p + distance < n)
                def _():
                    line(m, p + distance, 1).wait_recv()

                    @pl.when(p > 0)
                    def _():
                        line(m, p + distance, 1).start()

                    onward(m, p + distance)

            if distance <= n:
                each(distance - 1, functools.partial(landed, m))
            if distance >= 2:
                each(distance - 2, functools.partial(far_landed, m))

    def settle(q, carry):
        for m in range(count):

            @pl.when((q <= p) & (p < n - 1))
            def _():
                line(m, q, 0).wait_send()

            @pl.when((q >= p) & (p > 0))
            def _():
                line(m, q, 1).wait_send()

            for half in range(2):
                for w in range(len(ways)):
                    way_copy(m, w, half, q).wait_send()
                if dp == 4:
                    far_copy(m, half, q).wait_send()
                for j in range(dp):
                    core_copy(m, j, q, half).wait()
        return carry

    lax.fori_loop(0, n, settle, 0)


def gather_weights(blocks, dp, groups, identity):
    count = len(blocks)
    width = blocks[0].shape[1]
    n = groups // 2
    cut = [block.reshape(2, block.shape[0] // 2, width) for block in blocks]
    ways = 2 if dp == 4 else dp - 1
    dma = pltpu.SemaphoreType.DMA
    outs = pl.pallas_call(
        functools.partial(gather_body, dp, n, count),
        out_shape=[jax.ShapeDtypeStruct((dp, groups) + block.shape, LOW) for block in cut],
        in_specs=[pl.BlockSpec(memory_space=pl.ANY)] * count,
        out_specs=[pl.BlockSpec(memory_space=pl.ANY)] * count,
        scratch_shapes=[
            dma((count,)),
            dma((count, 2, n)),
            dma((count, n)),
            dma((count, ways, 2, n)),
            dma((count, ways, 2, n)),
            dma((count, 2, n)),
            dma((count, 2, n)),
            dma((count, dp, n, 2)),
            dma((count, dp, n, 2)),
        ],
        compiler_params=pltpu.CompilerParams(collective_id=identity, has_side_effects=True),
        name="gather_weights",
    )(*cut)
    return [out.reshape(dp * groups, -1, width) for out in outs]


def dot_over(left, right, left_dim, right_dim):
    return lax.dot_general(
        left, right, (((left_dim,), (right_dim,)), ((), ())), preferred_element_type=jnp.float32
    )


def added(*values):
    total = values[0].astype(jnp.float32)
    for value in values[1:]:
        total = total + value.astype(jnp.float32)
    return total


def reduce_body(dp, n, pieces, g, out, core, far, near, last, right, left, core_sem, far_sem,
                near_sem, last_sem, line_sem):
    me = lax.axis_index("fsdp")
    row = lax.axis_index("dp")
    p = lax.div(me, 2)
    c = lax.rem(me, 2)
    partner = me + 1 - 2 * c
    ways = ways_of(row, dp)
    opposite = dp - 1 - row
    barrier = pltpu.get_barrier_semaphore()
    order = []
    for k in range((n + 1) // 2):
        order += [n - 1 - k] + ([k] if k != n - 1 - k else [])
    turns = [(i, q) for i in range(pieces) for q in order]

    def hello(where):
        pl.semaphore_signal(barrier, inc=1, device_id=where, device_id_type=pl.DeviceIdType.MESH)

    hello({"fsdp": partner})
    for way in ways:
        hello({"dp": way})

    @pl.when(p > 0)
    def _():
        hello({"fsdp": me - 2})

    @pl.when(p < n - 1)
    def _():
        hello({"fsdp": me + 2})

    @pl.when((p > 0) & (p < n - 1))
    def _():
        pl.semaphore_wait(barrier, 3 + len(ways))

    @pl.when((p == 0) | (p == n - 1))
    def _():
        pl.semaphore_wait(barrier, 2 + len(ways))

    def remote(src, dst, sems, index, where):
        return pltpu.make_async_remote_copy(
            src_ref=src,
            dst_ref=dst,
            send_sem=sems.at[(0,) + index],
            recv_sem=sems.at[(1,) + index],
            device_id=where,
            device_id_type=pl.DeviceIdType.MESH,
        )

    def core_copy(j, q, i, half):
        return remote(
            g.at[j, 2 * q + 1 - c, i, half],
            core.at[j, q, i, half],
            core_sem,
            (j, q, i, half),
            {"fsdp": partner},
        )

    def far_copy(q, i, w):
        return remote(
            core.at[opposite, q, i, w], far.at[q, i, w], far_sem, (q, i, w), {"dp": ways[w]}
        )

    def near_copy(q, i, w):
        return remote(
            core.at[ways[w], q, i, w], near.at[q, i, w], near_sem, (q, i, w, 0), {"dp": ways[w]}
        )

    def last_copy(q, i, w):
        return remote(
            far.at[q, i, w], last.at[q, i, w], last_sem, (q, i, w), {"dp": ways[1 - w]}
        )

    def direct_copy(hop, q, i, half):
        return remote(
            core.at[ways[hop], q, i, half],
            near.at[hop, q, i, half],
            near_sem,
            (q, i, half, hop),
            {"dp": ways[hop]},
        )

    def line_copy(buffer, q, i, side):
        return remote(
            buffer.at[q, i], buffer.at[q, i], line_sem, (q, i, side), {"fsdp": me + 2 - 4 * side}
        )

    for i, q in turns:
        for j in [opposite, *ways, row] if dp == 4 else range(dp):
            for half in range(2):
                core_copy(j, q, i, half).start()

    def pair(j, q, i, half):
        core_copy(j, q, i, half).wait_recv()
        core[j, q, i, half] = added(core[j, q, i, half], g[j, 2 * q + c, i, half]).astype(LOW)

    for i, q in turns:
        if dp == 4:
            for w in range(2):
                pair(opposite, q, i, w)
                far_copy(q, i, w).start()
            for w in range(2):
                pair(ways[w], q, i, w)
                near_copy(q, i, w).start()
            for w in range(2):
                pair(ways[w], q, i, 1 - w)
                pair(row, q, i, w)
        else:
            for half in range(2):
                for j in range(dp):
                    pair(j, q, i, half)
                for hop in range(dp - 1):
                    direct_copy(hop, q, i, half).start()

    def relay(i, q):
        if dp == 4:
            for w in range(2):
                far_copy(q, i, w).wait_recv()
                far[q, i, w] = added(far[q, i, w], core[ways[1 - w], q, i, w]).astype(LOW)
                last_copy(q, i, w).start()

    def total(q, i, half):
        if dp == 4:
            near_copy(q, i, half).wait_recv()
            last_copy(q, i, half).wait_recv()
            return added(core[row, q, i, half], near[q, i, half], last[q, i, half])
        parts = [core[row, q, i, half]]
        for hop in range(dp - 1):
            direct_copy(hop, q, i, half).wait_recv()
            parts.append(near[hop, q, i, half])
        return added(*parts)

    def line_up(i, q):
        sums = [total(q, i, half) for half in range(2)]

        def store(buffer, side, first):
            for half in range(2):
                if first:
                    buffer[q, i, half] = sums[half].astype(LOW)
                else:
                    buffer[q, i, half] = added(sums[half], buffer[q, i, half]).astype(LOW)
            line_copy(buffer, q, i, side).start()

        if q > 0:

            @pl.when((p > 0) & (p < q))
            def _():
                line_copy(right, q, i, 0).wait_recv()
                store(right, 0, False)

            @pl.when((p == 0) & (p < q))
            def _():
                store(right, 0, True)

        if q < n - 1:

            @pl.when((p < n - 1) & (p > q))
            def _():
                line_copy(left, q, i, 1).wait_recv()
                store(left, 1, False)

            @pl.when((p == n - 1) & (p > q))
            def _():
                store(left, 1, True)

        @pl.when(p == q)
        def _():
            for half in range(2):
                out[i, half] = sums[half]

    for k in range(len(turns) + n):
        if k < len(turns):
            relay(*turns[k])
        if k >= n:
            line_up(*turns[k - n])

    @pl.when(p > 0)
    def _():
        for i in range(pieces):
            line_copy(right, p, i, 0).wait_recv()
            out[i] = added(out[i], right[p, i])

    @pl.when(p < n - 1)
    def _():
        for i in range(pieces):
            line_copy(left, p, i, 1).wait_recv()
            out[i] = added(out[i], left[p, i])

    for i, q in turns:
        for half in range(2):
            for j in range(dp):
                core_copy(j, q, i, half).wait_send()
            if dp == 4:
                far_copy(q, i, half).wait_send()
                near_copy(q, i, half).wait_send()
                last_copy(q, i, half).wait_send()
            else:
                for hop in range(dp - 1):
                    direct_copy(hop, q, i, half).wait_send()

        @pl.when(p < q)
        def _():
            line_copy(right, q, i, 0).wait_send()

        @pl.when(p > q)
        def _():
            line_copy(left, q, i, 1).wait_send()


def reduce_weights(g, dp, groups, pieces, identity):
    devices, rows, width = g.shape
    n = groups // 2
    half = rows // (2 * pieces)
    g = g.reshape(dp, groups, pieces, 2, half, width)
    dma = pltpu.SemaphoreType.DMA
    block = pltpu.VMEM((n, pieces, 2, half, width), LOW)
    near = block if dp == 4 else pltpu.VMEM((dp - 1, n, pieces, 2, half, width), LOW)
    out = pl.pallas_call(
        functools.partial(reduce_body, dp, n, pieces),
        out_shape=jax.ShapeDtypeStruct((pieces, 2, half, width), jnp.float32),
        in_specs=[pl.BlockSpec(memory_space=pltpu.VMEM)],
        out_specs=pl.BlockSpec(memory_space=pltpu.VMEM),
        scratch_shapes=[
            pltpu.VMEM((dp, n, pieces, 2, half, width), LOW),
            block,
            near,
            block,
            block,
            block,
            dma((2, dp, n, pieces, 2)),
            dma((2, n, pieces, 2)),
            dma((2, n, pieces, 2, max(1, dp - 1))),
            dma((2, n, pieces, 2)),
            dma((2, n, pieces, 2)),
        ],
        compiler_params=pltpu.CompilerParams(
            collective_id=identity, has_side_effects=True, vmem_limit_bytes=56 * MIB
        ),
        name="reduce_weights",
    )(g)
    return out.reshape(rows, width)


def fold_body(dp, step, share, ids, rows, base, out, squares, g, near_buffer, far_buffer, last_buffer, sems):
    me = lax.axis_index("dp")
    half_rows = base.shape[2]
    tokens = rows.shape[0]

    def fill(dest, half):
        first = (dest * 2 + half) * half_rows
        vocab = lax.broadcasted_iota(jnp.int32, (half_rows, step), 0) + first

        def turn(k, total):
            chosen = (vocab == ids[k]).astype(jnp.float32).astype(LOW)
            start = pl.multiple_of(k * step, step)
            return total + dot_over(chosen, rows[pl.ds(start, step), :], 1, 0)

        return lax.fori_loop(0, tokens // step, turn, base[dest, half])

    if dp == 4:
        near = [flipped(me, 1), flipped(me, 2)]
        far = dp - 1 - me
        greet([{"dp": near[0]}, {"dp": near[1]}])

        def send(kind, w, src, dst, way):
            return push(src, dst, sems.at[0, kind, w], sems.at[1, kind, w], {"dp": near[way]})

        first, second, third = [], [], []
        for w in range(2):
            g[far, w] = fill(far, w).astype(LOW)
            first.append(send(0, w, g.at[far, w], far_buffer.at[w], w))
        for w in range(2):
            g[near[w], w] = fill(near[w], w).astype(LOW)
            second.append(send(1, w, g.at[near[w], w], near_buffer.at[w], w))
        for w in range(2):
            part = fill(near[1 - w], w)
            first[w].wait_recv()
            far_buffer[w] = (part + far_buffer[w].astype(jnp.float32)).astype(LOW)
            third.append(send(2, w, far_buffer.at[w], last_buffer.at[w], 1 - w))
        for w in range(2):
            out[w] = fill(me, w)
        for w in range(2):
            second[w].wait_recv()
            third[w].wait_recv()
            out[w] = (
                out[w]
                + near_buffer[w].astype(jnp.float32)
                + last_buffer[w].astype(jnp.float32)
            )
        for copy in first + second + third:
            copy.wait_send()
    else:
        peers = [lax.rem(me + hop, dp) for hop in range(1, dp)]
        greet([{"dp": peer} for peer in peers])
        sent = []
        for hop, peer in enumerate(peers):
            for half in range(2):
                g[peer, half] = fill(peer, half).astype(LOW)
            sent.append(
                push(
                    g.at[peer],
                    near_buffer.at[hop],
                    sems.at[0, hop, 0],
                    sems.at[1, hop, 0],
                    {"dp": peer},
                )
            )
        for half in range(2):
            out[half] = fill(me, half)
        for hop in range(dp - 1):
            sent[hop].wait()
            out[...] = out[...] + near_buffer[hop].astype(jnp.float32)
    total = jnp.zeros((1, out.shape[2]), jnp.float32)
    for half in range(2):
        index = lax.broadcasted_iota(jnp.int32, (half_rows, 1), 0) + half * half_rows
        value = jnp.where(index < share, out[half], 0.0)
        total = total + jnp.sum(value * value, axis=0, keepdims=True)
    squares[...] = total


def fold_dp(ids, rows, base, dp, share, step, identity):
    tokens, width = rows.shape
    padded = base.shape[0] // dp
    half = padded // 2
    block = pltpu.VMEM((2, half, width), LOW)
    first = block if dp == 4 else pltpu.VMEM((dp - 1, 2, half, width), LOW)
    vmem = pl.BlockSpec(memory_space=pltpu.VMEM)
    out, squares = pl.pallas_call(
        functools.partial(fold_body, dp, step, share),
        out_shape=[
            jax.ShapeDtypeStruct((2, half, width), jnp.float32),
            jax.ShapeDtypeStruct((1, width), jnp.float32),
        ],
        in_specs=[vmem, vmem, vmem],
        out_specs=[vmem, vmem],
        scratch_shapes=[
            pltpu.VMEM((dp, 2, half, width), LOW),
            first,
            block,
            block,
            pltpu.SemaphoreType.DMA((2, max(3, dp - 1), 2)),
        ],
        compiler_params=pltpu.CompilerParams(
            collective_id=identity, has_side_effects=True, vmem_limit_bytes=58 * MIB
        ),
        name="fold_table",
    )(ids.reshape(tokens // step, 1, step), rows, base.reshape(dp, 2, half, width))
    return out.reshape(padded, width), squares


def share_body(groups, x, out, send, recv):
    me = lax.axis_index("fsdp")
    peers = [lax.rem(me + hop, groups) for hop in range(1, groups)]
    greet([{"fsdp": peer} for peer in peers])
    sent = []
    for hop, peer in enumerate(peers):
        sent.append(push(x, out.at[me], send.at[hop], recv.at[hop], {"fsdp": peer}))
    out[me] = x[...]
    for copy in sent:
        copy.wait()


def share_small(x, groups, identity):
    return pl.pallas_call(
        functools.partial(share_body, groups),
        out_shape=jax.ShapeDtypeStruct((groups,) + x.shape, x.dtype),
        in_specs=[pl.BlockSpec(memory_space=pltpu.VMEM)],
        out_specs=pl.BlockSpec(memory_space=pltpu.VMEM),
        scratch_shapes=[pltpu.SemaphoreType.DMA((groups - 1,))] * 2,
        compiler_params=pltpu.CompilerParams(collective_id=identity, has_side_effects=True),
        name="share_small",
    )(x)


def total_body(dp, groups, x, out, fsdp_parts, dp_value, dp_parts, send, recv):
    me = lax.axis_index("fsdp")
    row = lax.axis_index("dp")
    peers = [lax.rem(me + hop, groups) for hop in range(1, groups)]
    rows = [lax.rem(row + hop, dp) for hop in range(1, dp)]
    greet([{"fsdp": peer} for peer in peers] + [{"dp": peer} for peer in rows])
    sent = []
    for hop, peer in enumerate(peers):
        sent.append(push(x, fsdp_parts.at[me], send.at[hop], recv.at[hop], {"fsdp": peer}))
    fsdp_parts[me] = x[...]
    for copy in sent:
        copy.wait()
    value = fsdp_parts[0]
    for k in range(1, groups):
        value = value + fsdp_parts[k]
    dp_value[...] = value
    dp_parts[row] = value
    sent = []
    for hop, peer in enumerate(rows):
        place = groups - 1 + hop
        sent.append(
            push(dp_value, dp_parts.at[row], send.at[place], recv.at[place], {"dp": peer})
        )
    for copy in sent:
        copy.wait()
    value = dp_parts[0]
    for k in range(1, dp):
        value = value + dp_parts[k]
    out[...] = value


def total_all(x, dp, groups, identity):
    count = dp + groups - 2
    tile = (8, 128)
    return pl.pallas_call(
        functools.partial(total_body, dp, groups),
        out_shape=jax.ShapeDtypeStruct(tile, jnp.float32),
        in_specs=[pl.BlockSpec(memory_space=pltpu.VMEM)],
        out_specs=pl.BlockSpec(memory_space=pltpu.VMEM),
        scratch_shapes=[
            pltpu.VMEM((groups,) + tile, jnp.float32),
            pltpu.VMEM(tile, jnp.float32),
            pltpu.VMEM((dp,) + tile, jnp.float32),
            pltpu.SemaphoreType.DMA((count,)),
            pltpu.SemaphoreType.DMA((count,)),
        ],
        compiler_params=pltpu.CompilerParams(collective_id=identity, has_side_effects=True),
        name="total",
    )(x)


def block_rows(ref_rows, share):
    block = pl.program_id(0)
    index = lax.broadcasted_iota(jnp.int32, (ref_rows, 1), 0)
    real = index + lax.rem(block, 2) * ref_rows < share
    return index + block * ref_rows, real


def student_logits_body(share, rows, table, target, logits, stats):
    index, real = block_rows(table.shape[0], share)
    value = jnp.where(real, dot_over(table[...], rows[...], 1, 1), NEGATIVE)
    logits[...] = value
    top = jnp.max(value, axis=0, keepdims=True)
    hit = jnp.sum(jnp.where(index == target[...], value, 0.0), axis=0, keepdims=True)

    @pl.when(pl.program_id(0) == 0)
    def _():
        half = jnp.exp((value - top) / SOFTMAX_HEAT)
        stats[0:1] = top
        stats[1:2] = jnp.sum(half * half, axis=0, keepdims=True)
        stats[2:3] = jnp.sum(half, axis=0, keepdims=True)
        stats[3:4] = hit

    @pl.when(pl.program_id(0) > 0)
    def _():
        before = stats[0:1]
        peak = jnp.maximum(before, top)
        fall = jnp.exp((before - peak) / SOFTMAX_HEAT)
        half = jnp.exp((value - peak) / SOFTMAX_HEAT)
        stats[0:1] = peak
        stats[1:2] = stats[1:2] * fall * fall + jnp.sum(half * half, axis=0, keepdims=True)
        stats[2:3] = stats[2:3] * fall + jnp.sum(half, axis=0, keepdims=True)
        stats[3:4] = stats[3:4] + hit


def teacher_logits_body(share, rows, table, student, logits, stats):
    _, real = block_rows(table.shape[0], share)
    value = jnp.where(real, dot_over(table[...], rows[...], 1, 1), NEGATIVE)
    logits[...] = value
    top = jnp.max(value, axis=0, keepdims=True)
    gap = (value - student[...]) / SOFTMAX_HEAT

    @pl.when(pl.program_id(0) == 0)
    def _():
        exponent = jnp.exp((value - top) / SOFTMAX_HEAT)
        stats[0:1] = top
        stats[1:2] = jnp.sum(exponent, axis=0, keepdims=True)
        stats[2:3] = jnp.sum(exponent * gap, axis=0, keepdims=True)
        stats[3:4] = jnp.zeros_like(top)

    @pl.when(pl.program_id(0) > 0)
    def _():
        before = stats[0:1]
        peak = jnp.maximum(before, top)
        fall = jnp.exp((before - peak) / SOFTMAX_HEAT)
        exponent = jnp.exp((value - peak) / SOFTMAX_HEAT)
        stats[0:1] = peak
        stats[1:2] = stats[1:2] * fall + jnp.sum(exponent, axis=0, keepdims=True)
        stats[2:3] = stats[2:3] * fall + jnp.sum(exponent * gap, axis=0, keepdims=True)


def logits_call(body, rows, table, other, block, name):
    count, width = rows.shape
    vocab = table.shape[0]
    wide = pl.BlockSpec((block, count), lambda v: (v, 0))
    whole = pl.BlockSpec(memory_space=pltpu.VMEM)
    return pl.pallas_call(
        body,
        grid=(vocab // block,),
        in_specs=[
            whole,
            pl.BlockSpec((block, width), lambda v: (v, 0)),
            wide if other.shape[0] == vocab else whole,
        ],
        out_specs=[wide, pl.BlockSpec((4, count), lambda v: (0, 0))],
        out_shape=[
            jax.ShapeDtypeStruct((vocab, count), jnp.float32),
            jax.ShapeDtypeStruct((4, count), jnp.float32),
        ],
        compiler_params=pltpu.CompilerParams(vmem_limit_bytes=40 * MIB),
        cost_estimate=pl.CostEstimate(
            flops=2 * vocab * count * width,
            bytes_accessed=4 * vocab * count + 2 * vocab * width,
            transcendentals=vocab * count,
        ),
        name=name,
    )(rows, table, other)


def logits_back_body(student, teacher, table, consts, target, d_logits, d_rows, total):
    index = lax.broadcasted_iota(jnp.int32, (table.shape[0], 1), 0)
    index = index + pl.program_id(0) * table.shape[0]
    value = student[...]
    hard = jnp.exp(value - consts[0:1]) - (index == target[...]).astype(jnp.float32)
    soft = jnp.exp(value / SOFTMAX_HEAT - consts[1:2]) - jnp.exp(
        teacher[...] / SOFTMAX_HEAT - consts[2:3]
    )
    mixed = consts[3:4] * (
        (1.0 - SOFT_FRACTION) * hard + SOFT_FRACTION * SOFTMAX_HEAT * soft
    )
    low = mixed.astype(LOW)
    d_logits[...] = low
    part = dot_over(low, table[...], 0, 0)

    @pl.when(pl.program_id(0) == 0)
    def _():
        total[...] = part

    @pl.when(pl.program_id(0) > 0)
    def _():
        total[...] += part

    @pl.when(pl.program_id(0) == pl.num_programs(0) - 1)
    def _():
        d_rows[...] = total[...].astype(LOW)


def logits_back(student, teacher, table, consts, target, block):
    vocab, count = student.shape
    width = table.shape[1]
    wide = pl.BlockSpec((block, count), lambda v: (v, 0))
    whole = pl.BlockSpec(memory_space=pltpu.VMEM)
    return pl.pallas_call(
        logits_back_body,
        grid=(vocab // block,),
        in_specs=[wide, wide, pl.BlockSpec((block, width), lambda v: (v, 0)), whole, whole],
        out_specs=[wide, pl.BlockSpec((count, width), lambda v: (0, 0))],
        out_shape=[
            jax.ShapeDtypeStruct((vocab, count), LOW),
            jax.ShapeDtypeStruct((count, width), LOW),
        ],
        scratch_shapes=[pltpu.VMEM((count, width), jnp.float32)],
        compiler_params=pltpu.CompilerParams(vmem_limit_bytes=48 * MIB),
        cost_estimate=pl.CostEstimate(
            flops=2 * vocab * count * width,
            bytes_accessed=10 * vocab * count + 2 * vocab * width,
            transcendentals=3 * vocab * count,
        ),
        name="logits_back",
    )(student, teacher, table, consts, target)


def attend_body(lengths, q_ref, k_ref, v_ref, out_ref):
    live = jnp.maximum(lengths[pl.program_id(0)], 1)
    span = q_ref.shape[1]
    k, v = k_ref[0], v_ref[0]
    keep = lax.broadcasted_iota(jnp.int32, (span, CHUNK), 0) < live
    low_lane = lax.broadcasted_iota(jnp.int32, (CHUNK, 2 * HD), 1) < HD
    for first in range(0, span, CHUNK):
        q = q_ref[0, first : first + CHUNK, :]
        parts = []
        for head in range(2):
            mine = low_lane if head == 0 else jnp.logical_not(low_lane)
            scores = dot_over(k, jnp.where(mine, q * 0.125, jnp.zeros_like(q)), 1, 1)
            scores = jnp.where(keep, scores, NEGATIVE)
            exponent = jnp.exp(scores - jnp.max(scores, axis=0, keepdims=True))
            scale = 1.0 / jnp.sum(exponent, axis=0, keepdims=True)
            parts.append(dot_over((exponent * scale).astype(LOW), v, 0, 0))
        out_ref[0, first : first + CHUNK, :] = jnp.where(low_lane, parts[0], parts[1]).astype(LOW)


def attend(joined, lengths):
    micro, span, wide = joined.shape
    width = wide // 3
    pairs = width // (2 * HD)

    def place(third):
        return pl.BlockSpec((1, span, 2 * HD), lambda b, h, _: (b, 0, third * pairs + h))

    return pl.pallas_call(
        attend_body,
        grid_spec=pltpu.PrefetchScalarGridSpec(
            num_scalar_prefetch=1,
            grid=(micro, pairs),
            in_specs=[place(0), place(1), place(2)],
            out_specs=pl.BlockSpec((1, span, 2 * HD), lambda b, h, _: (b, 0, h)),
        ),
        out_shape=jax.ShapeDtypeStruct((micro, span, width), LOW),
        cost_estimate=pl.CostEstimate(
            flops=4 * micro * span * span * width,
            bytes_accessed=8 * micro * span * width,
            transcendentals=micro * span * span * width // HD,
        ),
        name="attend",
    )(lengths, joined, joined, joined)


def attend_back_body(lengths, q_ref, k_ref, v_ref, d_ref, out_ref, g_keys, g_values):
    live = jnp.maximum(lengths[pl.program_id(0)], 1)
    span = q_ref.shape[1]
    k, v = k_ref[0], v_ref[0]
    keep = lax.broadcasted_iota(jnp.int32, (span, CHUNK), 0) < live
    low_lane = lax.broadcasted_iota(jnp.int32, (CHUNK, 2 * HD), 1) < HD
    low_wide = lax.broadcasted_iota(jnp.int32, (span, 2 * HD), 1) < HD
    for first in range(0, span, CHUNK):
        q = q_ref[0, first : first + CHUNK, :]
        d = d_ref[0, first : first + CHUNK, :]
        parts = []
        for head in range(2):
            mine = low_lane if head == 0 else jnp.logical_not(low_lane)
            scores = dot_over(k, jnp.where(mine, q * 0.125, jnp.zeros_like(q)), 1, 1)
            scores = jnp.where(keep, scores, NEGATIVE)
            exponent = jnp.exp(scores - jnp.max(scores, axis=0, keepdims=True))
            probs = exponent * (1.0 / jnp.sum(exponent, axis=0, keepdims=True))
            d_probs = dot_over(v, jnp.where(mine, d, jnp.zeros_like(d)), 1, 1)
            inner = jnp.sum(probs * d_probs, axis=0, keepdims=True)
            d_scores = (probs * (d_probs - inner)).astype(LOW)
            value_part = dot_over(probs.astype(LOW), d, 1, 0)
            key_part = dot_over(d_scores, q, 1, 0)
            if first == 0:
                g_values[head] = value_part
                g_keys[head] = key_part
            else:
                g_values[head] += value_part
                g_keys[head] += key_part
            parts.append(dot_over(d_scores, k, 0, 0))
        out_ref[0, 0, first : first + CHUNK, :] = (
            jnp.where(low_lane, parts[0], parts[1]) * 0.125
        ).astype(LOW)
    out_ref[1, 0] = (jnp.where(low_wide, g_keys[0], g_keys[1]) * 0.125).astype(LOW)
    out_ref[2, 0] = jnp.where(low_wide, g_values[0], g_values[1]).astype(LOW)


def attend_back(joined, d_context, lengths):
    micro, span, width = d_context.shape
    pairs = width // (2 * HD)

    def place(third):
        return pl.BlockSpec((1, span, 2 * HD), lambda b, h, _: (b, 0, third * pairs + h))

    return pl.pallas_call(
        attend_back_body,
        grid_spec=pltpu.PrefetchScalarGridSpec(
            num_scalar_prefetch=1,
            grid=(micro, pairs),
            in_specs=[place(0), place(1), place(2), place(0)],
            out_specs=pl.BlockSpec((3, 1, span, 2 * HD), lambda b, h, _: (0, b, 0, h)),
            scratch_shapes=[
                pltpu.VMEM((2, span, 2 * HD), jnp.float32),
                pltpu.VMEM((2, span, 2 * HD), jnp.float32),
            ],
        ),
        out_shape=jax.ShapeDtypeStruct((3, micro, span, width), LOW),
        cost_estimate=pl.CostEstimate(
            flops=10 * micro * span * span * width,
            bytes_accessed=14 * micro * span * width,
            transcendentals=micro * span * span * width // HD,
        ),
        name="attend_back",
    )(lengths, joined, joined, joined, d_context)


def product_of(form, left, right):
    return jnp.einsum(form, left, right, preferred_element_type=jnp.float32)


def owned(ids, share, padded, groups, own):
    block = ids // share
    inside = block % groups == own
    local = block // groups * padded + ids % share
    return (inside, jnp.where(inside, local, share))


def layer_norm_keep(value, gain, shift):
    mean = jnp.mean(value, axis=-1, keepdims=True)
    centred = value - mean
    inverse = lax.rsqrt(jnp.mean(centred * centred, axis=-1, keepdims=True) + EPSILON)
    normed = centred * inverse
    return (normed * gain + shift, normed, inverse)


def layer_norm_back(grad, normed, inverse, gain):
    axes = tuple(range(grad.ndim - 1))
    gain_grad = jnp.sum(grad * normed, axis=axes)
    shift_grad = jnp.sum(grad, axis=axes)
    scaled = grad * gain
    centred = scaled - jnp.mean(scaled, axis=-1, keepdims=True)
    return (
        inverse * (centred - normed * jnp.mean(scaled * normed, axis=-1, keepdims=True)),
        gain_grad,
        shift_grad,
    )


def gelu_parts(upward):
    normal_cdf = 0.5 * (1.0 + lax.erf(upward * 0.7071067811865476))
    density = jnp.exp(-0.5 * upward * upward) * 0.3989422804014327
    return (upward * normal_cdf, normal_cdf + upward * density)


def label_valid(lengths, labels, span):
    needed = (lengths * labels + span - 1) // span
    return (jnp.arange(labels)[None, :] < needed[:, None]).astype(jnp.float32)


def pack_body(*refs):
    out = refs[-1]
    width = out.shape[1]
    first = 0
    for ref in refs[:-1]:
        rows = ref.shape[0]
        for k in range(ref.shape[1] // width):
            piece = ref[:, k * width : (k + 1) * width]
            out[first : first + rows, :] = piece.astype(LOW)
            first += rows
    if first < out.shape[0]:
        out[first:, :] = jnp.zeros((out.shape[0] - first, width), LOW)


def pack_rows(arrays, width):
    filled = sum(array.size // width for array in arrays)
    padded = filled + -filled % 32
    if any(array.shape[0] % 16 for array in arrays) and arrays[0].shape[0] % 8:
        pieces = []
        for array in arrays:
            for k in range(array.shape[1] // width):
                pieces.append(array[:, k * width : (k + 1) * width].astype(LOW))
        return jnp.pad(jnp.concatenate(pieces, axis=0), ((0, padded - filled), (0, 0)))
    vmem = pl.BlockSpec(memory_space=pltpu.VMEM)
    return pl.pallas_call(
        pack_body,
        in_specs=[vmem] * len(arrays),
        out_specs=vmem,
        out_shape=jax.ShapeDtypeStruct((padded, width), LOW),
        name="pack_rows",
    )(*arrays)


def pack_rest(small, position, extra, width):
    rest = [position.astype(LOW).T, small.astype(LOW).T]
    rest = jnp.concatenate(rest + ([] if extra is None else [extra]), axis=1)
    return jnp.pad(rest, ((0, 0), (0, width - rest.shape[1])))


def unpack_rows(packed, layout):
    devices, _, width = packed.shape
    parts = []
    first = 0
    for rows, count in layout:
        pieces = []
        for k in range(count):
            piece = packed[:, first : first + rows].reshape(devices * rows, width)
            pieces.append(piece)
            first += rows
        parts.append(pieces[0] if count == 1 else jnp.concatenate(pieces, axis=1))
    return parts


def unpack_rest(rest, span, slots):
    position = rest[:, :span].T.astype(jnp.float32)
    small = rest[:, span : span + slots].T.astype(jnp.float32)
    return small, position, rest[:, span + slots :]


def embed_forward(token_rows, weights, segment_ids):
    small, position = weights[4:]
    segment_rows = jnp.where(segment_ids[..., None] == 0, small[14], small[15])
    return layer_norm_keep(token_rows + position + segment_rows, small[12], small[13])


def layer_forward(value, weights, lengths):
    w_qkv, w_out, w_up, w_down, small = weights[:5]
    micro, span, width = value.shape
    value_low = value.astype(LOW)
    bias = jnp.concatenate([small[0], jnp.zeros_like(small[0]), small[1]])
    joined = (product_of("bsd,df->bsf", value_low, w_qkv) + bias).astype(LOW)
    context = attend(joined, lengths)
    attn = product_of("bsc,cd->bsd", context, w_out) + small[2]
    first, normed_first, inverse_first = layer_norm_keep(value + attn, small[8], small[9])
    first_low = first.astype(LOW)
    upward = product_of("bsd,df->bsf", first_low, w_up) + small[3:7].reshape(-1)
    act, slope = gelu_parts(upward)
    slope = slope.astype(LOW)
    act_low = act.astype(LOW)
    down = product_of("bsf,fd->bsd", act_low, w_down) + small[7]
    out, normed_second, inverse_second = layer_norm_keep(first + down, small[10], small[11])
    return (
        out,
        (
            value_low,
            joined,
            context,
            normed_first,
            inverse_first,
            first_low,
            slope,
            act_low,
            normed_second,
            inverse_second,
        ),
    )


def layer_backward(grad, weights, kept, lengths):
    w_qkv, w_out, w_up, w_down, small = weights[:5]
    (
        value_low,
        joined,
        context,
        normed_first,
        inverse_first,
        first_low,
        slope,
        act_low,
        normed_second,
        inverse_second,
    ) = kept
    micro, span, width = value_low.shape
    d_second, gain_second, shift_second = layer_norm_back(
        grad, normed_second, inverse_second, small[10]
    )
    d_second, d_down = lax.optimization_barrier((d_second, d_second.astype(LOW)))
    d_up = (product_of("bsd,fd->bsf", d_down, w_down) * slope).astype(LOW)
    d_first = d_second + product_of("bsf,df->bsd", d_up, w_up)
    d_sum, gain_first, shift_first = layer_norm_back(d_first, normed_first, inverse_first, small[8])
    d_attn = d_sum.astype(LOW)
    d_context = product_of("bsd,cd->bsc", d_attn, w_out).astype(LOW)
    d_joined = jnp.concatenate(list(attend_back(joined, d_context, lengths)), axis=-1)
    d_value = d_sum + product_of("bsf,df->bsd", d_joined, w_qkv)

    def column_sum(value):
        return jnp.sum(value.astype(jnp.float32), axis=(0, 1))

    joined_sum = column_sum(d_joined)
    rows_grad = jnp.concatenate(
        [
            joined_sum[:width][None],
            joined_sum[2 * width :][None],
            column_sum(d_attn)[None],
            column_sum(d_up).reshape(-1, width),
            column_sum(d_down)[None],
            gain_first[None],
            shift_first[None],
            gain_second[None],
            shift_second[None],
        ]
    )
    factors = (
        (value_low, d_joined),
        (context, d_attn),
        (first_low, d_up),
        (act_low, d_down),
    )
    return factors, rows_grad, d_value


def label_rows(pick, out):
    micro, labels, _ = pick.shape
    rows = product_of("bps,bsd->bpd", pick, out.astype(LOW)).astype(LOW)
    return rows.reshape(micro * labels, out.shape[-1])


def label_head(
    all_student, all_teacher, pick, tables, targets, valid_mask, own, share, padded, groups, count
):
    table_student, table_teacher = tables
    vocab_rows = table_student.shape[0]
    micro, labels, span = pick.shape
    width = all_student.shape[1]
    mine = micro * labels
    inside, local_target = owned(targets, share, padded, groups, own)
    target = jnp.where(inside, local_target, -1)[None, :]
    block = padded // 2
    student, student_stats = logits_call(
        functools.partial(student_logits_body, share),
        all_student,
        table_student,
        target,
        block,
        "student_logits",
    )
    teacher, teacher_stats = logits_call(
        functools.partial(teacher_logits_body, share),
        all_teacher,
        table_teacher,
        student,
        block,
        "teacher_logits",
    )
    stats = share_small(jnp.concatenate([student_stats, teacher_stats]), groups, 8)
    peak_student = jnp.max(stats[:, 0], axis=0)
    peak_teacher = jnp.max(stats[:, 4], axis=0)
    fall_student = jnp.exp((stats[:, 0] - peak_student) / SOFTMAX_HEAT)
    fall_teacher = jnp.exp((stats[:, 4] - peak_teacher) / SOFTMAX_HEAT)
    sum_plain = jnp.sum(stats[:, 1] * fall_student * fall_student, axis=0)
    sum_soft = jnp.sum(stats[:, 2] * fall_student, axis=0)
    sum_teacher = jnp.sum(stats[:, 5] * fall_teacher, axis=0)
    cross = jnp.sum(stats[:, 6] * fall_teacher, axis=0)
    target_logit = jnp.sum(stats[:, 3], axis=0)
    lse_plain = peak_student + jnp.log(sum_plain)
    lse_soft = peak_student / SOFTMAX_HEAT + jnp.log(sum_soft)
    lse_teacher = peak_teacher / SOFTMAX_HEAT + jnp.log(sum_teacher)
    cross_entropy = lse_plain - target_logit
    divergence_loss = cross / sum_teacher - lse_teacher + lse_soft
    share_lab = valid_mask / count
    consts = jnp.stack([lse_plain, lse_soft, lse_teacher, share_lab])
    d_logits, d_rows = logits_back(student, teacher, table_student, consts, target, block)
    d_rows = lax.psum_scatter(d_rows, "fsdp", scatter_dimension=0, tiled=True)
    table_term = product_of("vp,pd->vd", d_logits, all_student)
    d_rows, table_term = lax.optimization_barrier((d_rows, table_term))
    terms = share_lab * (
        (1.0 - SOFT_FRACTION) * cross_entropy
        + SOFT_FRACTION * SOFTMAX_HEAT * SOFTMAX_HEAT * divergence_loss
    )
    local = lax.dynamic_slice_in_dim(terms, own * mine, mine)
    d_out = product_of("bps,bpd->bsd", pick, d_rows.reshape(micro, -1, width))
    return (d_out, table_term, jnp.sum(local))


def pack_grads(g_qkv, g_out, g_up, g_down, small_grad, position_grad, devices):
    width = g_out.shape[0]
    rows = width // devices

    def shards(grad):
        return grad.astype(LOW).reshape(devices, -1, width)

    pieces = [shards(g_qkv[:, k * width : (k + 1) * width]) for k in range(3)]
    pieces += [shards(g_out)]
    pieces += [shards(g_up[:, k * width : (k + 1) * width]) for k in range(4)]
    pieces += [shards(g_down)]
    rest = jnp.concatenate([position_grad, small_grad], axis=0)
    rest = jnp.pad(rest, ((0, width - rest.shape[0]), (0, 0))).T
    pieces += [shards(rest)]
    filled = 8 * rows + g_down.shape[0] // devices + rows
    pad = -filled % 64
    if pad:
        pieces += [jnp.zeros((devices, pad, width), LOW)]
    return jnp.concatenate(pieces, axis=1)


def unpack_grads(packed, rows, span, slots):
    width = packed.shape[1]
    down = packed.shape[1] * 4 * rows // width
    low = 8 * rows

    def part(first):
        return packed[first * rows : (first + 1) * rows]

    rest = packed[low + down : low + down + rows]
    return (
        jnp.concatenate([part(k) for k in range(3)], axis=1),
        part(3),
        jnp.concatenate([part(4 + k) for k in range(4)], axis=1),
        packed[low : low + down],
        rest[:, span : span + slots].T,
        rest[:, :span].T,
    )


def unit_of(cls):
    scale = lax.rsqrt(jnp.sum(cls * cls, axis=-1, keepdims=True) + 1e-06)
    return cls * scale, scale


def on_device(
    tok_ids,
    segments,
    seq_len,
    label_pos,
    label_ids,
    table,
    w_qkv,
    w_out,
    w_up,
    w_down,
    small,
    position,
    t_table,
    t_qkv,
    t_out,
    t_up,
    t_down,
    t_small,
    t_position,
    mom_table,
    mom_qkv,
    mom_out,
    mom_up,
    mom_down,
    mom_small,
    mom_position,
    avg_table,
    avg_qkv,
    avg_out,
    avg_up,
    avg_down,
    avg_small,
    avg_position,
):
    micro, span = tok_ids.shape
    labels = label_pos.shape[1]
    share, width = table.shape
    groups = lax.axis_size("fsdp")
    dp = lax.axis_size("dp")
    devices = groups * dp
    own = lax.axis_index("fsdp")
    padded = (share // 32 + 1) * 32
    pad = padded - share
    rows_own = w_qkv.shape[0]
    slots = small.shape[0]

    info = jnp.concatenate(
        [tok_ids, label_ids, jnp.broadcast_to(seq_len[:, None], (micro, labels))], axis=1
    )
    info = jnp.pad(info, ((0, -micro % 8), (0, 0)))
    student_table, info = spread_dp(
        [jnp.pad(table.astype(LOW), ((0, pad), (0, 0)))], dp, 1, info, groups
    )
    info = info[:, :micro].reshape(groups * micro, span + 2 * labels)
    ids_all = info[:, :span]
    targets_all = info[:, span : span + labels].reshape(-1)
    lengths_all = info[:, span + labels]
    valid_local = label_valid(seq_len, labels, span)
    counts = jnp.stack([jnp.sum(valid_local), jnp.sum((seq_len > 0).astype(jnp.float32))])
    extra = jnp.broadcast_to(counts.astype(LOW)[None, :], (rows_own, 2))

    safe_ids = owned(ids_all, share, padded, groups, own)[1]
    packed_teacher = pack_rows(
        (t_qkv, t_out, t_up, t_down, pack_rest(t_small, t_position, None, width)), width
    )
    packed_teacher = lax.all_gather(packed_teacher, BOTH)
    safe_flat = safe_ids.reshape(-1)
    student_hits = student_table[safe_flat].reshape(groups * micro, span, width)
    student_hits, t_table = lax.optimization_barrier((student_hits, t_table))
    teacher_table = spread_dp([jnp.pad(t_table, ((0, pad), (0, 0)))], dp, 2)[0]
    tokens_student = lax.psum_scatter(
        student_hits,
        "fsdp",
        scatter_dimension=0,
        tiled=True,
    ).astype(jnp.float32)
    teacher_hits = teacher_table[safe_flat].reshape(groups * micro, span, width)
    s_weights, teacher_hits, packed_teacher = lax.optimization_barrier(
        ((w_qkv, w_out, w_up, w_down, small, position), teacher_hits, packed_teacher)
    )
    tokens_teacher = lax.psum_scatter(teacher_hits, "fsdp", scatter_dimension=0, tiled=True)
    packed_student = pack_rows(
        s_weights[:2] + (pack_rest(s_weights[4], s_weights[5], extra, width),), width
    )
    packed_student, up_student, down_student = gather_weights(
        [packed_student, pack_rows((s_weights[2],), width), pack_rows((s_weights[3],), width)],
        dp,
        groups,
        5,
    )
    layout = (
        (rows_own, 3),
        (rows_own, 1),
        (rows_own, 4),
        (w_down.shape[0], 1),
        (rows_own, 1),
    )
    full_qkv, full_out, rest = unpack_rows(packed_student, layout[:2] + layout[4:])
    full_small, full_position, rest = unpack_rest(rest, span, slots)
    full_up = unpack_rows(up_student, layout[2:3])[0]
    full_down = down_student[:, : w_down.shape[0]].reshape(-1, width)
    weights = (full_qkv, full_out, full_up, full_down, full_small, full_position)
    counted = jnp.sum(rest[::rows_own, :2].astype(jnp.float32), axis=0)
    label_count, count_seq = counted[0], counted[1]

    tables = (student_table, teacher_table)
    vocab_rows = student_table.shape[0]
    start, normed_start, inverse_start = embed_forward(tokens_student, weights, segments)
    student_out, kept = layer_forward(start, weights, seq_len)
    pick = (label_pos[..., None] == jnp.arange(span)).astype(LOW)
    student_rows = label_rows(pick, student_out)
    student_rows, packed_teacher = lax.optimization_barrier((student_rows, packed_teacher))
    *teacher, teacher_rest = unpack_rows(packed_teacher, layout)
    teacher = tuple(teacher) + unpack_rest(teacher_rest, span, slots)[:2]
    student_rows, teacher, tokens_teacher = lax.optimization_barrier(
        (student_rows, teacher, tokens_teacher)
    )
    student_rows = lax.all_gather(student_rows, "fsdp", axis=0, tiled=True)
    teacher_start = embed_forward(tokens_teacher.astype(jnp.float32), teacher, segments)[0]
    teacher_out = layer_forward(teacher_start, teacher, seq_len)[0]
    teacher_rows = label_rows(pick, teacher_out)
    teacher_rows = lax.all_gather(teacher_rows, "fsdp", axis=0, tiled=True)
    valid_group = label_valid(lengths_all, labels, span).reshape(-1)
    d_out, table_grad, label_loss = label_head(
        student_rows,
        teacher_rows,
        pick,
        tables,
        targets_all,
        valid_group,
        own,
        share,
        padded,
        groups,
        label_count,
    )
    cls_student = student_out[:, 0]
    unit_student, scale_student = unit_of(cls_student)
    unit_teacher = unit_of(teacher_out[:, 0])[0]
    weight_pkd = (PKD_WEIGHT * (seq_len > 0).astype(jnp.float32) / count_seq)[:, None]
    gap = unit_student - unit_teacher
    d_unit = 2.0 * weight_pkd * gap
    d_cls = scale_student * d_unit - cls_student * scale_student**3 * jnp.sum(
        cls_student * d_unit, axis=-1, keepdims=True
    )
    first_row = (jnp.arange(span) == 0).astype(jnp.float32)[None, :, None]
    d_out = d_out + first_row * d_cls[:, None, :]
    loss_part = label_loss + jnp.sum(weight_pkd * gap * gap)

    factors, rows_grad, d_start = layer_backward(d_out, weights, kept, seq_len)
    d_embed, gain_embed, shift_embed = layer_norm_back(
        d_start, normed_start, inverse_start, weights[4][12]
    )
    zero_segment = (segments == 0).astype(jnp.float32)[..., None]
    small_grad = jnp.concatenate(
        [
            rows_grad,
            gain_embed[None],
            shift_embed[None],
            jnp.sum(d_embed * zero_segment, axis=(0, 1))[None],
            jnp.sum(d_embed * (1.0 - zero_segment), axis=(0, 1))[None],
        ]
    )
    position_grad = jnp.sum(d_embed, axis=0)
    d_embed_low, factors = lax.optimization_barrier((d_embed.astype(LOW), factors))
    embed_grads = lax.all_gather(d_embed_low, "fsdp", axis=0, tiled=True)
    matrices = [
        product_of("bsd,bsf->df", left, right) for left, right in factors
    ]
    packed_grads = pack_grads(*matrices, small_grad, position_grad, devices)
    packed_grads = reduce_weights(packed_grads, dp, groups, 2, 6)
    layer_squares = jnp.sum(packed_grads * packed_grads)
    table_grad, embed_grads, packed_grads, layer_squares = lax.optimization_barrier(
        (table_grad, embed_grads, packed_grads, layer_squares)
    )
    table_shard, table_squares = fold_dp(
        safe_flat, embed_grads.reshape(-1, width), table_grad, dp, share, 2048, 3
    )
    table_shard = table_shard[:share]
    grads = (table_shard,) + unpack_grads(packed_grads, rows_own, span, slots)
    squares = layer_squares + jnp.sum(table_squares)
    column = jnp.arange(128)[None, :]
    sums = jnp.where(column == 0, squares, jnp.where(column == 1, loss_part, 0.0))
    sums = total_all(jnp.broadcast_to(sums, (8, 128)), dp, groups, 4)
    total_sq, loss_value = sums[0, 0], sums[0, 1]
    grad_norm = jnp.sqrt(total_sq)
    factor = CLIP / jnp.maximum(grad_norm, CLIP)
    rate = RATE_SCALE * math.sqrt(NPARAM)
    params = (table, w_qkv, w_out, w_up, w_down, small, position)
    moms = (mom_table, mom_qkv, mom_out, mom_up, mom_down, mom_small, mom_position)
    avgs = (avg_table, avg_qkv, avg_out, avg_up, avg_down, avg_small, avg_position)
    news, moments, averages = ([], [], [])
    for weight, grad, momentum, average in zip(params, grads, moms, avgs):
        clipped = grad * factor
        moment = MOMENTUM * momentum + clipped
        fresh = weight - rate * (clipped + MOMENTUM * moment)
        news.append(fresh)
        moments.append(moment)
        averages.append(AVERAGE * average + (1.0 - AVERAGE) * fresh)
    return tuple(news) + tuple(moments) + tuple(averages) + (grad_norm, loss_value)


def solution(mesh):
    placed = (
        P(("dp", "fsdp"), None),
        P(("dp", "fsdp"), None),
        P(("dp", "fsdp")),
        P(("dp", "fsdp"), None),
        P(("dp", "fsdp"), None),
        P(("dp", "fsdp"), None),
        P(("dp", "fsdp"), None),
        P(("dp", "fsdp"), None),
        P(("dp", "fsdp"), None),
        P(("dp", "fsdp"), None),
        P(None, ("dp", "fsdp")),
        P(None, ("dp", "fsdp")),
        P(("dp", "fsdp"), None),
        P(("dp", "fsdp"), None),
        P(("dp", "fsdp"), None),
        P(("dp", "fsdp"), None),
        P(("dp", "fsdp"), None),
        P(None, ("dp", "fsdp")),
        P(None, ("dp", "fsdp")),
        P(("dp", "fsdp"), None),
        P(("dp", "fsdp"), None),
        P(("dp", "fsdp"), None),
        P(("dp", "fsdp"), None),
        P(("dp", "fsdp"), None),
        P(None, ("dp", "fsdp")),
        P(None, ("dp", "fsdp")),
        P(("dp", "fsdp"), None),
        P(("dp", "fsdp"), None),
        P(("dp", "fsdp"), None),
        P(("dp", "fsdp"), None),
        P(("dp", "fsdp"), None),
        P(None, ("dp", "fsdp")),
        P(None, ("dp", "fsdp")),
    )
    return jax.shard_map(
        on_device,
        mesh=mesh,
        in_specs=placed,
        out_specs=(
            P(("dp", "fsdp"), None),
            P(("dp", "fsdp"), None),
            P(("dp", "fsdp"), None),
            P(("dp", "fsdp"), None),
            P(("dp", "fsdp"), None),
            P(None, ("dp", "fsdp")),
            P(None, ("dp", "fsdp")),
            P(("dp", "fsdp"), None),
            P(("dp", "fsdp"), None),
            P(("dp", "fsdp"), None),
            P(("dp", "fsdp"), None),
            P(("dp", "fsdp"), None),
            P(None, ("dp", "fsdp")),
            P(None, ("dp", "fsdp")),
            P(("dp", "fsdp"), None),
            P(("dp", "fsdp"), None),
            P(("dp", "fsdp"), None),
            P(("dp", "fsdp"), None),
            P(("dp", "fsdp"), None),
            P(None, ("dp", "fsdp")),
            P(None, ("dp", "fsdp")),
            P(),
            P(),
        ),
        check_vma=False,
    )
```

```python
import functools
import math

import jax
import jax.numpy as jnp
from jax import lax
from jax.experimental import pallas as pl
from jax.experimental.pallas import tpu as pltpu
from jax.sharding import PartitionSpec as P

HD = 64
NPARAM = 30978048


SOFTMAX_HEAT = 2.0
SOFT_FRACTION = 0.5
PKD_WEIGHT = 10.0
MOMENTUM = 0.9
AVERAGE = 0.75
CLIP = 0.002
RATE_SCALE = 20.0
EPSILON = 1e-12
NEGATIVE = -1e30
BOTH = ("dp", "fsdp")
LOW = jnp.bfloat16
MIB = 1 << 20
CHUNK = 512


def push(src, dst, send, recv, where):
    copy = pltpu.make_async_remote_copy(
        src_ref=src,
        dst_ref=dst,
        send_sem=send,
        recv_sem=recv,
        device_id=where,
        device_id_type=pl.DeviceIdType.MESH,
    )
    copy.start()
    return copy


def greet(peers):
    barrier = pltpu.get_barrier_semaphore()
    for peer in peers:
        pl.semaphore_signal(barrier, inc=1, device_id=peer, device_id_type=pl.DeviceIdType.MESH)
    pl.semaphore_wait(barrier, len(peers))


def flipped(index, bit):
    return index + bit - 2 * bit * (lax.div(index, bit) % 2)


def spread_body(dp, count, groups, *refs):
    blocks, outs = refs[:count], refs[count : 2 * count]
    local, send, recv = refs[2 * count : 2 * count + 3]
    extra = refs[2 * count + 3 :]
    shared = []
    friends = []
    if groups:
        spot = lax.axis_index("fsdp")
        friends = [{"fsdp": lax.rem(spot + hop, groups)} for hop in range(1, groups)]

    def share_info():
        if groups:
            note, notes, note_send, note_recv = extra
            for hop, friend in enumerate(friends):
                shared.append(
                    push(note, notes.at[spot], note_send.at[hop], note_recv.at[hop], friend)
                )
            notes[spot] = note[...]

    me = lax.axis_index("dp")
    own = [pltpu.make_async_copy(blocks[k], outs[k].at[me], local.at[k]) for k in range(count)]
    for copy in own:
        copy.start()
    if dp == 4:
        near = [flipped(me, 1), flipped(me, 2)]
        greet([{"dp": near[0]}, {"dp": near[1]}] + friends)
        share_info()
        first = []
        for k in range(count):
            for step in range(2):
                for link in range(2):
                    half = step if link == 0 else 1 - step
                    first.append(
                        push(
                            blocks[k].at[half],
                            outs[k].at[me, half],
                            send.at[k, link, half],
                            recv.at[k, link, half],
                            {"dp": near[link]},
                        )
                    )
        for k in range(count):
            for link in range(2):
                first[k * 4 + link].wait_recv()
                origin = near[link]
                other = 1 - link
                first.append(
                    push(
                        outs[k].at[origin, link],
                        outs[k].at[origin, link],
                        send.at[k, 2, other],
                        recv.at[k, 2, other],
                        {"dp": near[other]},
                    )
                )
        for place, copy in enumerate(first):
            if place >= 4 * count or place % 4 >= 2:
                copy.wait_recv()
        for copy in first:
            copy.wait_send()
    else:
        peers = [lax.rem(me + hop, dp) for hop in range(1, dp)]
        greet([{"dp": peer} for peer in peers] + friends)
        share_info()
        sent = []
        for k in range(count):
            for hop, peer in enumerate(peers):
                sent.append(
                    push(
                        blocks[k],
                        outs[k].at[me],
                        send.at[k, hop, 0],
                        recv.at[k, hop, 0],
                        {"dp": peer},
                    )
                )
        for copy in sent:
            copy.wait()
    for copy in own:
        copy.wait()
    for copy in shared:
        copy.wait()


def spread_dp(blocks, dp, identity, info=None, groups=0):
    count = len(blocks)
    rows, width = blocks[0].shape
    cut = [block.reshape(2, rows // 2, width) for block in blocks]
    anywhere = pl.BlockSpec(memory_space=pl.ANY)
    vmem = pl.BlockSpec(memory_space=pltpu.VMEM)
    dma = pltpu.SemaphoreType.DMA
    out_shape = [jax.ShapeDtypeStruct((dp, 2, rows // 2, width), LOW)] * count
    in_specs, out_specs = [anywhere] * count, [anywhere] * count
    scratch = [
        dma((count,)),
        dma((count, max(3, dp - 1), 2)),
        dma((count, max(3, dp - 1), 2)),
    ]
    body = functools.partial(spread_body, dp, count, 0)
    if info is not None:
        cut.append(info)
        in_specs.append(vmem)
        out_shape.append(jax.ShapeDtypeStruct((groups,) + info.shape, info.dtype))
        out_specs.append(vmem)
        scratch += [dma((groups - 1,)), dma((groups - 1,))]

        def body(*refs):
            size = count + 1
            ins, outs, rest = refs[:size], refs[size : 2 * size], refs[2 * size :]
            spread_body(
                dp,
                count,
                groups,
                *ins[:count],
                *outs[:count],
                *rest[:3],
                ins[count],
                outs[count],
                *rest[3:],
            )

    outs = pl.pallas_call(
        body,
        out_shape=out_shape,
        in_specs=in_specs,
        out_specs=out_specs,
        scratch_shapes=scratch,
        compiler_params=pltpu.CompilerParams(collective_id=identity, has_side_effects=True),
        name="spread_tables",
    )(*cut)
    return [out.reshape(dp * rows, width) for out in outs[:count]] + list(outs[count:])


def ways_of(me, dp):
    if dp == 4:
        return [flipped(me, 1), flipped(me, 2)]
    return [lax.rem(me + hop, dp) for hop in range(1, dp)]


def sources_of(me, dp):
    if dp == 4:
        return [flipped(me, 1), flipped(me, 2)]
    return [lax.rem(me + dp - hop, dp) for hop in range(1, dp)]


def gather_body(dp, n, count, *refs):
    blocks, outs = refs[:count], refs[count : 2 * count]
    local, z_send, z_recv, way_send, way_recv, far_send, far_recv, core_send, core_recv = refs[
        2 * count :
    ]
    me = lax.axis_index("fsdp")
    row = lax.axis_index("dp")
    p = lax.div(me, 2)
    c = lax.rem(me, 2)
    partner = me + 1 - 2 * c
    ways = ways_of(row, dp)
    sources = sources_of(row, dp)
    barrier = pltpu.get_barrier_semaphore()

    def hello(where):
        pl.semaphore_signal(barrier, inc=1, device_id=where, device_id_type=pl.DeviceIdType.MESH)

    hello({"fsdp": partner})
    for way in ways:
        hello({"dp": way})

    @pl.when(p > 0)
    def _():
        hello({"fsdp": me - 2})

    @pl.when(p < n - 1)
    def _():
        hello({"fsdp": me + 2})

    @pl.when((p > 0) & (p < n - 1))
    def _():
        pl.semaphore_wait(barrier, 3 + len(ways))

    @pl.when((p == 0) | (p == n - 1))
    def _():
        pl.semaphore_wait(barrier, 2 + len(ways))

    def remote(src, dst, send, recv, where):
        return pltpu.make_async_remote_copy(
            src_ref=src,
            dst_ref=dst,
            send_sem=send,
            recv_sem=recv,
            device_id=where,
            device_id_type=pl.DeviceIdType.MESH,
        )

    def line(m, q, side):
        shard = outs[m].at[row, 2 * q + c]
        where = {"fsdp": me + 2 - 4 * side}
        return remote(shard, shard, z_send.at[m, side, q], z_recv.at[m, q], where)

    def way_copy(m, w, half, q):
        shard = outs[m].at[row, 2 * q + c, half]
        return remote(
            shard, shard, way_send.at[m, w, half, q], way_recv.at[m, w, half, q], {"dp": ways[w]}
        )

    def far_copy(m, w, q):
        shard = outs[m].at[sources[w], 2 * q + c, w]
        return remote(
            shard, shard, far_send.at[m, w, q], far_recv.at[m, w, q], {"dp": ways[1 - w]}
        )

    def core_copy(m, j, q, half):
        shard = outs[m].at[j, 2 * q + c, half]
        return remote(
            shard,
            shard,
            core_send.at[m, j, q, half],
            core_recv.at[m, j, q, half],
            {"fsdp": partner},
        )

    def onward(m, q):
        for half in range(2):
            for w in range(len(ways)):
                way_copy(m, w, half if w == 0 else 1 - half, q).start()
        for half in range(2):
            core_copy(m, row, q, half).start()

    def landed(m, q):
        for half in range(2):
            for w in range(len(ways)):
                part = half if w == 0 else 1 - half
                way_copy(m, w, part, q).wait_recv()
                if dp == 4 and part == w:
                    far_copy(m, w, q).start()
                core_copy(m, sources[w], q, part).start()

    def far_landed(m, q):
        if dp == 4:
            for w in range(2):
                far_copy(m, w, q).wait_recv()
                core_copy(m, dp - 1 - row, q, w).start()

    def each(distance, act):
        if distance == 0:
            act(p)
            return

        @pl.when(p >= distance)
        def _():
            act(p - distance)

        @pl.when(p + distance < n)
        def _():
            act(p + distance)

    for m in range(count):
        copy = pltpu.make_async_copy(blocks[m], outs[m].at[row, me], local.at[m])
        copy.start()
        copy.wait()

        @pl.when(p < n - 1)
        def _():
            line(m, p, 0).start()

        @pl.when(p > 0)
        def _():
            line(m, p, 1).start()

        onward(m, p)
    for distance in range(1, n + 2):
        for m in range(count):
            if distance < n:

                @pl.when(p >= distance)
                def _():
                    line(m, p - distance, 0).wait_recv()

                    @pl.when(p < n - 1)
                    def _():
                        line(m, p - distance, 0).start()

                    onward(m, p - distance)

                @pl.when(p + distance < n)
                def _():
                    line(m, p + distance, 1).wait_recv()

                    @pl.when(p > 0)
                    def _():
                        line(m, p + distance, 1).start()

                    onward(m, p + distance)

            if distance <= n:
                each(distance - 1, functools.partial(landed, m))
            if distance >= 2:
                each(distance - 2, functools.partial(far_landed, m))

    def settle(q, carry):
        for m in range(count):

            @pl.when((q <= p) & (p < n - 1))
            def _():
                line(m, q, 0).wait_send()

            @pl.when((q >= p) & (p > 0))
            def _():
                line(m, q, 1).wait_send()

            for half in range(2):
                for w in range(len(ways)):
                    way_copy(m, w, half, q).wait_send()
                if dp == 4:
                    far_copy(m, half, q).wait_send()
                for j in range(dp):
                    core_copy(m, j, q, half).wait()
        return carry

    lax.fori_loop(0, n, settle, 0)


def gather_weights(blocks, dp, groups, identity):
    count = len(blocks)
    width = blocks[0].shape[1]
    n = groups // 2
    cut = [block.reshape(2, block.shape[0] // 2, width) for block in blocks]
    ways = 2 if dp == 4 else dp - 1
    dma = pltpu.SemaphoreType.DMA
    outs = pl.pallas_call(
        functools.partial(gather_body, dp, n, count),
        out_shape=[jax.ShapeDtypeStruct((dp, groups) + block.shape, LOW) for block in cut],
        in_specs=[pl.BlockSpec(memory_space=pl.ANY)] * count,
        out_specs=[pl.BlockSpec(memory_space=pl.ANY)] * count,
        scratch_shapes=[
            dma((count,)),
            dma((count, 2, n)),
            dma((count, n)),
            dma((count, ways, 2, n)),
            dma((count, ways, 2, n)),
            dma((count, 2, n)),
            dma((count, 2, n)),
            dma((count, dp, n, 2)),
            dma((count, dp, n, 2)),
        ],
        compiler_params=pltpu.CompilerParams(collective_id=identity, has_side_effects=True),
        name="gather_weights",
    )(*cut)
    return [out.reshape(dp * groups, -1, width) for out in outs]


def dot_over(left, right, left_dim, right_dim):
    return lax.dot_general(
        left, right, (((left_dim,), (right_dim,)), ((), ())), preferred_element_type=jnp.float32
    )


def added(*values):
    total = values[0].astype(jnp.float32)
    for value in values[1:]:
        total = total + value.astype(jnp.float32)
    return total


def reduce_body(dp, n, pieces, g, out, core, far, near, last, right, left, core_sem, far_sem,
                near_sem, last_sem, line_sem):
    me = lax.axis_index("fsdp")
    row = lax.axis_index("dp")
    p = lax.div(me, 2)
    c = lax.rem(me, 2)
    partner = me + 1 - 2 * c
    ways = ways_of(row, dp)
    opposite = dp - 1 - row
    barrier = pltpu.get_barrier_semaphore()
    order = []
    for k in range((n + 1) // 2):
        order += [n - 1 - k] + ([k] if k != n - 1 - k else [])
    turns = [(i, q) for i in range(pieces) for q in order]

    def hello(where):
        pl.semaphore_signal(barrier, inc=1, device_id=where, device_id_type=pl.DeviceIdType.MESH)

    hello({"fsdp": partner})
    for way in ways:
        hello({"dp": way})

    @pl.when(p > 0)
    def _():
        hello({"fsdp": me - 2})

    @pl.when(p < n - 1)
    def _():
        hello({"fsdp": me + 2})

    @pl.when((p > 0) & (p < n - 1))
    def _():
        pl.semaphore_wait(barrier, 3 + len(ways))

    @pl.when((p == 0) | (p == n - 1))
    def _():
        pl.semaphore_wait(barrier, 2 + len(ways))

    def remote(src, dst, sems, index, where):
        return pltpu.make_async_remote_copy(
            src_ref=src,
            dst_ref=dst,
            send_sem=sems.at[(0,) + index],
            recv_sem=sems.at[(1,) + index],
            device_id=where,
            device_id_type=pl.DeviceIdType.MESH,
        )

    def core_copy(j, q, i, half):
        return remote(
            g.at[j, 2 * q + 1 - c, i, half],
            core.at[j, q, i, half],
            core_sem,
            (j, q, i, half),
            {"fsdp": partner},
        )

    def far_copy(q, i, w):
        return remote(
            core.at[opposite, q, i, w], far.at[q, i, w], far_sem, (q, i, w), {"dp": ways[w]}
        )

    def near_copy(q, i, w):
        return remote(
            core.at[ways[w], q, i, w], near.at[q, i, w], near_sem, (q, i, w, 0), {"dp": ways[w]}
        )

    def last_copy(q, i, w):
        return remote(
            far.at[q, i, w], last.at[q, i, w], last_sem, (q, i, w), {"dp": ways[1 - w]}
        )

    def direct_copy(hop, q, i, half):
        return remote(
            core.at[ways[hop], q, i, half],
            near.at[hop, q, i, half],
            near_sem,
            (q, i, half, hop),
            {"dp": ways[hop]},
        )

    def line_copy(buffer, q, i, side):
        return remote(
            buffer.at[q, i], buffer.at[q, i], line_sem, (q, i, side), {"fsdp": me + 2 - 4 * side}
        )

    for i, q in turns:
        for j in [opposite, *ways, row] if dp == 4 else range(dp):
            for half in range(2):
                core_copy(j, q, i, half).start()

    def pair(j, q, i, half):
        core_copy(j, q, i, half).wait_recv()
        core[j, q, i, half] = added(core[j, q, i, half], g[j, 2 * q + c, i, half]).astype(LOW)

    for i, q in turns:
        if dp == 4:
            for w in range(2):
                pair(opposite, q, i, w)
                far_copy(q, i, w).start()
            for w in range(2):
                pair(ways[w], q, i, w)
                near_copy(q, i, w).start()
            for w in range(2):
                pair(ways[w], q, i, 1 - w)
                pair(row, q, i, w)
        else:
            for half in range(2):
                for j in range(dp):
                    pair(j, q, i, half)
                for hop in range(dp - 1):
                    direct_copy(hop, q, i, half).start()

    def relay(i, q):
        if dp == 4:
            for w in range(2):
                far_copy(q, i, w).wait_recv()
                far[q, i, w] = added(far[q, i, w], core[ways[1 - w], q, i, w]).astype(LOW)
                last_copy(q, i, w).start()

    def total(q, i, half):
        if dp == 4:
            near_copy(q, i, half).wait_recv()
            last_copy(q, i, half).wait_recv()
            return added(core[row, q, i, half], near[q, i, half], last[q, i, half])
        parts = [core[row, q, i, half]]
        for hop in range(dp - 1):
            direct_copy(hop, q, i, half).wait_recv()
            parts.append(near[hop, q, i, half])
        return added(*parts)

    def line_up(i, q):
        sums = [total(q, i, half) for half in range(2)]

        def store(buffer, side, first):
            for half in range(2):
                if first:
                    buffer[q, i, half] = sums[half].astype(LOW)
                else:
                    buffer[q, i, half] = added(sums[half], buffer[q, i, half]).astype(LOW)
            line_copy(buffer, q, i, side).start()

        if q > 0:

            @pl.when((p > 0) & (p < q))
            def _():
                line_copy(right, q, i, 0).wait_recv()
                store(right, 0, False)

            @pl.when((p == 0) & (p < q))
            def _():
                store(right, 0, True)

        if q < n - 1:

            @pl.when((p < n - 1) & (p > q))
            def _():
                line_copy(left, q, i, 1).wait_recv()
                store(left, 1, False)

            @pl.when((p == n - 1) & (p > q))
            def _():
                store(left, 1, True)

        @pl.when(p == q)
        def _():
            for half in range(2):
                out[i, half] = sums[half]

    for k in range(len(turns) + n):
        if k < len(turns):
            relay(*turns[k])
        if k >= n:
            line_up(*turns[k - n])

    @pl.when(p > 0)
    def _():
        for i in range(pieces):
            line_copy(right, p, i, 0).wait_recv()
            out[i] = added(out[i], right[p, i])

    @pl.when(p < n - 1)
    def _():
        for i in range(pieces):
            line_copy(left, p, i, 1).wait_recv()
            out[i] = added(out[i], left[p, i])

    for i, q in turns:
        for half in range(2):
            for j in range(dp):
                core_copy(j, q, i, half).wait_send()
            if dp == 4:
                far_copy(q, i, half).wait_send()
                near_copy(q, i, half).wait_send()
                last_copy(q, i, half).wait_send()
            else:
                for hop in range(dp - 1):
                    direct_copy(hop, q, i, half).wait_send()

        @pl.when(p < q)
        def _():
            line_copy(right, q, i, 0).wait_send()

        @pl.when(p > q)
        def _():
            line_copy(left, q, i, 1).wait_send()


def reduce_weights(g, dp, groups, pieces, identity):
    devices, rows, width = g.shape
    n = groups // 2
    half = rows // (2 * pieces)
    g = g.reshape(dp, groups, pieces, 2, half, width)
    dma = pltpu.SemaphoreType.DMA
    block = pltpu.VMEM((n, pieces, 2, half, width), LOW)
    near = block if dp == 4 else pltpu.VMEM((dp - 1, n, pieces, 2, half, width), LOW)
    out = pl.pallas_call(
        functools.partial(reduce_body, dp, n, pieces),
        out_shape=jax.ShapeDtypeStruct((pieces, 2, half, width), jnp.float32),
        in_specs=[pl.BlockSpec(memory_space=pltpu.VMEM)],
        out_specs=pl.BlockSpec(memory_space=pltpu.VMEM),
        scratch_shapes=[
            pltpu.VMEM((dp, n, pieces, 2, half, width), LOW),
            block,
            near,
            block,
            block,
            block,
            dma((2, dp, n, pieces, 2)),
            dma((2, n, pieces, 2)),
            dma((2, n, pieces, 2, max(1, dp - 1))),
            dma((2, n, pieces, 2)),
            dma((2, n, pieces, 2)),
        ],
        compiler_params=pltpu.CompilerParams(
            collective_id=identity, has_side_effects=True, vmem_limit_bytes=56 * MIB
        ),
        name="reduce_weights",
    )(g)
    return out.reshape(rows, width)


def fold_body(dp, step, share, ids, rows, base, out, squares, g, near_buffer, far_buffer, last_buffer, sems):
    me = lax.axis_index("dp")
    half_rows = base.shape[2]
    tokens = rows.shape[0]

    def fill(dest, half):
        first = (dest * 2 + half) * half_rows
        vocab = lax.broadcasted_iota(jnp.int32, (half_rows, step), 0) + first

        def turn(k, total):
            chosen = (vocab == ids[k]).astype(jnp.float32).astype(LOW)
            start = pl.multiple_of(k * step, step)
            return total + dot_over(chosen, rows[pl.ds(start, step), :], 1, 0)

        return lax.fori_loop(0, tokens // step, turn, base[dest, half])

    if dp == 4:
        near = [flipped(me, 1), flipped(me, 2)]
        far = dp - 1 - me
        greet([{"dp": near[0]}, {"dp": near[1]}])

        def send(kind, w, src, dst, way):
            return push(src, dst, sems.at[0, kind, w], sems.at[1, kind, w], {"dp": near[way]})

        first, second, third = [], [], []
        for w in range(2):
            g[far, w] = fill(far, w).astype(LOW)
            first.append(send(0, w, g.at[far, w], far_buffer.at[w], w))
        for w in range(2):
            g[near[w], w] = fill(near[w], w).astype(LOW)
            second.append(send(1, w, g.at[near[w], w], near_buffer.at[w], w))
        for w in range(2):
            part = fill(near[1 - w], w)
            first[w].wait_recv()
            far_buffer[w] = (part + far_buffer[w].astype(jnp.float32)).astype(LOW)
            third.append(send(2, w, far_buffer.at[w], last_buffer.at[w], 1 - w))
        for w in range(2):
            out[w] = fill(me, w)
        for w in range(2):
            second[w].wait_recv()
            third[w].wait_recv()
            out[w] = (
                out[w]
                + near_buffer[w].astype(jnp.float32)
                + last_buffer[w].astype(jnp.float32)
            )
        for copy in first + second + third:
            copy.wait_send()
    else:
        peers = [lax.rem(me + hop, dp) for hop in range(1, dp)]
        greet([{"dp": peer} for peer in peers])
        sent = []
        for hop, peer in enumerate(peers):
            for half in range(2):
                g[peer, half] = fill(peer, half).astype(LOW)
            sent.append(
                push(
                    g.at[peer],
                    near_buffer.at[hop],
                    sems.at[0, hop, 0],
                    sems.at[1, hop, 0],
                    {"dp": peer},
                )
            )
        for half in range(2):
            out[half] = fill(me, half)
        for hop in range(dp - 1):
            sent[hop].wait()
            out[...] = out[...] + near_buffer[hop].astype(jnp.float32)
    total = jnp.zeros((1, out.shape[2]), jnp.float32)
    for half in range(2):
        index = lax.broadcasted_iota(jnp.int32, (half_rows, 1), 0) + half * half_rows
        value = jnp.where(index < share, out[half], 0.0)
        total = total + jnp.sum(value * value, axis=0, keepdims=True)
    squares[...] = total


def fold_dp(ids, rows, base, dp, share, step, identity):
    tokens, width = rows.shape
    padded = base.shape[0] // dp
    half = padded // 2
    block = pltpu.VMEM((2, half, width), LOW)
    first = block if dp == 4 else pltpu.VMEM((dp - 1, 2, half, width), LOW)
    vmem = pl.BlockSpec(memory_space=pltpu.VMEM)
    out, squares = pl.pallas_call(
        functools.partial(fold_body, dp, step, share),
        out_shape=[
            jax.ShapeDtypeStruct((2, half, width), jnp.float32),
            jax.ShapeDtypeStruct((1, width), jnp.float32),
        ],
        in_specs=[vmem, vmem, vmem],
        out_specs=[vmem, vmem],
        scratch_shapes=[
            pltpu.VMEM((dp, 2, half, width), LOW),
            first,
            block,
            block,
            pltpu.SemaphoreType.DMA((2, max(3, dp - 1), 2)),
        ],
        compiler_params=pltpu.CompilerParams(
            collective_id=identity, has_side_effects=True, vmem_limit_bytes=58 * MIB
        ),
        name="fold_table",
    )(ids.reshape(tokens // step, 1, step), rows, base.reshape(dp, 2, half, width))
    return out.reshape(padded, width), squares


def share_body(groups, x, out, send, recv):
    me = lax.axis_index("fsdp")
    peers = [lax.rem(me + hop, groups) for hop in range(1, groups)]
    greet([{"fsdp": peer} for peer in peers])
    sent = []
    for hop, peer in enumerate(peers):
        sent.append(push(x, out.at[me], send.at[hop], recv.at[hop], {"fsdp": peer}))
    out[me] = x[...]
    for copy in sent:
        copy.wait()


def share_small(x, groups, identity):
    return pl.pallas_call(
        functools.partial(share_body, groups),
        out_shape=jax.ShapeDtypeStruct((groups,) + x.shape, x.dtype),
        in_specs=[pl.BlockSpec(memory_space=pltpu.VMEM)],
        out_specs=pl.BlockSpec(memory_space=pltpu.VMEM),
        scratch_shapes=[pltpu.SemaphoreType.DMA((groups - 1,))] * 2,
        compiler_params=pltpu.CompilerParams(collective_id=identity, has_side_effects=True),
        name="share_small",
    )(x)


def total_body(dp, groups, x, out, fsdp_parts, dp_value, dp_parts, send, recv):
    me = lax.axis_index("fsdp")
    row = lax.axis_index("dp")
    peers = [lax.rem(me + hop, groups) for hop in range(1, groups)]
    rows = [lax.rem(row + hop, dp) for hop in range(1, dp)]
    greet([{"fsdp": peer} for peer in peers] + [{"dp": peer} for peer in rows])
    sent = []
    for hop, peer in enumerate(peers):
        sent.append(push(x, fsdp_parts.at[me], send.at[hop], recv.at[hop], {"fsdp": peer}))
    fsdp_parts[me] = x[...]
    for copy in sent:
        copy.wait()
    value = fsdp_parts[0]
    for k in range(1, groups):
        value = value + fsdp_parts[k]
    dp_value[...] = value
    dp_parts[row] = value
    sent = []
    for hop, peer in enumerate(rows):
        place = groups - 1 + hop
        sent.append(
            push(dp_value, dp_parts.at[row], send.at[place], recv.at[place], {"dp": peer})
        )
    for copy in sent:
        copy.wait()
    value = dp_parts[0]
    for k in range(1, dp):
        value = value + dp_parts[k]
    out[...] = value


def total_all(x, dp, groups, identity):
    count = dp + groups - 2
    tile = (8, 128)
    return pl.pallas_call(
        functools.partial(total_body, dp, groups),
        out_shape=jax.ShapeDtypeStruct(tile, jnp.float32),
        in_specs=[pl.BlockSpec(memory_space=pltpu.VMEM)],
        out_specs=pl.BlockSpec(memory_space=pltpu.VMEM),
        scratch_shapes=[
            pltpu.VMEM((groups,) + tile, jnp.float32),
            pltpu.VMEM(tile, jnp.float32),
            pltpu.VMEM((dp,) + tile, jnp.float32),
            pltpu.SemaphoreType.DMA((count,)),
            pltpu.SemaphoreType.DMA((count,)),
        ],
        compiler_params=pltpu.CompilerParams(collective_id=identity, has_side_effects=True),
        name="total",
    )(x)


def block_rows(ref_rows, share):
    block = pl.program_id(0)
    index = lax.broadcasted_iota(jnp.int32, (ref_rows, 1), 0)
    return index + block * ref_rows, index < share


def student_logits_body(share, rows, table, target, logits, stats):
    index, real = block_rows(table.shape[0], share)
    value = jnp.where(real, dot_over(table[...], rows[...], 1, 1), NEGATIVE)
    logits[...] = value
    top = jnp.max(value, axis=0, keepdims=True)
    hit = jnp.sum(jnp.where(index == target[...], value, 0.0), axis=0, keepdims=True)

    @pl.when(pl.program_id(0) == 0)
    def _():
        half = jnp.exp((value - top) / SOFTMAX_HEAT)
        stats[0:1] = top
        stats[1:2] = jnp.sum(half * half, axis=0, keepdims=True)
        stats[2:3] = jnp.sum(half, axis=0, keepdims=True)
        stats[3:4] = hit

    @pl.when(pl.program_id(0) > 0)
    def _():
        before = stats[0:1]
        peak = jnp.maximum(before, top)
        fall = jnp.exp((before - peak) / SOFTMAX_HEAT)
        half = jnp.exp((value - peak) / SOFTMAX_HEAT)
        stats[0:1] = peak
        stats[1:2] = stats[1:2] * fall * fall + jnp.sum(half * half, axis=0, keepdims=True)
        stats[2:3] = stats[2:3] * fall + jnp.sum(half, axis=0, keepdims=True)
        stats[3:4] = stats[3:4] + hit


def teacher_logits_body(share, rows, table, student, logits, stats):
    _, real = block_rows(table.shape[0], share)
    value = jnp.where(real, dot_over(table[...], rows[...], 1, 1), NEGATIVE)
    logits[...] = value
    top = jnp.max(value, axis=0, keepdims=True)
    gap = (value - student[...]) / SOFTMAX_HEAT

    @pl.when(pl.program_id(0) == 0)
    def _():
        exponent = jnp.exp((value - top) / SOFTMAX_HEAT)
        stats[0:1] = top
        stats[1:2] = jnp.sum(exponent, axis=0, keepdims=True)
        stats[2:3] = jnp.sum(exponent * gap, axis=0, keepdims=True)
        stats[3:4] = jnp.zeros_like(top)

    @pl.when(pl.program_id(0) > 0)
    def _():
        before = stats[0:1]
        peak = jnp.maximum(before, top)
        fall = jnp.exp((before - peak) / SOFTMAX_HEAT)
        exponent = jnp.exp((value - peak) / SOFTMAX_HEAT)
        stats[0:1] = peak
        stats[1:2] = stats[1:2] * fall + jnp.sum(exponent, axis=0, keepdims=True)
        stats[2:3] = stats[2:3] * fall + jnp.sum(exponent * gap, axis=0, keepdims=True)


def logits_call(body, rows, table, other, block, name):
    count, width = rows.shape
    vocab = table.shape[0]
    wide = pl.BlockSpec((block, count), lambda v: (v, 0))
    whole = pl.BlockSpec(memory_space=pltpu.VMEM)
    return pl.pallas_call(
        body,
        grid=(vocab // block,),
        in_specs=[
            whole,
            pl.BlockSpec((block, width), lambda v: (v, 0)),
            wide if other.shape[0] == vocab else whole,
        ],
        out_specs=[wide, pl.BlockSpec((4, count), lambda v: (0, 0))],
        out_shape=[
            jax.ShapeDtypeStruct((vocab, count), jnp.float32),
            jax.ShapeDtypeStruct((4, count), jnp.float32),
        ],
        compiler_params=pltpu.CompilerParams(vmem_limit_bytes=40 * MIB),
        cost_estimate=pl.CostEstimate(
            flops=2 * vocab * count * width,
            bytes_accessed=4 * vocab * count + 2 * vocab * width,
            transcendentals=vocab * count,
        ),
        name=name,
    )(rows, table, other)


def logits_back_body(student, teacher, table, consts, target, d_logits, d_rows, total):
    index = lax.broadcasted_iota(jnp.int32, (table.shape[0], 1), 0)
    index = index + pl.program_id(0) * table.shape[0]
    value = student[...]
    hard = jnp.exp(value - consts[0:1]) - (index == target[...]).astype(jnp.float32)
    soft = jnp.exp(value / SOFTMAX_HEAT - consts[1:2]) - jnp.exp(
        teacher[...] / SOFTMAX_HEAT - consts[2:3]
    )
    mixed = consts[3:4] * (
        (1.0 - SOFT_FRACTION) * hard + SOFT_FRACTION * SOFTMAX_HEAT * soft
    )
    low = mixed.astype(LOW)
    d_logits[...] = low
    part = dot_over(low, table[...], 0, 0)

    @pl.when(pl.program_id(0) == 0)
    def _():
        total[...] = part

    @pl.when(pl.program_id(0) > 0)
    def _():
        total[...] += part

    @pl.when(pl.program_id(0) == pl.num_programs(0) - 1)
    def _():
        d_rows[...] = total[...].astype(LOW)


def logits_back(student, teacher, table, consts, target, block):
    vocab, count = student.shape
    width = table.shape[1]
    wide = pl.BlockSpec((block, count), lambda v: (v, 0))
    whole = pl.BlockSpec(memory_space=pltpu.VMEM)
    return pl.pallas_call(
        logits_back_body,
        grid=(vocab // block,),
        in_specs=[wide, wide, pl.BlockSpec((block, width), lambda v: (v, 0)), whole, whole],
        out_specs=[wide, pl.BlockSpec((count, width), lambda v: (0, 0))],
        out_shape=[
            jax.ShapeDtypeStruct((vocab, count), LOW),
            jax.ShapeDtypeStruct((count, width), LOW),
        ],
        scratch_shapes=[pltpu.VMEM((count, width), jnp.float32)],
        compiler_params=pltpu.CompilerParams(vmem_limit_bytes=48 * MIB),
        cost_estimate=pl.CostEstimate(
            flops=2 * vocab * count * width,
            bytes_accessed=10 * vocab * count + 2 * vocab * width,
            transcendentals=3 * vocab * count,
        ),
        name="logits_back",
    )(student, teacher, table, consts, target)


def attend_body(lengths, q_ref, k_ref, v_ref, out_ref):
    live = jnp.maximum(lengths[pl.program_id(0)], 1)
    span = q_ref.shape[1]
    k, v = k_ref[0], v_ref[0]
    keep = lax.broadcasted_iota(jnp.int32, (span, CHUNK), 0) < live
    low_lane = lax.broadcasted_iota(jnp.int32, (CHUNK, 2 * HD), 1) < HD
    for first in range(0, span, CHUNK):
        q = q_ref[0, first : first + CHUNK, :]
        parts = []
        for head in range(2):
            mine = low_lane if head == 0 else jnp.logical_not(low_lane)
            scores = dot_over(k, jnp.where(mine, q * 0.125, jnp.zeros_like(q)), 1, 1)
            scores = jnp.where(keep, scores, NEGATIVE)
            exponent = jnp.exp(scores - jnp.max(scores, axis=0, keepdims=True))
            scale = 1.0 / jnp.sum(exponent, axis=0, keepdims=True)
            parts.append(dot_over((exponent * scale).astype(LOW), v, 0, 0))
        out_ref[0, first : first + CHUNK, :] = jnp.where(low_lane, parts[0], parts[1]).astype(LOW)


def attend(joined, lengths):
    micro, span, wide = joined.shape
    width = wide // 3
    pairs = width // (2 * HD)

    def place(third):
        return pl.BlockSpec((1, span, 2 * HD), lambda b, h, _: (b, 0, third * pairs + h))

    return pl.pallas_call(
        attend_body,
        grid_spec=pltpu.PrefetchScalarGridSpec(
            num_scalar_prefetch=1,
            grid=(micro, pairs),
            in_specs=[place(0), place(1), place(2)],
            out_specs=pl.BlockSpec((1, span, 2 * HD), lambda b, h, _: (b, 0, h)),
        ),
        out_shape=jax.ShapeDtypeStruct((micro, span, width), LOW),
        cost_estimate=pl.CostEstimate(
            flops=4 * micro * span * span * width,
            bytes_accessed=8 * micro * span * width,
            transcendentals=micro * span * span * width // HD,
        ),
        name="attend",
    )(lengths, joined, joined, joined)


def attend_back_body(lengths, q_ref, k_ref, v_ref, d_ref, out_ref, g_keys, g_values):
    live = jnp.maximum(lengths[pl.program_id(0)], 1)
    span = q_ref.shape[1]
    k, v = k_ref[0], v_ref[0]
    keep = lax.broadcasted_iota(jnp.int32, (span, CHUNK), 0) < live
    low_lane = lax.broadcasted_iota(jnp.int32, (CHUNK, 2 * HD), 1) < HD
    low_wide = lax.broadcasted_iota(jnp.int32, (span, 2 * HD), 1) < HD
    for first in range(0, span, CHUNK):
        q = q_ref[0, first : first + CHUNK, :]
        d = d_ref[0, first : first + CHUNK, :]
        parts = []
        for head in range(2):
            mine = low_lane if head == 0 else jnp.logical_not(low_lane)
            scores = dot_over(k, jnp.where(mine, q * 0.125, jnp.zeros_like(q)), 1, 1)
            scores = jnp.where(keep, scores, NEGATIVE)
            exponent = jnp.exp(scores - jnp.max(scores, axis=0, keepdims=True))
            probs = exponent * (1.0 / jnp.sum(exponent, axis=0, keepdims=True))
            d_probs = dot_over(v, jnp.where(mine, d, jnp.zeros_like(d)), 1, 1)
            inner = jnp.sum(probs * d_probs, axis=0, keepdims=True)
            d_scores = (probs * (d_probs - inner)).astype(LOW)
            value_part = dot_over(probs.astype(LOW), d, 1, 0)
            key_part = dot_over(d_scores, q, 1, 0)
            if first == 0:
                g_values[head] = value_part
                g_keys[head] = key_part
            else:
                g_values[head] += value_part
                g_keys[head] += key_part
            parts.append(dot_over(d_scores, k, 0, 0))
        out_ref[0, 0, first : first + CHUNK, :] = (
            jnp.where(low_lane, parts[0], parts[1]) * 0.125
        ).astype(LOW)
    out_ref[1, 0] = (jnp.where(low_wide, g_keys[0], g_keys[1]) * 0.125).astype(LOW)
    out_ref[2, 0] = jnp.where(low_wide, g_values[0], g_values[1]).astype(LOW)


def attend_back(joined, d_context, lengths):
    micro, span, width = d_context.shape
    pairs = width // (2 * HD)

    def place(third):
        return pl.BlockSpec((1, span, 2 * HD), lambda b, h, _: (b, 0, third * pairs + h))

    return pl.pallas_call(
        attend_back_body,
        grid_spec=pltpu.PrefetchScalarGridSpec(
            num_scalar_prefetch=1,
            grid=(micro, pairs),
            in_specs=[place(0), place(1), place(2), place(0)],
            out_specs=pl.BlockSpec((3, 1, span, 2 * HD), lambda b, h, _: (0, b, 0, h)),
            scratch_shapes=[
                pltpu.VMEM((2, span, 2 * HD), jnp.float32),
                pltpu.VMEM((2, span, 2 * HD), jnp.float32),
            ],
        ),
        out_shape=jax.ShapeDtypeStruct((3, micro, span, width), LOW),
        cost_estimate=pl.CostEstimate(
            flops=10 * micro * span * span * width,
            bytes_accessed=14 * micro * span * width,
            transcendentals=micro * span * span * width // HD,
        ),
        name="attend_back",
    )(lengths, joined, joined, joined, d_context)


def product_of(form, left, right):
    return jnp.einsum(form, left, right, preferred_element_type=jnp.float32)


def owned(ids, share, padded, groups, own):
    block = ids // share
    inside = block % groups == own
    local = block // groups * padded + ids % share
    return (inside, jnp.where(inside, local, share))


def layer_norm_keep(value, gain, shift):
    mean = jnp.mean(value, axis=-1, keepdims=True)
    centred = value - mean
    inverse = lax.rsqrt(jnp.mean(centred * centred, axis=-1, keepdims=True) + EPSILON)
    normed = centred * inverse
    return (normed * gain + shift, normed, inverse)


def layer_norm_back(grad, normed, inverse, gain):
    axes = tuple(range(grad.ndim - 1))
    gain_grad = jnp.sum(grad * normed, axis=axes)
    shift_grad = jnp.sum(grad, axis=axes)
    scaled = grad * gain
    centred = scaled - jnp.mean(scaled, axis=-1, keepdims=True)
    return (
        inverse * (centred - normed * jnp.mean(scaled * normed, axis=-1, keepdims=True)),
        gain_grad,
        shift_grad,
    )


def gelu_parts(upward):
    normal_cdf = 0.5 * (1.0 + lax.erf(upward * 0.7071067811865476))
    density = jnp.exp(-0.5 * upward * upward) * 0.3989422804014327
    return (upward * normal_cdf, normal_cdf + upward * density)


def label_valid(lengths, labels, span):
    needed = (lengths * labels + span - 1) // span
    return (jnp.arange(labels)[None, :] < needed[:, None]).astype(jnp.float32)


def pack_body(*refs):
    out = refs[-1]
    width = out.shape[1]
    first = 0
    for ref in refs[:-1]:
        rows = ref.shape[0]
        for k in range(ref.shape[1] // width):
            piece = ref[:, k * width : (k + 1) * width]
            out[first : first + rows, :] = piece.astype(LOW)
            first += rows
    if first < out.shape[0]:
        out[first:, :] = jnp.zeros((out.shape[0] - first, width), LOW)


def pack_rows(arrays, width):
    filled = sum(array.size // width for array in arrays)
    padded = filled + -filled % 32
    if any(array.shape[0] % 16 for array in arrays) and arrays[0].shape[0] % 8:
        pieces = []
        for array in arrays:
            for k in range(array.shape[1] // width):
                pieces.append(array[:, k * width : (k + 1) * width].astype(LOW))
        return jnp.pad(jnp.concatenate(pieces, axis=0), ((0, padded - filled), (0, 0)))
    vmem = pl.BlockSpec(memory_space=pltpu.VMEM)
    return pl.pallas_call(
        pack_body,
        in_specs=[vmem] * len(arrays),
        out_specs=vmem,
        out_shape=jax.ShapeDtypeStruct((padded, width), LOW),
        name="pack_rows",
    )(*arrays)


def pack_rest(small, position, extra, width):
    rest = [position.astype(LOW).T, small.astype(LOW).T]
    rest = jnp.concatenate(rest + ([] if extra is None else [extra]), axis=1)
    return jnp.pad(rest, ((0, 0), (0, width - rest.shape[1])))


def unpack_rows(packed, layout):
    devices, _, width = packed.shape
    parts = []
    first = 0
    for rows, count in layout:
        pieces = []
        for k in range(count):
            piece = packed[:, first : first + rows].reshape(devices * rows, width)
            pieces.append(piece)
            first += rows
        parts.append(pieces[0] if count == 1 else jnp.concatenate(pieces, axis=1))
    return parts


def unpack_rest(rest, span, slots):
    position = rest[:, :span].T.astype(jnp.float32)
    small = rest[:, span : span + slots].T.astype(jnp.float32)
    return small, position, rest[:, span + slots :]


def embed_forward(token_rows, weights, segment_ids):
    small, position = weights[4:]
    segment_rows = jnp.where(segment_ids[..., None] == 0, small[14], small[15])
    return layer_norm_keep(token_rows + position + segment_rows, small[12], small[13])


def layer_forward(value, weights, lengths):
    w_qkv, w_out, w_up, w_down, small = weights[:5]
    micro, span, width = value.shape
    value_low = value.astype(LOW)
    bias = jnp.concatenate([small[0], jnp.zeros_like(small[0]), small[1]])
    joined = (product_of("bsd,df->bsf", value_low, w_qkv) + bias).astype(LOW)
    context = attend(joined, lengths)
    attn = product_of("bsc,cd->bsd", context, w_out) + small[2]
    first, normed_first, inverse_first = layer_norm_keep(value + attn, small[8], small[9])
    first_low = first.astype(LOW)
    upward = product_of("bsd,df->bsf", first_low, w_up) + small[3:7].reshape(-1)
    act, slope = gelu_parts(upward)
    slope = slope.astype(LOW)
    act_low = act.astype(LOW)
    down = product_of("bsf,fd->bsd", act_low, w_down) + small[7]
    out, normed_second, inverse_second = layer_norm_keep(first + down, small[10], small[11])
    return (
        out,
        (
            value_low,
            joined,
            context,
            normed_first,
            inverse_first,
            first_low,
            slope,
            act_low,
            normed_second,
            inverse_second,
        ),
    )


def layer_backward(grad, weights, kept, lengths):
    w_qkv, w_out, w_up, w_down, small = weights[:5]
    (
        value_low,
        joined,
        context,
        normed_first,
        inverse_first,
        first_low,
        slope,
        act_low,
        normed_second,
        inverse_second,
    ) = kept
    micro, span, width = value_low.shape
    d_second, gain_second, shift_second = layer_norm_back(
        grad, normed_second, inverse_second, small[10]
    )
    d_second, d_down = lax.optimization_barrier((d_second, d_second.astype(LOW)))
    d_up = (product_of("bsd,fd->bsf", d_down, w_down) * slope).astype(LOW)
    d_first = d_second + product_of("bsf,df->bsd", d_up, w_up)
    d_sum, gain_first, shift_first = layer_norm_back(d_first, normed_first, inverse_first, small[8])
    d_attn = d_sum.astype(LOW)
    d_context = product_of("bsd,cd->bsc", d_attn, w_out).astype(LOW)
    d_joined = jnp.concatenate(list(attend_back(joined, d_context, lengths)), axis=-1)
    d_value = d_sum + product_of("bsf,df->bsd", d_joined, w_qkv)

    def column_sum(value):
        return jnp.sum(value.astype(jnp.float32), axis=(0, 1))

    joined_sum = column_sum(d_joined)
    rows_grad = jnp.concatenate(
        [
            joined_sum[:width][None],
            joined_sum[2 * width :][None],
            column_sum(d_attn)[None],
            column_sum(d_up).reshape(-1, width),
            column_sum(d_down)[None],
            gain_first[None],
            shift_first[None],
            gain_second[None],
            shift_second[None],
        ]
    )
    factors = (
        (value_low, d_joined),
        (context, d_attn),
        (first_low, d_up),
        (act_low, d_down),
    )
    return factors, rows_grad, d_value


def label_rows(pick, out):
    micro, labels, _ = pick.shape
    rows = product_of("bps,bsd->bpd", pick, out.astype(LOW)).astype(LOW)
    return rows.reshape(micro * labels, out.shape[-1])


def label_head(
    all_student, all_teacher, pick, tables, targets, valid_mask, own, share, padded, groups, count
):
    table_student, table_teacher = tables
    vocab_rows = table_student.shape[0]
    micro, labels, span = pick.shape
    width = all_student.shape[1]
    mine = micro * labels
    inside, local_target = owned(targets, share, padded, groups, own)
    target = jnp.where(inside, local_target, -1)[None, :]
    student, student_stats = logits_call(
        functools.partial(student_logits_body, share),
        all_student,
        table_student,
        target,
        padded,
        "student_logits",
    )
    teacher, teacher_stats = logits_call(
        functools.partial(teacher_logits_body, share),
        all_teacher,
        table_teacher,
        student,
        padded,
        "teacher_logits",
    )
    stats = share_small(jnp.concatenate([student_stats, teacher_stats]), groups, 8)
    peak_student = jnp.max(stats[:, 0], axis=0)
    peak_teacher = jnp.max(stats[:, 4], axis=0)
    fall_student = jnp.exp((stats[:, 0] - peak_student) / SOFTMAX_HEAT)
    fall_teacher = jnp.exp((stats[:, 4] - peak_teacher) / SOFTMAX_HEAT)
    sum_plain = jnp.sum(stats[:, 1] * fall_student * fall_student, axis=0)
    sum_soft = jnp.sum(stats[:, 2] * fall_student, axis=0)
    sum_teacher = jnp.sum(stats[:, 5] * fall_teacher, axis=0)
    cross = jnp.sum(stats[:, 6] * fall_teacher, axis=0)
    target_logit = jnp.sum(stats[:, 3], axis=0)
    lse_plain = peak_student + jnp.log(sum_plain)
    lse_soft = peak_student / SOFTMAX_HEAT + jnp.log(sum_soft)
    lse_teacher = peak_teacher / SOFTMAX_HEAT + jnp.log(sum_teacher)
    cross_entropy = lse_plain - target_logit
    divergence_loss = cross / sum_teacher - lse_teacher + lse_soft
    share_lab = valid_mask / count
    consts = jnp.stack([lse_plain, lse_soft, lse_teacher, share_lab])
    d_logits, d_rows = logits_back(student, teacher, table_student, consts, target, padded)
    d_rows = lax.psum_scatter(d_rows, "fsdp", scatter_dimension=0, tiled=True)
    table_term = product_of("vp,pd->vd", d_logits, all_student)
    d_rows, table_term = lax.optimization_barrier((d_rows, table_term))
    terms = share_lab * (
        (1.0 - SOFT_FRACTION) * cross_entropy
        + SOFT_FRACTION * SOFTMAX_HEAT * SOFTMAX_HEAT * divergence_loss
    )
    local = lax.dynamic_slice_in_dim(terms, own * mine, mine)
    d_out = product_of("bps,bpd->bsd", pick, d_rows.reshape(micro, -1, width))
    return (d_out, table_term, jnp.sum(local))


def pack_grads(g_qkv, g_out, g_up, g_down, small_grad, position_grad, devices):
    width = g_out.shape[0]
    rows = width // devices

    def shards(grad):
        return grad.astype(LOW).reshape(devices, -1, width)

    pieces = [shards(g_qkv[:, k * width : (k + 1) * width]) for k in range(3)]
    pieces += [shards(g_out)]
    pieces += [shards(g_up[:, k * width : (k + 1) * width]) for k in range(4)]
    pieces += [shards(g_down)]
    rest = jnp.concatenate([position_grad, small_grad], axis=0)
    rest = jnp.pad(rest, ((0, width - rest.shape[0]), (0, 0))).T
    pieces += [shards(rest)]
    filled = 8 * rows + g_down.shape[0] // devices + rows
    pad = -filled % 64
    if pad:
        pieces += [jnp.zeros((devices, pad, width), LOW)]
    return jnp.concatenate(pieces, axis=1)


def unpack_grads(packed, rows, span, slots):
    width = packed.shape[1]
    down = packed.shape[1] * 4 * rows // width
    low = 8 * rows

    def part(first):
        return packed[first * rows : (first + 1) * rows]

    rest = packed[low + down : low + down + rows]
    return (
        jnp.concatenate([part(k) for k in range(3)], axis=1),
        part(3),
        jnp.concatenate([part(4 + k) for k in range(4)], axis=1),
        packed[low : low + down],
        rest[:, span : span + slots].T,
        rest[:, :span].T,
    )


def unit_of(cls):
    scale = lax.rsqrt(jnp.sum(cls * cls, axis=-1, keepdims=True) + 1e-06)
    return cls * scale, scale


def on_device(
    tok_ids,
    segments,
    seq_len,
    label_pos,
    label_ids,
    table,
    w_qkv,
    w_out,
    w_up,
    w_down,
    small,
    position,
    t_table,
    t_qkv,
    t_out,
    t_up,
    t_down,
    t_small,
    t_position,
    mom_table,
    mom_qkv,
    mom_out,
    mom_up,
    mom_down,
    mom_small,
    mom_position,
    avg_table,
    avg_qkv,
    avg_out,
    avg_up,
    avg_down,
    avg_small,
    avg_position,
):
    micro, span = tok_ids.shape
    labels = label_pos.shape[1]
    share, width = table.shape
    groups = lax.axis_size("fsdp")
    dp = lax.axis_size("dp")
    devices = groups * dp
    own = lax.axis_index("fsdp")
    padded = (share // 32 + 1) * 32
    pad = padded - share
    rows_own = w_qkv.shape[0]
    slots = small.shape[0]

    info = jnp.concatenate(
        [tok_ids, label_ids, jnp.broadcast_to(seq_len[:, None], (micro, labels))], axis=1
    )
    info = jnp.pad(info, ((0, -micro % 8), (0, 0)))
    student_table, info = spread_dp(
        [jnp.pad(table.astype(LOW), ((0, pad), (0, 0)))], dp, 1, info, groups
    )
    info = info[:, :micro].reshape(groups * micro, span + 2 * labels)
    ids_all = info[:, :span]
    targets_all = info[:, span : span + labels].reshape(-1)
    lengths_all = info[:, span + labels]
    valid_local = label_valid(seq_len, labels, span)
    counts = jnp.stack([jnp.sum(valid_local), jnp.sum((seq_len > 0).astype(jnp.float32))])
    extra = jnp.broadcast_to(counts.astype(LOW)[None, :], (rows_own, 2))

    safe_ids = owned(ids_all, share, padded, groups, own)[1]
    packed_teacher = pack_rows(
        (t_qkv, t_out, t_up, t_down, pack_rest(t_small, t_position, None, width)), width
    )
    packed_teacher = lax.all_gather(packed_teacher, BOTH)
    safe_flat = safe_ids.reshape(-1)
    student_hits = student_table[safe_flat].reshape(groups * micro, span, width)
    student_hits, t_table = lax.optimization_barrier((student_hits, t_table))
    teacher_table = spread_dp([jnp.pad(t_table, ((0, pad), (0, 0)))], dp, 2)[0]
    tokens_student = lax.psum_scatter(
        student_hits,
        "fsdp",
        scatter_dimension=0,
        tiled=True,
    ).astype(jnp.float32)
    teacher_hits = teacher_table[safe_flat].reshape(groups * micro, span, width)
    s_weights, teacher_hits, packed_teacher = lax.optimization_barrier(
        ((w_qkv, w_out, w_up, w_down, small, position), teacher_hits, packed_teacher)
    )
    tokens_teacher = lax.psum_scatter(teacher_hits, "fsdp", scatter_dimension=0, tiled=True)
    packed_student = pack_rows(
        s_weights[:2] + (pack_rest(s_weights[4], s_weights[5], extra, width),), width
    )
    packed_student, up_student, down_student = gather_weights(
        [packed_student, pack_rows((s_weights[2],), width), pack_rows((s_weights[3],), width)],
        dp,
        groups,
        5,
    )
    layout = (
        (rows_own, 3),
        (rows_own, 1),
        (rows_own, 4),
        (w_down.shape[0], 1),
        (rows_own, 1),
    )
    full_qkv, full_out, rest = unpack_rows(packed_student, layout[:2] + layout[4:])
    full_small, full_position, rest = unpack_rest(rest, span, slots)
    full_up = unpack_rows(up_student, layout[2:3])[0]
    full_down = down_student[:, : w_down.shape[0]].reshape(-1, width)
    weights = (full_qkv, full_out, full_up, full_down, full_small, full_position)
    counted = jnp.sum(rest[::rows_own, :2].astype(jnp.float32), axis=0)
    label_count, count_seq = counted[0], counted[1]

    tables = (student_table, teacher_table)
    vocab_rows = student_table.shape[0]
    start, normed_start, inverse_start = embed_forward(tokens_student, weights, segments)
    student_out, kept = layer_forward(start, weights, seq_len)
    pick = (label_pos[..., None] == jnp.arange(span)).astype(LOW)
    student_rows = label_rows(pick, student_out)
    student_rows, packed_teacher = lax.optimization_barrier((student_rows, packed_teacher))
    *teacher, teacher_rest = unpack_rows(packed_teacher, layout)
    teacher = tuple(teacher) + unpack_rest(teacher_rest, span, slots)[:2]
    student_rows, teacher, tokens_teacher = lax.optimization_barrier(
        (student_rows, teacher, tokens_teacher)
    )
    student_rows = lax.all_gather(student_rows, "fsdp", axis=0, tiled=True)
    teacher_start = embed_forward(tokens_teacher.astype(jnp.float32), teacher, segments)[0]
    teacher_out = layer_forward(teacher_start, teacher, seq_len)[0]
    teacher_rows = label_rows(pick, teacher_out)
    teacher_rows = lax.all_gather(teacher_rows, "fsdp", axis=0, tiled=True)
    valid_group = label_valid(lengths_all, labels, span).reshape(-1)
    d_out, table_grad, label_loss = label_head(
        student_rows,
        teacher_rows,
        pick,
        tables,
        targets_all,
        valid_group,
        own,
        share,
        padded,
        groups,
        label_count,
    )
    cls_student = student_out[:, 0]
    unit_student, scale_student = unit_of(cls_student)
    unit_teacher = unit_of(teacher_out[:, 0])[0]
    weight_pkd = (PKD_WEIGHT * (seq_len > 0).astype(jnp.float32) / count_seq)[:, None]
    gap = unit_student - unit_teacher
    d_unit = 2.0 * weight_pkd * gap
    d_cls = scale_student * d_unit - cls_student * scale_student**3 * jnp.sum(
        cls_student * d_unit, axis=-1, keepdims=True
    )
    first_row = (jnp.arange(span) == 0).astype(jnp.float32)[None, :, None]
    d_out = d_out + first_row * d_cls[:, None, :]
    loss_part = label_loss + jnp.sum(weight_pkd * gap * gap)

    factors, rows_grad, d_start = layer_backward(d_out, weights, kept, seq_len)
    d_embed, gain_embed, shift_embed = layer_norm_back(
        d_start, normed_start, inverse_start, weights[4][12]
    )
    zero_segment = (segments == 0).astype(jnp.float32)[..., None]
    small_grad = jnp.concatenate(
        [
            rows_grad,
            gain_embed[None],
            shift_embed[None],
            jnp.sum(d_embed * zero_segment, axis=(0, 1))[None],
            jnp.sum(d_embed * (1.0 - zero_segment), axis=(0, 1))[None],
        ]
    )
    position_grad = jnp.sum(d_embed, axis=0)
    d_embed_low, factors = lax.optimization_barrier((d_embed.astype(LOW), factors))
    embed_grads = lax.all_gather(d_embed_low, "fsdp", axis=0, tiled=True)
    matrices = [
        product_of("bsd,bsf->df", left, right) for left, right in factors
    ]
    packed_grads = pack_grads(*matrices, small_grad, position_grad, devices)
    packed_grads = reduce_weights(packed_grads, dp, groups, 2, 6)
    layer_squares = jnp.sum(packed_grads * packed_grads)
    table_grad, embed_grads, packed_grads, layer_squares = lax.optimization_barrier(
        (table_grad, embed_grads, packed_grads, layer_squares)
    )
    table_shard, table_squares = fold_dp(
        safe_flat, embed_grads.reshape(-1, width), table_grad, dp, share, 2048, 3
    )
    table_shard = table_shard[:share]
    grads = (table_shard,) + unpack_grads(packed_grads, rows_own, span, slots)
    squares = layer_squares + jnp.sum(table_squares)
    column = jnp.arange(128)[None, :]
    sums = jnp.where(column == 0, squares, jnp.where(column == 1, loss_part, 0.0))
    sums = total_all(jnp.broadcast_to(sums, (8, 128)), dp, groups, 4)
    total_sq, loss_value = sums[0, 0], sums[0, 1]
    grad_norm = jnp.sqrt(total_sq)
    factor = CLIP / jnp.maximum(grad_norm, CLIP)
    rate = RATE_SCALE * math.sqrt(NPARAM)
    params = (table, w_qkv, w_out, w_up, w_down, small, position)
    moms = (mom_table, mom_qkv, mom_out, mom_up, mom_down, mom_small, mom_position)
    avgs = (avg_table, avg_qkv, avg_out, avg_up, avg_down, avg_small, avg_position)
    news, moments, averages = ([], [], [])
    for weight, grad, momentum, average in zip(params, grads, moms, avgs):
        clipped = grad * factor
        moment = MOMENTUM * momentum + clipped
        fresh = weight - rate * (clipped + MOMENTUM * moment)
        news.append(fresh)
        moments.append(moment)
        averages.append(AVERAGE * average + (1.0 - AVERAGE) * fresh)
    return tuple(news) + tuple(moments) + tuple(averages) + (grad_norm, loss_value)


def solution(mesh):
    placed = (
        P(("dp", "fsdp"), None),
        P(("dp", "fsdp"), None),
        P(("dp", "fsdp")),
        P(("dp", "fsdp"), None),
        P(("dp", "fsdp"), None),
        P(("dp", "fsdp"), None),
        P(("dp", "fsdp"), None),
        P(("dp", "fsdp"), None),
        P(("dp", "fsdp"), None),
        P(("dp", "fsdp"), None),
        P(None, ("dp", "fsdp")),
        P(None, ("dp", "fsdp")),
        P(("dp", "fsdp"), None),
        P(("dp", "fsdp"), None),
        P(("dp", "fsdp"), None),
        P(("dp", "fsdp"), None),
        P(("dp", "fsdp"), None),
        P(None, ("dp", "fsdp")),
        P(None, ("dp", "fsdp")),
        P(("dp", "fsdp"), None),
        P(("dp", "fsdp"), None),
        P(("dp", "fsdp"), None),
        P(("dp", "fsdp"), None),
        P(("dp", "fsdp"), None),
        P(None, ("dp", "fsdp")),
        P(None, ("dp", "fsdp")),
        P(("dp", "fsdp"), None),
        P(("dp", "fsdp"), None),
        P(("dp", "fsdp"), None),
        P(("dp", "fsdp"), None),
        P(("dp", "fsdp"), None),
        P(None, ("dp", "fsdp")),
        P(None, ("dp", "fsdp")),
    )
    return jax.shard_map(
        on_device,
        mesh=mesh,
        in_specs=placed,
        out_specs=(
            P(("dp", "fsdp"), None),
            P(("dp", "fsdp"), None),
            P(("dp", "fsdp"), None),
            P(("dp", "fsdp"), None),
            P(("dp", "fsdp"), None),
            P(None, ("dp", "fsdp")),
            P(None, ("dp", "fsdp")),
            P(("dp", "fsdp"), None),
            P(("dp", "fsdp"), None),
            P(("dp", "fsdp"), None),
            P(("dp", "fsdp"), None),
            P(("dp", "fsdp"), None),
            P(None, ("dp", "fsdp")),
            P(None, ("dp", "fsdp")),
            P(("dp", "fsdp"), None),
            P(("dp", "fsdp"), None),
            P(("dp", "fsdp"), None),
            P(("dp", "fsdp"), None),
            P(("dp", "fsdp"), None),
            P(None, ("dp", "fsdp")),
            P(None, ("dp", "fsdp")),
            P(),
            P(),
        ),
        check_vma=False,
    )
```
